512 devices in a mesh: lat: 64 (over y, z), lev: 8 (over x, core).
Axes of the slice: x: 4, y: 4, z: 16, core: 2. Of those that a mesh axis runs over, the one named last changes fastest.
Arguments:
- grid_fields: bfloat16 [32, 1280, 2688], P('lev', 'lat'), may hold values from -6 to 6
- legendre: bfloat16 [1024, 2, 640, 512], P(('lat', 'lev')), may hold values from -0.15625 to 0.15625
- weights: float32 [640], replicated, may hold values from 0.2 to 1.6
- kept_waves: int32 [1280], P('lat'), may hold values from 8 to 1024, as said below
- slot_wavenumber: int32 [1024], replicated, may hold values from 0 to 1023, as said below
- diffusion: float32 [32], replicated, may hold values from 0.5 to 50
Outputs:
- grid_out: float32 [32, 1280, 2688], P('lev', 'lat')
- spectral: float32 [1024, 2, 32, 2, 512], P(('lat', 'lev'))
- spectrum: float32 [1024], replicated
The draws below stay inside these ranges and needn't reach their ends.
Inputs may be any that keep to these rules, and one draw needn't show every extreme that they name: kept_waves[j] wavenumbers are retained at latitude j; it equals 1024 at the two latitudes nearest the equator. `slot_wavenumber`: a permutation of 0 to 1023 whose entries 2k and 2k + 1 add up to 1023; device d of the lat, lev mesh in that order owns slots d * 2 to (d + 1) * 2 - 1.
All inputs are finite; a program needn't handle non-finite values.
Results may differ from the reference program's by a relative error of at most 0.0071.
Values may be sent and summed in bfloat16 or wider, within the bound.
No kernel may reach another device: no remote copies, remote signals or barrier semaphores. Data moves between devices by JAX's collectives and lax.ppermute only.
A program may use at most 128 MiB of HBM per device.

```python
import math
import jax
import jax.numpy as jnp
from jax import lax

NLAT = 1280
NLON = 2688
MM = 1024
LEVELS = 32


def draw_kept_waves(key, part):
    key = jax.random.fold_in(key, 11)
    latitude = jnp.arange(NLAT, dtype=jnp.int32)
    distance = jnp.minimum(latitude, NLAT - 1 - latitude)
    jitter = jax.random.randint(key, (NLAT,), 0, 4, dtype=jnp.int32)
    return jnp.minimum(MM, 8 + jitter + 3 * MM * distance // (NLAT // 2)).astype(jnp.int32)


def draw_slot_wavenumber(key, part):
    key = jax.random.fold_in(key, 23)
    lower = jax.random.permutation(key, jnp.arange(MM // 2, dtype=jnp.int32))
    return jnp.stack([lower, MM - 1 - lower], axis=1).reshape(MM).astype(jnp.int32)


def block_scale(key, dims, split, smallest, high):
    factor_of = 1.0
    for dim, shards_of in split:
        draws = jax.random.uniform(jax.random.fold_in(jax.random.fold_in(key, 6), dim), (shards_of,), jnp.float32, smallest / len(split), high / len(split))
        factor_of = factor_of * jnp.repeat(jnp.exp(draws), dims[dim] // shards_of).reshape((-1,) + (1,) * (len(dims) - 1 - dim))
    return factor_of


def noise(own_key, shape, scale, bound, cuts=(), kind=jnp.bfloat16):
    drawn = jax.random.normal(own_key, shape, jnp.float32) * scale
    if len(cuts) > 0:
        drawn = block_scale(own_key, shape, cuts, -0.22, 0.18) * drawn
    return jnp.clip(drawn, min=-bound, max=bound).astype(kind)


def setup_inputs(seed: int = 0) -> dict:
    seeds = jax.random.split(jax.random.key(seed), 7)
    return {
        "grid_fields": noise(seeds[0], (LEVELS, NLAT, NLON), 1.0, 6.0, ((0, 8), (1, 64))),
        "legendre": noise(seeds[1], (MM, 2, NLAT // 2, MM // 2), NLAT ** -0.5, 0.15625, ((0, 512),)),
        "weights": jnp.clip(jax.random.uniform(seeds[2], (NLAT // 2,), jnp.float32, 0.2, 1.6), 0.2, 1.6),
        "kept_waves": draw_kept_waves(jax.random.fold_in(seeds[6], 71), 0),
        "slot_wavenumber": draw_slot_wavenumber(jax.random.fold_in(seeds[6], 71), 0),
        "diffusion": jnp.clip(jnp.exp(jax.random.uniform(seeds[5], (LEVELS,), jnp.float32, math.log(0.5), math.log(50.0))), 0.5, 50.0),
    }


def dft_table(points, wave_count):
    sample = jnp.arange(points, dtype=jnp.int32)[:, None]
    number = jnp.arange(wave_count, dtype=jnp.int32)[None, :]
    angles = (sample * number % points).astype(jnp.float32) * (2.0 * math.pi / points)
    norm_scale = 1.0 / math.sqrt(points)
    return (jnp.concatenate([jnp.cos(angles), -jnp.sin(angles)], axis=1) * norm_scale).astype(jnp.bfloat16)

def spread_by_degree(values, offsets):
    width = values.shape[1]
    padded = jnp.concatenate([jnp.zeros_like(values), values], axis=1)

    def placed(row_values, offset_value):
        return lax.dynamic_slice_in_dim(row_values, (width - offset_value).astype(jnp.int32), width)
    return jax.vmap(placed)(padded, offsets)

def reference(grid_fields, legendre, weights, kept_waves, slot_wavenumber, diffusion):
    half_lat = NLAT // 2
    half_wave = MM // 2
    group_size = 16
    groups = MM // group_size
    transform = dft_table(NLON, MM)
    fourier_raw = jnp.dot(grid_fields.reshape(LEVELS * NLAT, NLON).astype(jnp.float32), transform.astype(jnp.float32), precision=lax.Precision.HIGHEST)
    fourier_raw = fourier_raw.reshape(LEVELS, NLAT, 2, MM)
    latitude = jnp.arange(NLAT, dtype=jnp.int32)
    mirror = jnp.minimum(latitude, NLAT - 1 - latitude)
    kept_mask = jnp.arange(MM, dtype=jnp.int32)[None, :] < kept_waves[:, None]
    factor = jnp.where(kept_mask, jnp.take(weights, mirror)[:, None], 0.0)
    fourier = (fourier_raw * factor[None, :, None, :]).astype(jnp.bfloat16)
    slotted = jnp.take(fourier, slot_wavenumber, axis=3)
    northern = slotted[:, :half_lat].astype(jnp.float32)
    southern = slotted[:, ::-1][:, :half_lat].astype(jnp.float32)
    combined = jnp.stack([northern + southern, northern - southern]).astype(jnp.bfloat16)
    table_groups = legendre.reshape(groups, group_size, 2, half_lat, half_wave)
    comb_groups = jnp.moveaxis(combined.reshape(2, LEVELS, half_lat, 2, groups, group_size), 4, 0)

    def forward(pieces):
        return jnp.einsum('sqji,qljrs->sqlri', pieces[0].astype(jnp.float32), pieces[1].astype(jnp.float32))
    spectral_raw = lax.map(forward, (table_groups, comb_groups)).reshape(MM, 2, LEVELS, 2, half_wave)
    parity = jnp.arange(2, dtype=jnp.int32)[None, :, None, None, None]
    column = jnp.arange(half_wave, dtype=jnp.int32)[None, None, None, None, :]
    degree = slot_wavenumber[:, None, None, None, None] + 2 * column + parity
    spectral = jnp.where(degree < MM, spectral_raw, 0.0)
    degree_float = degree.astype(jnp.float32)
    damping_ratio = degree_float * (degree_float + 1.0) / (MM * (MM + 1.0))
    damped = (spectral / (1.0 + diffusion[None, None, :, None, None] * damping_ratio * damping_ratio)).astype(jnp.bfloat16)
    damp_groups = damped.reshape(groups, group_size, 2, LEVELS, 2, half_wave)

    def inverse(pieces):
        return jnp.einsum('sqji,sqlri->qljrs', pieces[0].astype(jnp.float32), pieces[1].astype(jnp.float32))
    halves = lax.map(inverse, (table_groups, damp_groups))
    halves = jnp.moveaxis(halves, 0, 4).reshape(2, LEVELS, half_lat, 2, MM)
    north_back = (halves[0] + halves[1]).astype(jnp.bfloat16)
    south_back = (halves[0] - halves[1]).astype(jnp.bfloat16)
    back = jnp.concatenate([north_back, south_back[:, ::-1]], axis=1)
    position = jnp.argsort(slot_wavenumber).astype(jnp.int32)
    coefficients = jnp.where(kept_mask[None, :, None, :], jnp.take(back, position, axis=3), jnp.zeros((), jnp.bfloat16))
    grid_out = jnp.dot(coefficients.reshape(LEVELS * NLAT, 2 * MM).astype(jnp.float32), transform.astype(jnp.float32).T, precision=lax.Precision.HIGHEST)
    grid_out = (grid_out * math.sqrt(NLON / MM)).reshape(LEVELS, NLAT, NLON)
    energy = lax.optimization_barrier(jnp.sum(spectral * spectral, axis=(2, 3)))
    energy = jnp.swapaxes(energy, 1, 2).reshape(MM, MM)
    spectrum = lax.optimization_barrier(jnp.sum(spread_by_degree(energy, slot_wavenumber), axis=0))
    spectrum = spectrum / (2.0 * LEVELS * (jnp.arange(MM, dtype=jnp.float32) + 1.0))
    return (grid_out, spectral, spectrum)
```

```python
import math

import jax
import jax.numpy as jnp
import ml_dtypes
import numpy as np
from jax import lax
from jax.experimental import pallas as pl
from jax.experimental.pallas import tpu as pltpu
from jax.sharding import Mesh
from jax.sharding import PartitionSpec as P

NLAT = 1280
NLON = 2688
MM = 1024
HALF = MM // 2
LEVELS = 32
BAND = 20
LEV = 4
ROWS = BAND * LEV
LATS = 64
LEVS = 8
NORTH = LATS // 2
STEPS = 4
BLOCK = MM // STEPS
TILES = BAND // 4
LANES = 128

BF16 = jnp.bfloat16
F32 = jnp.float32
VMEM = pl.BlockSpec(memory_space=pltpu.VMEM)
SMEM = pl.BlockSpec(memory_space=pltpu.SMEM)
PARAMS = pltpu.CompilerParams(vmem_limit_bytes=48 * 1024 * 1024)


def dft_tables():
    sample = np.arange(NLON, dtype=np.int32)[:, None]
    number = np.arange(MM, dtype=np.int32)[None, :]
    angles = (sample * number % NLON).astype(np.float32) * np.float32(2.0 * math.pi / NLON)
    norm_scale = np.float32(1.0 / math.sqrt(NLON))
    cosine = (np.cos(angles) * norm_scale).astype(ml_dtypes.bfloat16)
    sine = (-np.sin(angles) * norm_scale).astype(ml_dtypes.bfloat16)
    both = np.stack([cosine, sine], axis=1).reshape(NLON, 2, STEPS, BLOCK)
    forward = np.ascontiguousarray(both.transpose(2, 0, 1, 3)).reshape(STEPS, NLON, 2 * BLOCK)
    inverse = np.ascontiguousarray(forward.transpose(0, 2, 1))
    return forward, inverse


def iota(shape, dim):
    return lax.broadcasted_iota(jnp.int32, shape, dim)


def slot_choice(slots_ref, step):
    number = iota((BLOCK, MM), 0) + step * BLOCK
    return jnp.where(slots_ref[...] == number, 1.0, 0.0).astype(BF16)


def per_latitude(ref, zero, start=None, mirrored=False):
    band = iota((ROWS, LANES), 0) // LEV
    column = jnp.full((ROWS, LANES), zero)
    for j in range(BAND):
        if mirrored:
            latitude = start * BAND + j
            scalar = ref[jnp.minimum(latitude, NLAT - 1 - latitude)]
        else:
            scalar = ref[j]
        column = jnp.where(band == j, scalar, column)
    return column


def row_choice(southern):
    to = iota((2 * ROWS, 2 * ROWS), 0)
    source = iota((2 * ROWS, 2 * ROWS), 1)
    band = to // (2 * LEV)
    band = jnp.where(southern, BAND - 1 - band, band)
    wanted = (to % 2) * ROWS + band * LEV + to // 2 % LEV
    return jnp.where(source == wanted, 1.0, 0.0).astype(BF16)


def fourier_kernel(lat_ref, kept_ref, weights_ref, slots_ref, x_ref, table_ref, o_ref, kept, factor, acc):
    step = pl.program_id(0)
    lat = lat_ref[0]

    @pl.when(step == 0)
    def _():
        kept[...] = per_latitude(kept_ref, jnp.int32(0))
        factor[...] = per_latitude(weights_ref, F32(0.0), lat, True)
        acc[...] = jnp.zeros_like(acc)

    raw = jnp.dot(x_ref[...], table_ref[0], preferred_element_type=F32)
    number = iota((ROWS, BLOCK), 1) + step * BLOCK
    mask = number < jnp.concatenate([kept[...]] * (BLOCK // LANES), axis=1)
    scale = jnp.where(mask, jnp.concatenate([factor[...]] * (BLOCK // LANES), axis=1), 0.0)
    fourier = jnp.concatenate([raw[:, :BLOCK] * scale, raw[:, BLOCK:] * scale], axis=0).astype(BF16)
    acc[...] += jnp.dot(fourier, slot_choice(slots_ref, step), preferred_element_type=F32)

    @pl.when(step == STEPS - 1)
    def _():
        choice = row_choice(lat >= NORTH)
        rows = jnp.dot(choice, acc[...].astype(BF16), preferred_element_type=F32).astype(BF16)
        for b in range(LEVS):
            o_ref[b] = rows[:, b * LANES : (b + 1) * LANES]


def gather_kernel(y_ref, o_ref, rows):
    for j in range(BAND):
        block = jnp.concatenate([y_ref[b, 8 * j : 8 * j + 8, :].astype(F32) for b in range(LEVS)], axis=0)
        turned = block.T
        rows[:, j % 4, (j // 4) * LANES : (j // 4 + 1) * LANES] = jnp.concatenate(
            [turned[:LATS], turned[LATS:]], axis=1
        )
    o_ref[...] = rows[...].astype(BF16)


def scatter_kernel(z_ref, o_ref, rows):
    rows[...] = z_ref[...].astype(F32)
    for j in range(BAND):
        block = rows[:, j % 4, (j // 4) * LANES : (j // 4 + 1) * LANES]
        turned = jnp.concatenate([block[:, :LATS], block[:, LATS:]], axis=0).T
        for b in range(LEVS):
            o_ref[b, 8 * j : 8 * j + 8, :] = turned[8 * b : 8 * b + 8].astype(BF16)


def legendre_kernel(waves_ref, diffusion_ref, z_ref, table_ref, spectral_ref, energy_ref, o_ref, comb):
    for group in range(NORTH * TILES // 4):
        north, south = [], []
        for u in range(4 * group, 4 * group + 4):
            a, tile = divmod(u, TILES)
            lanes = slice(tile * LANES, (tile + 1) * LANES)
            north.append(z_ref[a, :, lanes].astype(F32))
            south.append(z_ref[LATS - 1 - a, :, lanes].astype(F32))
        north = jnp.concatenate(north, axis=0)
        south = jnp.concatenate(south, axis=0)
        comb[0, 16 * group : 16 * group + 16, :] = north + south
        comb[1, 16 * group : 16 * group + 16, :] = north - south
    column = iota((64, HALF), 1)
    power = [jnp.zeros((1, HALF), F32), jnp.zeros((1, HALF), F32)]
    halves = []
    for q in range(2):
        left = comb[q].T.astype(BF16)
        parts = []
        for t in range(2):
            wave = waves_ref[t]
            raw = jnp.dot(left[64 * t : 64 * t + 64], table_ref[t, q], preferred_element_type=F32)
            degree = wave + 2 * column + q
            spectral = jnp.where(degree < MM, raw, 0.0)
            spectral_ref[t, q] = spectral
            degree = degree.astype(F32)
            ratio = degree * (degree + 1.0) / (MM * (MM + 1.0))
            damped = (spectral / (1.0 + diffusion_ref[...] * ratio * ratio)).astype(BF16)
            parts.append(
                lax.dot_general(
                    table_ref[t, q], damped, (((1,), (1,)), ((), ())), preferred_element_type=F32
                )
            )
            energy = jnp.sum(spectral * spectral, axis=0, keepdims=True)
            first = wave + q
            moved = pltpu.roll(jnp.broadcast_to(energy, (8, HALF)), first // 2 % HALF, 1)[:1]
            for odd in range(2):
                power[odd] += jnp.where(first % 2 == odd, moved, 0.0)
        halves.append(jnp.concatenate(parts, axis=1))
    energy_ref[...] = jnp.concatenate(power, axis=0)
    north = halves[0] + halves[1]
    south = halves[0] - halves[1]
    for u in range(NORTH * TILES):
        a, tile = divmod(u, TILES)
        lanes = slice(tile * LANES, (tile + 1) * LANES)
        o_ref[a, :, lanes] = north[4 * u : 4 * u + 4].astype(BF16)
        o_ref[LATS - 1 - a, :, lanes] = south[4 * u : 4 * u + 4].astype(BF16)


def grid_kernel(lat_ref, kept_ref, slots_ref, y_ref, table_ref, o_ref, kept, rows, acc):
    step = pl.program_id(0)

    @pl.when(step == 0)
    def _():
        kept[...] = per_latitude(kept_ref, jnp.int32(0))
        choice = row_choice(lat_ref[0] >= NORTH)
        back = jnp.concatenate([y_ref[b] for b in range(LEVS)], axis=1)
        rows[...] = lax.dot_general(
            choice, back, (((0,), (0,)), ((), ())), preferred_element_type=F32
        ).astype(BF16)
        acc[...] = jnp.zeros_like(acc)

    numbered = lax.dot_general(
        rows[...], slot_choice(slots_ref, step), (((1,), (1,)), ((), ())), preferred_element_type=F32
    )
    number = iota((ROWS, BLOCK), 1) + step * BLOCK
    mask = number < jnp.concatenate([kept[...]] * (BLOCK // LANES), axis=1)
    coefficients = jnp.concatenate(
        [jnp.where(mask, numbered[:ROWS], 0.0), jnp.where(mask, numbered[ROWS:], 0.0)], axis=1
    ).astype(BF16)
    acc[...] += jnp.dot(coefficients, table_ref[0], preferred_element_type=F32)

    @pl.when(step == STEPS - 1)
    def _():
        o_ref[...] = acc[...] * math.sqrt(NLON / MM)


def exchange(x, axes):
    return lax.all_to_all(x, axes, split_axis=0, concat_axis=0, tiled=True)


def body(grid_fields, legendre, weights, kept_waves, slot_wavenumber, diffusion):
    forward_table, inverse_table = dft_tables()
    lat = lax.axis_index(("y", "z")).astype(jnp.int32)
    lev = lax.axis_index(("x", "core")).astype(jnp.int32)
    lat_ref = lat.reshape(1)
    slots = slot_wavenumber.reshape(LATS, LEVS, 2).transpose(1, 2, 0).reshape(1, MM)
    waves = lax.dynamic_slice_in_dim(slot_wavenumber, (lat * LEVS + lev) * 2, 2)
    x = grid_fields.transpose(1, 0, 2).reshape(ROWS, NLON)

    sent = pl.pallas_call(
        fourier_kernel,
        grid=(STEPS,),
        in_specs=[
            SMEM,
            SMEM,
            SMEM,
            VMEM,
            VMEM,
            pl.BlockSpec((1, NLON, 2 * BLOCK), lambda i: (i, 0, 0)),
        ],
        out_specs=VMEM,
        out_shape=jax.ShapeDtypeStruct((LEVS, 2 * ROWS, LANES), BF16),
        scratch_shapes=[
            pltpu.VMEM((ROWS, LANES), jnp.int32),
            pltpu.VMEM((ROWS, LANES), F32),
            pltpu.VMEM((2 * ROWS, MM), F32),
        ],
        compiler_params=PARAMS,
        name="fourier",
    )(lat_ref, kept_waves, weights, slots, x, jnp.asarray(forward_table))
    arrived = exchange(sent, ("x", "core"))
    gathered = pl.pallas_call(
        gather_kernel,
        in_specs=[VMEM],
        out_specs=VMEM,
        out_shape=jax.ShapeDtypeStruct((LATS, 4, TILES * LANES), BF16),
        scratch_shapes=[pltpu.VMEM((LATS, 4, TILES * LANES), F32)],
        compiler_params=PARAMS,
        name="gather",
    )(arrived)
    gathered = exchange(gathered, ("y", "z"))
    spectral, energy, back = pl.pallas_call(
        legendre_kernel,
        in_specs=[SMEM, VMEM, VMEM, VMEM],
        out_specs=[VMEM, VMEM, VMEM],
        out_shape=[
            jax.ShapeDtypeStruct((2, 2, 2 * LEVELS, HALF), F32),
            jax.ShapeDtypeStruct((2, HALF), F32),
            jax.ShapeDtypeStruct((LATS, 4, TILES * LANES), BF16),
        ],
        scratch_shapes=[pltpu.VMEM((2, NLAT // 2, LANES), F32)],
        compiler_params=PARAMS,
        name="legendre",
    )(waves, jnp.repeat(diffusion, 2).reshape(2 * LEVELS, 1), gathered, legendre)

    power = jnp.sum(
        exchange(jnp.broadcast_to(energy.reshape(1, LEVS, LANES), (LEVS, LEVS, LANES)), ("x", "core")), axis=0
    )
    power = lax.dynamic_slice_in_dim(power, lev, 1)
    power = jnp.sum(
        exchange(jnp.broadcast_to(power.reshape(1, 1, LANES), (LATS, 1, LANES)), ("y", "z")), axis=0
    )
    power = exchange(jnp.broadcast_to(power.reshape(1, 1, LANES), (LEVS, 1, LANES)), ("x", "core"))
    summed = power.reshape(2, HALF).T.reshape(MM)
    spectrum = summed / (2.0 * LEVELS * (jnp.arange(MM, dtype=F32) + 1.0))

    back = exchange(back, ("y", "z"))
    scattered = pl.pallas_call(
        scatter_kernel,
        in_specs=[VMEM],
        out_specs=VMEM,
        out_shape=jax.ShapeDtypeStruct((LEVS, 2 * ROWS, LANES), BF16),
        scratch_shapes=[pltpu.VMEM((LATS, 4, TILES * LANES), F32)],
        compiler_params=PARAMS,
        name="scatter",
    )(back)
    returned = exchange(scattered, ("x", "core"))
    grid_out = pl.pallas_call(
        grid_kernel,
        grid=(STEPS,),
        in_specs=[
            SMEM,
            SMEM,
            VMEM,
            VMEM,
            pl.BlockSpec((1, 2 * BLOCK, NLON), lambda i: (i, 0, 0)),
        ],
        out_specs=VMEM,
        out_shape=jax.ShapeDtypeStruct((ROWS, NLON), F32),
        scratch_shapes=[
            pltpu.VMEM((ROWS, LANES), jnp.int32),
            pltpu.VMEM((2 * ROWS, MM), BF16),
            pltpu.VMEM((ROWS, NLON), F32),
        ],
        compiler_params=PARAMS,
        name="grid",
    )(lat_ref, kept_waves, slots, returned, jnp.asarray(inverse_table))
    grid_out = grid_out.reshape(BAND, LEV, NLON).transpose(1, 0, 2)
    return grid_out, spectral.reshape(2, 2, LEVELS, 2, HALF), spectrum


def solution(mesh):
    fine = Mesh(mesh.devices.reshape(4, 16, 4, 2), ("y", "z", "x", "core"))
    lat, lev = ("y", "z"), ("x", "core")
    both = lat + lev
    in_specs = (P(lev, lat, None), P(both, None, None, None), P(), P(lat), P(), P())
    out_specs = (P(lev, lat, None), P(both, None, None, None, None), P())
    return jax.shard_map(body, mesh=fine, in_specs=in_specs, out_specs=out_specs, check_vma=False)
```

```python
import math

import jax
import jax.numpy as jnp
import ml_dtypes
import numpy as np
from jax import lax
from jax.experimental import pallas as pl
from jax.experimental.pallas import tpu as pltpu
from jax.sharding import Mesh
from jax.sharding import PartitionSpec as P

NLAT = 1280
NLON = 2688
MM = 1024
HALF = MM // 2
LEVELS = 32
BAND = 20
LEV = 4
ROWS = BAND * LEV
LATS = 64
LEVS = 8
NORTH = LATS // 2
STEPS = 4
BLOCK = MM // STEPS
TILES = BAND // 4
LANES = 128
DATA = TILES * LANES

BF16 = jnp.bfloat16
F32 = jnp.float32
VMEM = pl.BlockSpec(memory_space=pltpu.VMEM)
HBM = pl.BlockSpec(memory_space=pltpu.HBM)
SMEM = pl.BlockSpec(memory_space=pltpu.SMEM)
PARAMS = pltpu.CompilerParams(vmem_limit_bytes=48 * 1024 * 1024)


def dft_tables():
    sample = np.arange(NLON, dtype=np.int32)[:, None]
    number = np.arange(MM, dtype=np.int32)[None, :]
    angles = (sample * number % NLON).astype(np.float32) * np.float32(2.0 * math.pi / NLON)
    norm_scale = np.float32(1.0 / math.sqrt(NLON))
    cosine = (np.cos(angles) * norm_scale).astype(ml_dtypes.bfloat16)
    sine = (-np.sin(angles) * norm_scale).astype(ml_dtypes.bfloat16)
    both = np.stack([cosine, sine], axis=1).reshape(NLON, 2, STEPS, BLOCK)
    forward = np.ascontiguousarray(both.transpose(2, 0, 1, 3)).reshape(STEPS, NLON, 2 * BLOCK)
    inverse = np.ascontiguousarray(forward.transpose(0, 2, 1))
    return forward, inverse


def iota(shape, dim):
    return lax.broadcasted_iota(jnp.int32, shape, dim)


def slot_choice(order, step):
    number = iota((BLOCK, MM), 0) + step * BLOCK
    return jnp.where(order == number, 1.0, 0.0).astype(BF16)


def slot_order(slots):
    digits = jnp.concatenate([slots // 32, slots % 32], axis=0).astype(F32).astype(BF16)
    source = iota((LANES, MM), 0)
    to = iota((LANES, MM), 1)
    choice = jnp.where(source == to % 8 * 16 + to // LANES * 2 + to // LATS % 2, 1.0, 0.0).astype(BF16)
    moved = jnp.dot(digits, choice, preferred_element_type=F32)
    row = iota((16, MM), 0)
    mine = row % 8 == iota((16, MM), 1) % LATS // 8
    value = jnp.where(mine, moved * jnp.where(row < 8, 32.0, 1.0), 0.0)
    return jnp.sum(value, axis=0, keepdims=True).astype(jnp.int32)


def kept_column(kept):
    shape = (ROWS, BAND)
    chosen = jnp.where(iota(shape, 1) == iota(shape, 0) // LEV, kept.astype(F32), 0.0)
    return jnp.sum(chosen, axis=1, keepdims=True).astype(jnp.int32)


def weight_column(weights, lat):
    shape = (ROWS, NLAT // 2)
    latitude = lat * BAND + iota(shape, 0) // LEV
    chosen = jnp.where(iota(shape, 1) == jnp.minimum(latitude, NLAT - 1 - latitude), weights, 0.0)
    return jnp.sum(chosen, axis=1, keepdims=True)


def row_choice(southern):
    to = iota((2 * ROWS, 2 * ROWS), 0)
    source = iota((2 * ROWS, 2 * ROWS), 1)
    band = to // (2 * LEV)
    band = jnp.where(southern, BAND - 1 - band, band)
    wanted = (to % 2) * ROWS + band * LEV + to // 2 % LEV
    return jnp.where(source == wanted, 1.0, 0.0).astype(BF16)


def fourier_kernel(
    lat_ref, kept_hbm, weights_hbm, slots_hbm, x_hbm, table_hbm, o_ref, order_ref, kept_v, weights_v, slots_v, x_v,
    table_v, rows, acc, sems
):
    small = [
        pltpu.make_async_copy(slots_hbm, slots_v, sems.at[0]),
        pltpu.make_async_copy(x_hbm, x_v, sems.at[1]),
        pltpu.make_async_copy(kept_hbm, kept_v, sems.at[2]),
        pltpu.make_async_copy(weights_hbm, weights_v, sems.at[3]),
    ]
    blocks = [pltpu.make_async_copy(table_hbm.at[i], table_v.at[i], sems.at[4 + i]) for i in range(STEPS)]
    for copy in small + blocks:
        copy.start()
    lat = lat_ref[0]
    small[0].wait()
    order = slot_order(slots_v[...])
    order_ref[...] = order
    small[1].wait()
    for group in range(ROWS // 16):
        rows[16 * group : 16 * group + 16, :] = jnp.concatenate(
            [x_v[4 * group + i].astype(F32) for i in range(4)], axis=0
        ).astype(BF16)
    small[2].wait()
    small[3].wait()
    kept = kept_column(kept_v[...])
    weight = weight_column(weights_v[...], lat)
    for step in range(STEPS):
        blocks[step].wait()
        raw = jnp.dot(rows[...], table_v[step], preferred_element_type=F32)
        number = iota((ROWS, BLOCK), 1) + step * BLOCK
        scale = jnp.where(number < kept, weight, 0.0)
        fourier = jnp.concatenate([raw[:, :BLOCK] * scale, raw[:, BLOCK:] * scale], axis=0).astype(BF16)
        part = jnp.dot(fourier, slot_choice(order, step), preferred_element_type=F32)
        if step == 0:
            acc[...] = part
        else:
            acc[...] += part
    choice = row_choice(lat >= NORTH)
    moved = jnp.dot(choice, acc[...].astype(BF16), preferred_element_type=F32).astype(BF16)
    for b in range(LEVS):
        o_ref[b] = moved[:, b * LANES : (b + 1) * LANES]


def gather_kernel(y_ref, o_ref, rows):
    for j in range(BAND):
        block = jnp.concatenate([y_ref[b, 8 * j : 8 * j + 8, :].astype(F32) for b in range(LEVS)], axis=0)
        turned = block.T
        rows[:, j % 4, (j // 4) * LANES : (j // 4 + 1) * LANES] = jnp.concatenate(
            [turned[:LATS], turned[LATS:]], axis=1
        )
    o_ref[...] = rows[...].astype(BF16)


def scatter_kernel(z_ref, o_ref, rows):
    rows[...] = z_ref[...].astype(F32)
    for j in range(BAND):
        block = rows[:, j % 4, (j // 4) * LANES : (j // 4 + 1) * LANES]
        turned = jnp.concatenate([block[:, :LATS], block[:, LATS:]], axis=0).T
        for b in range(LEVS):
            o_ref[b, 8 * j : 8 * j + 8, :] = turned[8 * b : 8 * b + 8].astype(BF16)
    power = jnp.sum(rows[:, :, DATA:], axis=0)
    power = jnp.concatenate([power[:, :LANES], power[:, LANES:]], axis=0)
    high = power.astype(BF16)
    both = jnp.concatenate([high.astype(F32), power - high.astype(F32)], axis=0).astype(BF16)
    for b in range(LEVS):
        o_ref[b, 2 * ROWS :, :] = both


def legendre_kernel(waves_ref, diffusion_ref, z_ref, table_ref, spectral_ref, o_ref, comb):
    for group in range(NORTH * TILES // 4):
        north, south = [], []
        for u in range(4 * group, 4 * group + 4):
            a, tile = divmod(u, TILES)
            lanes = slice(tile * LANES, (tile + 1) * LANES)
            north.append(z_ref[a, :, lanes].astype(F32))
            south.append(z_ref[LATS - 1 - a, :, lanes].astype(F32))
        north = jnp.concatenate(north, axis=0)
        south = jnp.concatenate(south, axis=0)
        comb[0, 16 * group : 16 * group + 16, :] = north + south
        comb[1, 16 * group : 16 * group + 16, :] = north - south
    column = iota((64, HALF), 1)
    power = [jnp.zeros((1, HALF), F32), jnp.zeros((1, HALF), F32)]
    halves = []
    for q in range(2):
        left = comb[q].T.astype(BF16)
        parts = []
        for t in range(2):
            wave = waves_ref[t]
            raw = jnp.dot(left[64 * t : 64 * t + 64], table_ref[t, q], preferred_element_type=F32)
            degree = wave + 2 * column + q
            spectral = jnp.where(degree < MM, raw, 0.0)
            spectral_ref[t, q] = spectral
            degree = degree.astype(F32)
            ratio = degree * (degree + 1.0) / (MM * (MM + 1.0))
            damped = (spectral / (1.0 + diffusion_ref[...] * ratio * ratio)).astype(BF16)
            parts.append(
                lax.dot_general(
                    table_ref[t, q], damped, (((1,), (1,)), ((), ())), preferred_element_type=F32
                )
            )
            energy = jnp.sum(spectral * spectral, axis=0, keepdims=True)
            first = wave + q
            moved = pltpu.roll(jnp.broadcast_to(energy, (8, HALF)), first // 2 % HALF, 1)[:1]
            for odd in range(2):
                power[odd] += jnp.where(first % 2 == odd, moved, 0.0)
        halves.append(jnp.concatenate(parts, axis=1))
    source = iota((LANES, 2 * LANES), 0)
    to = iota((LANES, 2 * LANES), 1)
    natural = jnp.zeros((8, 2 * LANES), F32)
    for odd in range(2):
        quarters = [power[odd][:, i * LANES : (i + 1) * LANES] for i in range(4)]
        quarters = jnp.concatenate(quarters + quarters, axis=0).astype(BF16)
        choice = jnp.where(to == 2 * source + odd, 1.0, 0.0).astype(BF16)
        natural += jnp.dot(quarters, choice, preferred_element_type=F32)
    natural = natural[:4].astype(BF16)
    for a in range(LATS):
        o_ref[a, :, DATA:] = natural
    north = halves[0] + halves[1]
    south = halves[0] - halves[1]
    for u in range(NORTH * TILES):
        a, tile = divmod(u, TILES)
        lanes = slice(tile * LANES, (tile + 1) * LANES)
        o_ref[a, :, lanes] = north[4 * u : 4 * u + 4].astype(BF16)
        o_ref[LATS - 1 - a, :, lanes] = south[4 * u : 4 * u + 4].astype(BF16)


def grid_kernel(lat_ref, kept_ref, order_ref, y_ref, table_ref, o_ref, spectrum_ref, acc):
    kept = kept_column(kept_ref[...])
    choice = row_choice(lat_ref[0] >= NORTH)
    back = jnp.concatenate([y_ref[b, : 2 * ROWS, :] for b in range(LEVS)], axis=1)
    rows = lax.dot_general(choice, back, (((0,), (0,)), ((), ())), preferred_element_type=F32).astype(BF16)
    for step in range(STEPS):
        numbered = lax.dot_general(
            rows, slot_choice(order_ref[...], step), (((1,), (1,)), ((), ())), preferred_element_type=F32
        )
        mask = iota((ROWS, BLOCK), 1) + step * BLOCK < kept
        coefficients = jnp.concatenate(
            [jnp.where(mask, numbered[:ROWS], 0.0), jnp.where(mask, numbered[ROWS:], 0.0)], axis=1
        ).astype(BF16)
        part = jnp.dot(coefficients, table_ref[step], preferred_element_type=F32)
        if step == 0:
            acc[...] = part
        else:
            acc[...] += part
    for j in range(BAND):
        o_ref[j] = acc[LEV * j : LEV * (j + 1), :] * math.sqrt(NLON / MM)
    power = jnp.zeros((16, LANES), F32)
    for b in range(LEVS):
        power += y_ref[b, 2 * ROWS :, :].astype(F32)
    power = power[:8] + power[8:]
    power = jnp.concatenate([power[i // 2 + 4 * (i % 2)][None] for i in range(8)], axis=0)
    degree = (iota((8, LANES), 0) * LANES + iota((8, LANES), 1)).astype(F32)
    spectrum_ref[...] = power / (2.0 * LEVELS * (degree + 1.0))


def exchange(x, axes):
    return lax.all_to_all(x, axes, split_axis=0, concat_axis=0, tiled=True)


def body(grid_fields, legendre, weights, kept_waves, slot_wavenumber, diffusion):
    forward_table, inverse_table = dft_tables()
    lat = lax.axis_index(("y", "z")).astype(jnp.int32)
    lev = lax.axis_index(("x", "core")).astype(jnp.int32)
    lat_ref = lat.reshape(1)
    waves = lax.dynamic_slice_in_dim(slot_wavenumber, (lat * LEVS + lev) * 2, 2)
    kept_row = kept_waves.reshape(1, BAND)
    chunk = (LATS, 4, DATA + 2 * LANES)

    sent, order = pl.pallas_call(
        fourier_kernel,
        in_specs=[SMEM, HBM, HBM, HBM, HBM, HBM],
        out_specs=[VMEM, VMEM],
        out_shape=[
            jax.ShapeDtypeStruct((LEVS, 2 * ROWS, LANES), BF16),
            jax.ShapeDtypeStruct((1, MM), jnp.int32),
        ],
        scratch_shapes=[
            pltpu.VMEM((1, BAND), jnp.int32),
            pltpu.VMEM((1, NLAT // 2), F32),
            pltpu.VMEM((8, LANES), jnp.int32),
            pltpu.VMEM((BAND, LEV, NLON), BF16),
            pltpu.VMEM((STEPS, NLON, 2 * BLOCK), BF16),
            pltpu.VMEM((ROWS, NLON), BF16),
            pltpu.VMEM((2 * ROWS, MM), F32),
            pltpu.SemaphoreType.DMA((4 + STEPS,)),
        ],
        compiler_params=PARAMS,
        name="fourier",
    )(
        lat_ref,
        kept_row,
        weights.reshape(1, NLAT // 2),
        slot_wavenumber.reshape(8, LANES),
        grid_fields.transpose(1, 0, 2),
        jnp.asarray(forward_table),
    )
    arrived = exchange(sent, ("x", "core"))
    gathered = pl.pallas_call(
        gather_kernel,
        in_specs=[VMEM],
        out_specs=VMEM,
        out_shape=jax.ShapeDtypeStruct((LATS, 4, DATA), BF16),
        scratch_shapes=[pltpu.VMEM((LATS, 4, DATA), F32)],
        compiler_params=PARAMS,
        name="gather",
    )(arrived)
    gathered = exchange(gathered, ("y", "z"))
    spectral, back = pl.pallas_call(
        legendre_kernel,
        in_specs=[SMEM, VMEM, VMEM, VMEM],
        out_specs=[VMEM, VMEM],
        out_shape=[
            jax.ShapeDtypeStruct((2, 2, 2 * LEVELS, HALF), F32),
            jax.ShapeDtypeStruct(chunk, BF16),
        ],
        scratch_shapes=[pltpu.VMEM((2, NLAT // 2, LANES), F32)],
        compiler_params=PARAMS,
        name="legendre",
    )(waves, jnp.repeat(diffusion, 2).reshape(2 * LEVELS, 1), gathered, legendre)
    back = exchange(back, ("y", "z"))
    scattered = pl.pallas_call(
        scatter_kernel,
        in_specs=[VMEM],
        out_specs=VMEM,
        out_shape=jax.ShapeDtypeStruct((LEVS, 2 * ROWS + 16, LANES), BF16),
        scratch_shapes=[pltpu.VMEM(chunk, F32)],
        compiler_params=PARAMS,
        name="scatter",
    )(back)
    returned = exchange(scattered, ("x", "core"))
    grid_out, spectrum = pl.pallas_call(
        grid_kernel,
        in_specs=[SMEM, VMEM, VMEM, VMEM, VMEM],
        out_specs=[VMEM, VMEM],
        out_shape=[
            jax.ShapeDtypeStruct((BAND, LEV, NLON), F32),
            jax.ShapeDtypeStruct((8, LANES), F32),
        ],
        scratch_shapes=[pltpu.VMEM((ROWS, NLON), F32)],
        compiler_params=PARAMS,
        name="grid",
    )(lat_ref, kept_row, order, returned, jnp.asarray(inverse_table))
    return (
        grid_out.transpose(1, 0, 2),
        spectral.reshape(2, 2, LEVELS, 2, HALF),
        spectrum.reshape(MM),
    )


def solution(mesh):
    fine = Mesh(mesh.devices.reshape(4, 16, 4, 2), ("y", "z", "x", "core"))
    lat, lev = ("y", "z"), ("x", "core")
    both = lat + lev
    in_specs = (P(lev, lat, None), P(both, None, None, None), P(), P(lat), P(), P())
    out_specs = (P(lev, lat, None), P(both, None, None, None, None), P())
    return jax.shard_map(body, mesh=fine, in_specs=in_specs, out_specs=out_specs, check_vma=False)
```

```python
import math

import jax
import jax.numpy as jnp
import ml_dtypes
import numpy as np
from jax import lax
from jax.experimental import pallas as pl
from jax.experimental.pallas import tpu as pltpu
from jax.sharding import Mesh
from jax.sharding import PartitionSpec as P

NLAT = 1280
NLON = 2688
MM = 1024
HALF = MM // 2
LEVELS = 32
BAND = 20
LEV = 4
ROWS = BAND * LEV
LATS = 64
LEVS = 8
NORTH = LATS // 2
QUARTER = NLON // 4
STEPS = 4
BLOCK = MM // STEPS
TILES = BAND // 4
LANES = 128
DATA = TILES * LANES

BF16 = jnp.bfloat16
F32 = jnp.float32
VMEM = pl.BlockSpec(memory_space=pltpu.VMEM)
HBM = pl.BlockSpec(memory_space=pltpu.HBM)
SMEM = pl.BlockSpec(memory_space=pltpu.SMEM)
PARAMS = pltpu.CompilerParams(vmem_limit_bytes=48 * 1024 * 1024)


def dft_tables():
    sample = np.arange(QUARTER, dtype=np.int32)[:, None]
    number = np.arange(MM, dtype=np.int32)[None, :]
    angles = (sample * number % NLON).astype(np.float32) * np.float32(2.0 * math.pi / NLON)
    norm_scale = np.float32(1.0 / math.sqrt(NLON))
    cosine = (np.cos(angles) * norm_scale).astype(ml_dtypes.bfloat16)
    sine = (-np.sin(angles) * norm_scale).astype(ml_dtypes.bfloat16)
    both = np.stack([cosine, sine], axis=1).reshape(QUARTER, 2, BLOCK, STEPS)
    forward = np.ascontiguousarray(both.transpose(3, 0, 1, 2)).reshape(STEPS, QUARTER, 2 * BLOCK)
    inverse = np.ascontiguousarray(forward.transpose(0, 2, 1))
    return forward, inverse


def iota(shape, dim):
    return lax.broadcasted_iota(jnp.int32, shape, dim)


def slot_choice(order, step):
    number = iota((BLOCK, MM), 0) * STEPS + step
    return jnp.where(order == number, 1.0, 0.0).astype(BF16)


def slot_order(slots):
    digits = jnp.concatenate([slots // 32, slots % 32], axis=0).astype(F32).astype(BF16)
    source = iota((LANES, MM), 0)
    to = iota((LANES, MM), 1)
    choice = jnp.where(source == to % 8 * 16 + to // LANES * 2 + to // LATS % 2, 1.0, 0.0).astype(BF16)
    moved = jnp.dot(digits, choice, preferred_element_type=F32)
    row = iota((16, MM), 0)
    mine = row % 8 == iota((16, MM), 1) % LATS // 8
    value = jnp.where(mine, moved * jnp.where(row < 8, 32.0, 1.0), 0.0)
    return jnp.sum(value, axis=0, keepdims=True).astype(jnp.int32)


def latitude_column(scalars, zero):
    band = iota((ROWS, 1), 0) // LEV
    column = jnp.full((ROWS, 1), zero)
    for j in range(BAND):
        column = jnp.where(band == j, scalars[j], column)
    return column


def class_mask(kept, step):
    return iota((ROWS, BLOCK), 1) * STEPS + step < kept


def row_choice(southern):
    to = iota((2 * ROWS, 2 * ROWS), 0)
    source = iota((2 * ROWS, 2 * ROWS), 1)
    band = to // (2 * LEV)
    band = jnp.where(southern, BAND - 1 - band, band)
    wanted = (to % 2) * ROWS + band * LEV + to // 2 % LEV
    return jnp.where(source == wanted, 1.0, 0.0).astype(BF16)


def fourier_kernel(
    lat_ref, kept_hbm, weights_hbm, slots_hbm, x_hbm, table_hbm, o_ref, order_ref, kept_ref, kept_s, weights_s, slots_v, x_v,
    table_v, even, odd, acc, sems
):
    small = [
        pltpu.make_async_copy(slots_hbm, slots_v, sems.at[0]),
        pltpu.make_async_copy(x_hbm, x_v, sems.at[1]),
        pltpu.make_async_copy(kept_hbm, kept_s, sems.at[2]),
        pltpu.make_async_copy(weights_hbm, weights_s, sems.at[3]),
    ]
    blocks = [pltpu.make_async_copy(table_hbm.at[i], table_v.at[i], sems.at[4 + i]) for i in range(STEPS)]
    for copy in small + blocks:
        copy.start()
    lat = lat_ref[0]
    small[0].wait()
    order = slot_order(slots_v[...])
    order_ref[...] = order
    small[2].wait()
    small[3].wait()
    kept = latitude_column([kept_s[j] for j in range(BAND)], jnp.int32(0))
    kept_ref[...] = kept
    latitudes = [lat * BAND + j for j in range(BAND)]
    weight = latitude_column([weights_s[jnp.minimum(i, NLAT - 1 - i)] for i in latitudes], F32(0.0))
    small[1].wait()

    def put(ref, place, value):
        high = value.astype(BF16)
        low = (value - high.astype(F32)).astype(BF16)
        for part, half in enumerate((high, low)):
            ref[pl.ds(place + part * ROWS, 16), :] = half

    for group in range(ROWS // 16):
        x = jnp.concatenate([x_v[4 * group + i].astype(F32) for i in range(4)], axis=0)
        x = [x[:, q * QUARTER : (q + 1) * QUARTER] for q in range(4)]
        sums = x[0] + x[2], x[1] + x[3]
        put(even.at[0], 16 * group, sums[0] + sums[1])
        put(even.at[1], 16 * group, sums[0] - sums[1])
        put(odd, 16 * group, x[0] - x[2])
        put(odd, 16 * group + 2 * ROWS, x[1] - x[3])
    for step in range(STEPS):
        blocks[step].wait()
        if step % 2 == 0:
            raw = jnp.dot(even[step // 2], table_v[step], preferred_element_type=F32)
            raw = raw[:ROWS] + raw[ROWS:]
            real, imaginary = raw[:, :BLOCK], raw[:, BLOCK:]
        else:
            raw = jnp.dot(odd[...], table_v[step], preferred_element_type=F32)
            first = raw[:ROWS] + raw[ROWS : 2 * ROWS]
            second = raw[2 * ROWS : 3 * ROWS] + raw[3 * ROWS :]
            if step == 3:
                second = -second
            real = first[:, :BLOCK] + second[:, BLOCK:]
            imaginary = first[:, BLOCK:] - second[:, :BLOCK]
        scale = jnp.where(class_mask(kept, step), weight, 0.0)
        fourier = jnp.concatenate([real * scale, imaginary * scale], axis=0).astype(BF16)
        part = jnp.dot(fourier, slot_choice(order, step), preferred_element_type=F32)
        if step == 0:
            acc[...] = part
        else:
            acc[...] += part
    choice = row_choice(lat >= NORTH)
    moved = jnp.dot(choice, acc[...].astype(BF16), preferred_element_type=F32).astype(BF16)
    for b in range(LEVS):
        o_ref[b] = moved[:, b * LANES : (b + 1) * LANES]


def gather_kernel(y_ref, o_ref, rows):
    for j in range(BAND):
        block = jnp.concatenate([y_ref[b, 8 * j : 8 * j + 8, :].astype(F32) for b in range(LEVS)], axis=0)
        turned = block.T
        rows[:, j % 4, (j // 4) * LANES : (j // 4 + 1) * LANES] = jnp.concatenate(
            [turned[:LATS], turned[LATS:]], axis=1
        )
    o_ref[...] = rows[...].astype(BF16)


def scatter_kernel(z_ref, o_ref, rows):
    rows[...] = z_ref[...].astype(F32)
    for j in range(BAND):
        block = rows[:, j % 4, (j // 4) * LANES : (j // 4 + 1) * LANES]
        turned = jnp.concatenate([block[:, :LATS], block[:, LATS:]], axis=0).T
        for b in range(LEVS):
            o_ref[b, 8 * j : 8 * j + 8, :] = turned[8 * b : 8 * b + 8].astype(BF16)
    power = jnp.sum(rows[:, :, DATA:], axis=0)
    power = jnp.concatenate([power[:, :LANES], power[:, LANES:]], axis=0)
    high = power.astype(BF16)
    both = jnp.concatenate([high.astype(F32), power - high.astype(F32)], axis=0).astype(BF16)
    for b in range(LEVS):
        o_ref[b, 2 * ROWS :, :] = both


def legendre_kernel(waves_ref, diffusion_ref, z_ref, table_ref, spectral_ref, o_ref, comb):
    for group in range(NORTH * TILES // 4):
        north, south = [], []
        for u in range(4 * group, 4 * group + 4):
            a, tile = divmod(u, TILES)
            lanes = slice(tile * LANES, (tile + 1) * LANES)
            north.append(z_ref[a, :, lanes].astype(F32))
            south.append(z_ref[LATS - 1 - a, :, lanes].astype(F32))
        north = jnp.concatenate(north, axis=0)
        south = jnp.concatenate(south, axis=0)
        comb[0, 16 * group : 16 * group + 16, :] = north + south
        comb[1, 16 * group : 16 * group + 16, :] = north - south
    column = iota((64, HALF), 1)
    power = [jnp.zeros((1, HALF), F32), jnp.zeros((1, HALF), F32)]
    halves = []
    for q in range(2):
        left = comb[q].T.astype(BF16)
        parts = []
        for t in range(2):
            wave = waves_ref[t]
            raw = jnp.dot(left[64 * t : 64 * t + 64], table_ref[t, q], preferred_element_type=F32)
            degree = wave + 2 * column + q
            spectral = jnp.where(degree < MM, raw, 0.0)
            spectral_ref[t, q] = spectral
            degree = degree.astype(F32)
            ratio = degree * (degree + 1.0) / (MM * (MM + 1.0))
            damped = (spectral / (1.0 + diffusion_ref[...] * ratio * ratio)).astype(BF16)
            parts.append(
                lax.dot_general(
                    table_ref[t, q], damped, (((1,), (1,)), ((), ())), preferred_element_type=F32
                )
            )
            energy = jnp.sum(spectral * spectral, axis=0, keepdims=True)
            first = wave + q
            moved = pltpu.roll(jnp.broadcast_to(energy, (8, HALF)), first // 2 % HALF, 1)[:1]
            for odd in range(2):
                power[odd] += jnp.where(first % 2 == odd, moved, 0.0)
        halves.append(jnp.concatenate(parts, axis=1))
    source = iota((LANES, 2 * LANES), 0)
    to = iota((LANES, 2 * LANES), 1)
    natural = jnp.zeros((8, 2 * LANES), F32)
    for odd in range(2):
        quarters = [power[odd][:, i * LANES : (i + 1) * LANES] for i in range(4)]
        quarters = jnp.concatenate(quarters + quarters, axis=0).astype(BF16)
        choice = jnp.where(to == 2 * source + odd, 1.0, 0.0).astype(BF16)
        natural += jnp.dot(quarters, choice, preferred_element_type=F32)
    natural = natural[:4].astype(BF16)
    for a in range(LATS):
        o_ref[a, :, DATA:] = natural
    north = halves[0] + halves[1]
    south = halves[0] - halves[1]
    for u in range(NORTH * TILES):
        a, tile = divmod(u, TILES)
        lanes = slice(tile * LANES, (tile + 1) * LANES)
        o_ref[a, :, lanes] = north[4 * u : 4 * u + 4].astype(BF16)
        o_ref[LATS - 1 - a, :, lanes] = south[4 * u : 4 * u + 4].astype(BF16)


def grid_kernel(lat_ref, kept_ref, order_ref, y_ref, table_ref, o_ref, spectrum_ref):
    kept = kept_ref[...]
    choice = row_choice(lat_ref[0] >= NORTH)
    back = jnp.concatenate([y_ref[b, : 2 * ROWS, :] for b in range(LEVS)], axis=1)
    rows = lax.dot_general(choice, back, (((0,), (0,)), ((), ())), preferred_element_type=F32).astype(BF16)
    parts = []
    for step in range(STEPS):
        numbered = lax.dot_general(
            rows, slot_choice(order_ref[...], step), (((1,), (1,)), ((), ())), preferred_element_type=F32
        )
        mask = class_mask(kept, step)
        real = jnp.where(mask, numbered[:ROWS], 0.0)
        imaginary = jnp.where(mask, numbered[ROWS:], 0.0)
        left = jnp.concatenate([real, imaginary], axis=1)
        if step == 1:
            left = jnp.concatenate([left, jnp.concatenate([-imaginary, real], axis=1)], axis=0)
        if step == 3:
            left = jnp.concatenate([left, jnp.concatenate([imaginary, -real], axis=1)], axis=0)
        parts.append(jnp.dot(left.astype(BF16), table_ref[step], preferred_element_type=F32))
    odd = parts[1] + parts[3]
    plus, minus = parts[0] + parts[2], parts[0] - parts[2]
    quarters = [plus + odd[:ROWS], minus + odd[ROWS:], plus - odd[:ROWS], minus - odd[ROWS:]]
    points = jnp.concatenate(quarters, axis=1) * math.sqrt(NLON / MM)
    for j in range(BAND):
        o_ref[j] = points[LEV * j : LEV * (j + 1), :]
    power = jnp.zeros((16, LANES), F32)
    for b in range(LEVS):
        power += y_ref[b, 2 * ROWS :, :].astype(F32)
    power = power[:8] + power[8:]
    power = jnp.concatenate([power[i // 2 + 4 * (i % 2)][None] for i in range(8)], axis=0)
    degree = (iota((8, LANES), 0) * LANES + iota((8, LANES), 1)).astype(F32)
    spectrum_ref[...] = power / (2.0 * LEVELS * (degree + 1.0))


def in_hbm(x):
    return pltpu.with_memory_space_constraint(x, pltpu.HBM)


def exchange(x, axes):
    return lax.all_to_all(x, axes, split_axis=0, concat_axis=0, tiled=True)


def body(grid_fields, legendre, weights, kept_waves, slot_wavenumber, diffusion):
    forward_table, inverse_table = dft_tables()
    lat = lax.axis_index(("y", "z")).astype(jnp.int32)
    lev = lax.axis_index(("x", "core")).astype(jnp.int32)
    lat_ref = lat.reshape(1)
    waves = lax.dynamic_slice_in_dim(slot_wavenumber, (lat * LEVS + lev) * 2, 2)
    chunk = (LATS, 4, DATA + 2 * LANES)

    sent, order, kept = pl.pallas_call(
        fourier_kernel,
        in_specs=[SMEM, HBM, HBM, HBM, HBM, HBM],
        out_specs=[VMEM, VMEM, VMEM],
        out_shape=[
            jax.ShapeDtypeStruct((LEVS, 2 * ROWS, LANES), BF16),
            jax.ShapeDtypeStruct((1, MM), jnp.int32),
            jax.ShapeDtypeStruct((ROWS, 1), jnp.int32),
        ],
        scratch_shapes=[
            pltpu.SMEM((BAND,), jnp.int32),
            pltpu.SMEM((NLAT // 2,), F32),
            pltpu.VMEM((8, LANES), jnp.int32),
            pltpu.VMEM((BAND, LEV, NLON), BF16),
            pltpu.VMEM((STEPS, QUARTER, 2 * BLOCK), BF16),
            pltpu.VMEM((2, 2 * ROWS, QUARTER), BF16),
            pltpu.VMEM((4 * ROWS, QUARTER), BF16),
            pltpu.VMEM((2 * ROWS, MM), F32),
            pltpu.SemaphoreType.DMA((4 + STEPS,)),
        ],
        compiler_params=PARAMS,
        name="fourier",
    )(
        lat_ref,
        in_hbm(kept_waves),
        in_hbm(weights),
        in_hbm(slot_wavenumber.reshape(8, LANES)),
        in_hbm(grid_fields.transpose(1, 0, 2)),
        in_hbm(jnp.asarray(forward_table)),
    )
    arrived = exchange(sent, ("x", "core"))
    gathered = pl.pallas_call(
        gather_kernel,
        in_specs=[VMEM],
        out_specs=VMEM,
        out_shape=jax.ShapeDtypeStruct((LATS, 4, DATA), BF16),
        scratch_shapes=[pltpu.VMEM((LATS, 4, DATA), F32)],
        compiler_params=PARAMS,
        name="gather",
    )(arrived)
    gathered = exchange(gathered, ("y", "z"))
    spectral, back = pl.pallas_call(
        legendre_kernel,
        in_specs=[SMEM, VMEM, VMEM, VMEM],
        out_specs=[VMEM, VMEM],
        out_shape=[
            jax.ShapeDtypeStruct((2, 2, 2 * LEVELS, HALF), F32),
            jax.ShapeDtypeStruct(chunk, BF16),
        ],
        scratch_shapes=[pltpu.VMEM((2, NLAT // 2, LANES), F32)],
        compiler_params=PARAMS,
        name="legendre",
    )(waves, jnp.repeat(diffusion, 2).reshape(2 * LEVELS, 1), gathered, legendre)
    back = exchange(back, ("y", "z"))
    scattered = pl.pallas_call(
        scatter_kernel,
        in_specs=[VMEM],
        out_specs=VMEM,
        out_shape=jax.ShapeDtypeStruct((LEVS, 2 * ROWS + 16, LANES), BF16),
        scratch_shapes=[pltpu.VMEM(chunk, F32)],
        compiler_params=PARAMS,
        name="scatter",
    )(back)
    returned = exchange(scattered, ("x", "core"))
    grid_out, spectrum = pl.pallas_call(
        grid_kernel,
        in_specs=[SMEM, VMEM, VMEM, VMEM, VMEM],
        out_specs=[VMEM, VMEM],
        out_shape=[
            jax.ShapeDtypeStruct((BAND, LEV, NLON), F32),
            jax.ShapeDtypeStruct((8, LANES), F32),
        ],
        compiler_params=PARAMS,
        name="grid",
    )(lat_ref, kept, order, returned, jnp.asarray(inverse_table))
    return (
        grid_out.transpose(1, 0, 2),
        spectral.reshape(2, 2, LEVELS, 2, HALF),
        spectrum.reshape(MM),
    )


def solution(mesh):
    fine = Mesh(mesh.devices.reshape(4, 16, 4, 2), ("y", "z", "x", "core"))
    lat, lev = ("y", "z"), ("x", "core")
    both = lat + lev
    in_specs = (P(lev, lat, None), P(both, None, None, None), P(), P(lat), P(), P())
    out_specs = (P(lev, lat, None), P(both, None, None, None, None), P())
    return jax.shard_map(body, mesh=fine, in_specs=in_specs, out_specs=out_specs, check_vma=False)
```

```python
import math

import jax
import jax.numpy as jnp
import ml_dtypes
import numpy as np
from jax import lax
from jax.experimental import pallas as pl
from jax.experimental.pallas import tpu as pltpu
from jax.sharding import Mesh
from jax.sharding import PartitionSpec as P

NLAT = 1280
NLON = 2688
MM = 1024
HALF = MM // 2
LEVELS = 32
BAND = 20
LEV = 4
ROWS = BAND * LEV
LATS = 64
LEVS = 8
NORTH = LATS // 2
QUARTER = NLON // 4
STEPS = 4
BLOCK = MM // STEPS
TILES = BAND // 4
LANES = 128
DATA = TILES * LANES

BF16 = jnp.bfloat16
F32 = jnp.float32
VMEM = pl.BlockSpec(memory_space=pltpu.VMEM)
HBM = pl.BlockSpec(memory_space=pltpu.HBM)
SMEM = pl.BlockSpec(memory_space=pltpu.SMEM)
PARAMS = pltpu.CompilerParams(vmem_limit_bytes=48 * 1024 * 1024)


def dft_tables():
    sample = np.arange(QUARTER, dtype=np.int32)[:, None]
    number = np.arange(MM, dtype=np.int32)[None, :]
    angles = (sample * number % NLON).astype(np.float32) * np.float32(2.0 * math.pi / NLON)
    norm_scale = np.float32(1.0 / math.sqrt(NLON))
    cosine = (np.cos(angles) * norm_scale).astype(ml_dtypes.bfloat16)
    sine = (-np.sin(angles) * norm_scale).astype(ml_dtypes.bfloat16)
    both = np.stack([cosine, sine], axis=1).reshape(QUARTER, 2, BLOCK, STEPS)
    forward = np.ascontiguousarray(both.transpose(3, 0, 1, 2)).reshape(STEPS, QUARTER, 2 * BLOCK)
    inverse = np.ascontiguousarray(forward.transpose(0, 2, 1))
    return forward, inverse


def iota(shape, dim):
    return lax.broadcasted_iota(jnp.int32, shape, dim)


def slot_choice(order, step):
    number = iota((BLOCK, MM), 0) * STEPS + step
    return jnp.where(order == number, 1.0, 0.0).astype(BF16)


def slot_order(slots):
    digits = jnp.concatenate([slots // 32, slots % 32], axis=0).astype(F32).astype(BF16)
    source = iota((LANES, MM), 0)
    to = iota((LANES, MM), 1)
    choice = jnp.where(source == to % 8 * 16 + to // LANES * 2 + to // LATS % 2, 1.0, 0.0).astype(BF16)
    moved = jnp.dot(digits, choice, preferred_element_type=F32)
    row = iota((16, MM), 0)
    mine = row % 8 == iota((16, MM), 1) % LATS // 8
    value = jnp.where(mine, moved * jnp.where(row < 8, 32.0, 1.0), 0.0)
    return jnp.sum(value, axis=0, keepdims=True).astype(jnp.int32)


def latitude_column(scalars, zero):
    band = iota((ROWS, 1), 0) // LEV
    column = jnp.full((ROWS, 1), zero)
    for j in range(BAND):
        column = jnp.where(band == j, scalars[j], column)
    return column


def class_mask(kept, step):
    return iota((ROWS, BLOCK), 1) * STEPS + step < kept


def row_choice(southern):
    to = iota((2 * ROWS, 2 * ROWS), 0)
    source = iota((2 * ROWS, 2 * ROWS), 1)
    band = to // (2 * LEV)
    band = jnp.where(southern, BAND - 1 - band, band)
    wanted = (to % 2) * ROWS + band * LEV + to // 2 % LEV
    return jnp.where(source == wanted, 1.0, 0.0).astype(BF16)


def fourier_kernel(
    lat_ref, kept_hbm, weights_hbm, slots_hbm, x_hbm, table_hbm, o_ref, order_ref, kept_ref, kept_s, weights_s, slots_v, x_v,
    table_v, even, odd, acc, sems
):
    small = [
        pltpu.make_async_copy(slots_hbm, slots_v, sems.at[0]),
        pltpu.make_async_copy(x_hbm, x_v, sems.at[1]),
        pltpu.make_async_copy(kept_hbm, kept_s, sems.at[2]),
        pltpu.make_async_copy(weights_hbm, weights_s, sems.at[3]),
    ]
    blocks = [pltpu.make_async_copy(table_hbm.at[i], table_v.at[i], sems.at[4 + i]) for i in range(STEPS)]
    for copy in small + blocks:
        copy.start()
    lat = lat_ref[0]
    small[0].wait()
    order = slot_order(slots_v[...])
    order_ref[...] = order
    small[2].wait()
    small[3].wait()
    kept = latitude_column([kept_s[j] for j in range(BAND)], jnp.int32(0))
    kept_ref[...] = kept
    latitudes = [lat * BAND + j for j in range(BAND)]
    weight = latitude_column([weights_s[jnp.minimum(i, NLAT - 1 - i)] for i in latitudes], F32(0.0))
    small[1].wait()

    def put(ref, place, value):
        high = value.astype(BF16)
        low = (value - high.astype(F32)).astype(BF16)
        for part, half in enumerate((high, low)):
            ref[pl.ds(place + part * ROWS, 16), :] = half

    for group in range(ROWS // 16):
        x = jnp.concatenate([x_v[4 * group + i].astype(F32) for i in range(4)], axis=0)
        x = [x[:, q * QUARTER : (q + 1) * QUARTER] for q in range(4)]
        sums = x[0] + x[2], x[1] + x[3]
        put(even.at[0], 16 * group, sums[0] + sums[1])
        put(even.at[1], 16 * group, sums[0] - sums[1])
        put(odd, 16 * group, x[0] - x[2])
        put(odd, 16 * group + 2 * ROWS, x[1] - x[3])
    for step in range(STEPS):
        blocks[step].wait()
        if step % 2 == 0:
            raw = jnp.dot(even[step // 2], table_v[step], preferred_element_type=F32)
            raw = raw[:ROWS] + raw[ROWS:]
            real, imaginary = raw[:, :BLOCK], raw[:, BLOCK:]
        else:
            raw = jnp.dot(odd[...], table_v[step], preferred_element_type=F32)
            first = raw[:ROWS] + raw[ROWS : 2 * ROWS]
            second = raw[2 * ROWS : 3 * ROWS] + raw[3 * ROWS :]
            if step == 3:
                second = -second
            real = first[:, :BLOCK] + second[:, BLOCK:]
            imaginary = first[:, BLOCK:] - second[:, :BLOCK]
        scale = jnp.where(class_mask(kept, step), weight, 0.0)
        fourier = jnp.concatenate([real * scale, imaginary * scale], axis=0).astype(BF16)
        part = jnp.dot(fourier, slot_choice(order, step), preferred_element_type=F32)
        if step == 0:
            acc[...] = part
        else:
            acc[...] += part
    choice = row_choice(lat >= NORTH)
    moved = jnp.dot(choice, acc[...].astype(BF16), preferred_element_type=F32).astype(BF16)
    for b in range(LEVS):
        o_ref[b] = moved[:, b * LANES : (b + 1) * LANES]


def gather_kernel(y_ref, o_ref, rows):
    for j in range(BAND):
        block = jnp.concatenate([y_ref[b, 8 * j : 8 * j + 8, :].astype(F32) for b in range(LEVS)], axis=0)
        turned = block.T
        rows[:, j % 4, (j // 4) * LANES : (j // 4 + 1) * LANES] = jnp.concatenate(
            [turned[:LATS], turned[LATS:]], axis=1
        )
    o_ref[...] = rows[...].astype(BF16)


def scatter_kernel(z_ref, o_ref, rows):
    rows[...] = z_ref[...].astype(F32)
    for j in range(BAND):
        block = rows[:, j % 4, (j // 4) * LANES : (j // 4 + 1) * LANES]
        turned = jnp.concatenate([block[:, :LATS], block[:, LATS:]], axis=0).T
        for b in range(LEVS):
            o_ref[b, 8 * j : 8 * j + 8, :] = turned[8 * b : 8 * b + 8].astype(BF16)
    power = jnp.sum(rows[:, :, DATA:], axis=0)
    power = jnp.concatenate([power[:, :LANES], power[:, LANES:]], axis=0)
    high = power.astype(BF16)
    both = jnp.concatenate([high.astype(F32), power - high.astype(F32)], axis=0).astype(BF16)
    for b in range(LEVS):
        o_ref[b, 2 * ROWS :, :] = both


def legendre_kernel(
    device_ref, slots_hbm, diffusion_hbm, z_ref, table_ref, spectral_ref, o_ref, slots_s, diffusion_s, comb, sems
):
    copies = [
        pltpu.make_async_copy(slots_hbm, slots_s, sems.at[0]),
        pltpu.make_async_copy(diffusion_hbm, diffusion_s, sems.at[1]),
    ]
    for copy in copies:
        copy.start()
    for group in range(NORTH * TILES // 4):
        north, south = [], []
        for u in range(4 * group, 4 * group + 4):
            a, tile = divmod(u, TILES)
            lanes = slice(tile * LANES, (tile + 1) * LANES)
            north.append(z_ref[a, :, lanes].astype(F32))
            south.append(z_ref[LATS - 1 - a, :, lanes].astype(F32))
        north = jnp.concatenate(north, axis=0)
        south = jnp.concatenate(south, axis=0)
        comb[0, 16 * group : 16 * group + 16, :] = north + south
        comb[1, 16 * group : 16 * group + 16, :] = north - south
    for copy in copies:
        copy.wait()
    column = iota((2 * LEVELS, HALF), 1)
    level = iota((2 * LEVELS, 1), 0) // 2
    diffusion = jnp.zeros((2 * LEVELS, 1), F32)
    for i in range(LEVELS):
        diffusion = jnp.where(level == i, diffusion_s[i], diffusion)
    power = [jnp.zeros((1, HALF), F32), jnp.zeros((1, HALF), F32)]
    halves = []
    for q in range(2):
        left = comb[q].T.astype(BF16)
        parts = []
        for t in range(2):
            wave = slots_s[device_ref[0] * 2 + t]
            raw = jnp.dot(left[64 * t : 64 * t + 64], table_ref[t, q], preferred_element_type=F32)
            degree = wave + 2 * column + q
            spectral = jnp.where(degree < MM, raw, 0.0)
            for level in range(LEVELS):
                spectral_ref[t, q, level] = spectral[2 * level : 2 * level + 2]
            degree = degree.astype(F32)
            ratio = degree * (degree + 1.0) / (MM * (MM + 1.0))
            damped = (spectral / (1.0 + diffusion * ratio * ratio)).astype(BF16)
            parts.append(
                lax.dot_general(
                    table_ref[t, q], damped, (((1,), (1,)), ((), ())), preferred_element_type=F32
                )
            )
            energy = jnp.sum(spectral * spectral, axis=0, keepdims=True)
            first = wave + q
            moved = pltpu.roll(jnp.broadcast_to(energy, (8, HALF)), first // 2 % HALF, 1)[:1]
            for odd in range(2):
                power[odd] += jnp.where(first % 2 == odd, moved, 0.0)
        halves.append(jnp.concatenate(parts, axis=1))
    source = iota((LANES, 2 * LANES), 0)
    to = iota((LANES, 2 * LANES), 1)
    natural = jnp.zeros((8, 2 * LANES), F32)
    for odd in range(2):
        quarters = [power[odd][:, i * LANES : (i + 1) * LANES] for i in range(4)]
        quarters = jnp.concatenate(quarters + quarters, axis=0).astype(BF16)
        choice = jnp.where(to == 2 * source + odd, 1.0, 0.0).astype(BF16)
        natural += jnp.dot(quarters, choice, preferred_element_type=F32)
    natural = natural[:4].astype(BF16)
    for a in range(LATS):
        o_ref[a, :, DATA:] = natural
    north = halves[0] + halves[1]
    south = halves[0] - halves[1]
    for u in range(NORTH * TILES):
        a, tile = divmod(u, TILES)
        lanes = slice(tile * LANES, (tile + 1) * LANES)
        o_ref[a, :, lanes] = north[4 * u : 4 * u + 4].astype(BF16)
        o_ref[LATS - 1 - a, :, lanes] = south[4 * u : 4 * u + 4].astype(BF16)


def grid_kernel(lat_ref, kept_ref, order_ref, y_ref, table_hbm, o_ref, spectrum_ref, table_v, sems):
    blocks = [pltpu.make_async_copy(table_hbm.at[i], table_v.at[i], sems.at[i]) for i in range(STEPS)]
    for copy in blocks:
        copy.start()
    kept = kept_ref[...]
    choice = row_choice(lat_ref[0] >= NORTH)
    back = jnp.concatenate([y_ref[b, : 2 * ROWS, :] for b in range(LEVS)], axis=1)
    rows = lax.dot_general(choice, back, (((0,), (0,)), ((), ())), preferred_element_type=F32).astype(BF16)
    parts = []
    for step in range(STEPS):
        numbered = lax.dot_general(
            rows, slot_choice(order_ref[...], step), (((1,), (1,)), ((), ())), preferred_element_type=F32
        )
        mask = class_mask(kept, step)
        real = jnp.where(mask, numbered[:ROWS], 0.0)
        imaginary = jnp.where(mask, numbered[ROWS:], 0.0)
        left = jnp.concatenate([real, imaginary], axis=1)
        if step == 1:
            left = jnp.concatenate([left, jnp.concatenate([-imaginary, real], axis=1)], axis=0)
        if step == 3:
            left = jnp.concatenate([left, jnp.concatenate([imaginary, -real], axis=1)], axis=0)
        blocks[step].wait()
        parts.append(jnp.dot(left.astype(BF16), table_v[step], preferred_element_type=F32))
    odd = parts[1] + parts[3]
    plus, minus = parts[0] + parts[2], parts[0] - parts[2]
    quarters = [plus + odd[:ROWS], minus + odd[ROWS:], plus - odd[:ROWS], minus - odd[ROWS:]]
    points = jnp.concatenate(quarters, axis=1) * math.sqrt(NLON / MM)
    for j in range(BAND):
        o_ref[j] = points[LEV * j : LEV * (j + 1), :]
    power = jnp.zeros((16, LANES), F32)
    for b in range(LEVS):
        power += y_ref[b, 2 * ROWS :, :].astype(F32)
    power = power[:8] + power[8:]
    power = jnp.concatenate([power[i // 2 + 4 * (i % 2)][None] for i in range(8)], axis=0)
    degree = (iota((8, LANES), 0) * LANES + iota((8, LANES), 1)).astype(F32)
    spectrum_ref[...] = power / (2.0 * LEVELS * (degree + 1.0))


def in_hbm(x):
    return pltpu.with_memory_space_constraint(x, pltpu.HBM)


def exchange(x, axes):
    return lax.all_to_all(x, axes, split_axis=0, concat_axis=0, tiled=True)


def body(grid_fields, legendre, weights, kept_waves, slot_wavenumber, diffusion):
    forward_table, inverse_table = dft_tables()
    lat = lax.axis_index(("y", "z")).astype(jnp.int32)
    lev = lax.axis_index(("x", "core")).astype(jnp.int32)
    lat_ref = lat.reshape(1)
    chunk = (LATS, 4, DATA + 2 * LANES)

    sent, order, kept = pl.pallas_call(
        fourier_kernel,
        in_specs=[SMEM, HBM, HBM, HBM, HBM, HBM],
        out_specs=[VMEM, VMEM, VMEM],
        out_shape=[
            jax.ShapeDtypeStruct((LEVS, 2 * ROWS, LANES), BF16),
            jax.ShapeDtypeStruct((1, MM), jnp.int32),
            jax.ShapeDtypeStruct((ROWS, 1), jnp.int32),
        ],
        scratch_shapes=[
            pltpu.SMEM((BAND,), jnp.int32),
            pltpu.SMEM((NLAT // 2,), F32),
            pltpu.VMEM((8, LANES), jnp.int32),
            pltpu.VMEM((BAND, LEV, NLON), BF16),
            pltpu.VMEM((STEPS, QUARTER, 2 * BLOCK), BF16),
            pltpu.VMEM((2, 2 * ROWS, QUARTER), BF16),
            pltpu.VMEM((4 * ROWS, QUARTER), BF16),
            pltpu.VMEM((2 * ROWS, MM), F32),
            pltpu.SemaphoreType.DMA((4 + STEPS,)),
        ],
        compiler_params=PARAMS,
        name="fourier",
    )(
        lat_ref,
        in_hbm(kept_waves),
        in_hbm(weights),
        in_hbm(slot_wavenumber.reshape(8, LANES)),
        in_hbm(grid_fields.transpose(1, 0, 2)),
        in_hbm(jnp.asarray(forward_table)),
    )
    arrived = exchange(sent, ("x", "core"))
    gathered = pl.pallas_call(
        gather_kernel,
        in_specs=[VMEM],
        out_specs=VMEM,
        out_shape=jax.ShapeDtypeStruct((LATS, 4, DATA), BF16),
        scratch_shapes=[pltpu.VMEM((LATS, 4, DATA), F32)],
        compiler_params=PARAMS,
        name="gather",
    )(arrived)
    gathered = exchange(gathered, ("y", "z"))
    spectral, back = pl.pallas_call(
        legendre_kernel,
        in_specs=[SMEM, HBM, HBM, VMEM, VMEM],
        out_specs=[VMEM, VMEM],
        out_shape=[
            jax.ShapeDtypeStruct((2, 2, LEVELS, 2, HALF), F32),
            jax.ShapeDtypeStruct(chunk, BF16),
        ],
        scratch_shapes=[
            pltpu.SMEM((MM,), jnp.int32),
            pltpu.SMEM((LEVELS,), F32),
            pltpu.VMEM((2, NLAT // 2, LANES), F32),
            pltpu.SemaphoreType.DMA((2,)),
        ],
        compiler_params=PARAMS,
        name="legendre",
    )((lat * LEVS + lev).reshape(1), in_hbm(slot_wavenumber), in_hbm(diffusion), gathered, legendre)
    back = exchange(back, ("y", "z"))
    scattered = pl.pallas_call(
        scatter_kernel,
        in_specs=[VMEM],
        out_specs=VMEM,
        out_shape=jax.ShapeDtypeStruct((LEVS, 2 * ROWS + 16, LANES), BF16),
        scratch_shapes=[pltpu.VMEM(chunk, F32)],
        compiler_params=PARAMS,
        name="scatter",
    )(back)
    returned = exchange(scattered, ("x", "core"))
    grid_out, spectrum = pl.pallas_call(
        grid_kernel,
        in_specs=[SMEM, VMEM, VMEM, VMEM, HBM],
        out_specs=[VMEM, VMEM],
        out_shape=[
            jax.ShapeDtypeStruct((BAND, LEV, NLON), F32),
            jax.ShapeDtypeStruct((8, LANES), F32),
        ],
        scratch_shapes=[
            pltpu.VMEM((STEPS, 2 * BLOCK, QUARTER), BF16),
            pltpu.SemaphoreType.DMA((STEPS,)),
        ],
        compiler_params=PARAMS,
        name="grid",
    )(lat_ref, kept, order, returned, in_hbm(jnp.asarray(inverse_table)))
    return (
        grid_out.transpose(1, 0, 2),
        spectral,
        spectrum.reshape(MM),
    )


def solution(mesh):
    fine = Mesh(mesh.devices.reshape(4, 16, 4, 2), ("y", "z", "x", "core"))
    lat, lev = ("y", "z"), ("x", "core")
    both = lat + lev
    in_specs = (P(lev, lat, None), P(both, None, None, None), P(), P(lat), P(), P())
    out_specs = (P(lev, lat, None), P(both, None, None, None, None), P())
    return jax.shard_map(body, mesh=fine, in_specs=in_specs, out_specs=out_specs, check_vma=False)
```

```python
import math

import jax
import jax.numpy as jnp
import ml_dtypes
import numpy as np
from jax import lax
from jax.experimental import pallas as pl
from jax.experimental.pallas import tpu as pltpu
from jax.sharding import Mesh
from jax.sharding import PartitionSpec as P

NLAT = 1280
NLON = 2688
MM = 1024
HALF = MM // 2
LEVELS = 32
BAND = 20
LEV = 4
ROWS = BAND * LEV
LATS = 64
LEVS = 8
YS = 4
ZS = 16
NORTH = LATS // 2
QUARTER = NLON // 4
STEPS = 4
BLOCK = MM // STEPS
TILES = BAND // 4
LANES = 128
DATA = TILES * LANES

BF16 = jnp.bfloat16
F32 = jnp.float32
VMEM = pl.BlockSpec(memory_space=pltpu.VMEM)
HBM = pl.BlockSpec(memory_space=pltpu.HBM)
SMEM = pl.BlockSpec(memory_space=pltpu.SMEM)
PARAMS = pltpu.CompilerParams(vmem_limit_bytes=48 * 1024 * 1024)


def dft_tables():
    sample = np.arange(QUARTER, dtype=np.int32)[:, None]
    number = np.arange(MM, dtype=np.int32)[None, :]
    angles = (sample * number % NLON).astype(np.float32) * np.float32(2.0 * math.pi / NLON)
    norm_scale = np.float32(1.0 / math.sqrt(NLON))
    cosine = (np.cos(angles) * norm_scale).astype(ml_dtypes.bfloat16)
    sine = (-np.sin(angles) * norm_scale).astype(ml_dtypes.bfloat16)
    both = np.stack([cosine, sine], axis=1).reshape(QUARTER, 2, BLOCK, STEPS)
    forward = np.ascontiguousarray(both.transpose(3, 0, 1, 2)).reshape(STEPS, QUARTER, 2 * BLOCK)
    inverse = np.ascontiguousarray(forward.transpose(0, 2, 1))
    return forward, inverse


def iota(shape, dim):
    return lax.broadcasted_iota(jnp.int32, shape, dim)


def slot_choice(order, step):
    number = iota((BLOCK, MM), 0) * STEPS + step
    return jnp.where(order == number, 1.0, 0.0).astype(BF16)


def slot_order(slots):
    digits = jnp.concatenate([slots // 32, slots % 32], axis=0).astype(F32).astype(BF16)
    source = iota((LANES, MM), 0)
    to = iota((LANES, MM), 1)
    choice = jnp.where(source == to % 8 * 16 + to // LANES * 2 + to // LATS % 2, 1.0, 0.0).astype(BF16)
    moved = jnp.dot(digits, choice, preferred_element_type=F32)
    row = iota((16, MM), 0)
    mine = row % 8 == iota((16, MM), 1) % LATS // 8
    value = jnp.where(mine, moved * jnp.where(row < 8, 32.0, 1.0), 0.0)
    return jnp.sum(value, axis=0, keepdims=True).astype(jnp.int32)


def latitude_column(scalars, zero):
    band = iota((ROWS, 1), 0) // LEV
    column = jnp.full((ROWS, 1), zero)
    for j in range(BAND):
        column = jnp.where(band == j, scalars[j], column)
    return column


def class_mask(kept, step):
    return iota((ROWS, BLOCK), 1) * STEPS + step < kept


def row_choice(southern):
    to = iota((2 * ROWS, 2 * ROWS), 0)
    source = iota((2 * ROWS, 2 * ROWS), 1)
    band = to // (2 * LEV)
    band = jnp.where(southern, BAND - 1 - band, band)
    wanted = (to % 2) * ROWS + band * LEV + to // 2 % LEV
    return jnp.where(source == wanted, 1.0, 0.0).astype(BF16)


def fourier_kernel(
    lat_ref, kept_hbm, weights_hbm, slots_hbm, x_hbm, table_hbm, o_ref, order_ref, kept_ref, kept_s, weights_s, slots_v, x_v,
    table_v, even, odd, acc, sems
):
    small = [
        pltpu.make_async_copy(slots_hbm, slots_v, sems.at[0]),
        pltpu.make_async_copy(x_hbm, x_v, sems.at[1]),
        pltpu.make_async_copy(kept_hbm, kept_s, sems.at[2]),
        pltpu.make_async_copy(weights_hbm, weights_s, sems.at[3]),
    ]
    blocks = [pltpu.make_async_copy(table_hbm.at[i], table_v.at[i], sems.at[4 + i]) for i in range(STEPS)]
    for copy in small + blocks:
        copy.start()
    lat = lat_ref[0]
    small[0].wait()
    order = slot_order(slots_v[...])
    order_ref[...] = order
    small[2].wait()
    small[3].wait()
    kept = latitude_column([kept_s[j] for j in range(BAND)], jnp.int32(0))
    kept_ref[...] = kept
    latitudes = [lat * BAND + j for j in range(BAND)]
    weight = latitude_column([weights_s[jnp.minimum(i, NLAT - 1 - i)] for i in latitudes], F32(0.0))
    small[1].wait()

    def put(ref, place, value):
        high = value.astype(BF16)
        low = (value - high.astype(F32)).astype(BF16)
        for part, half in enumerate((high, low)):
            ref[pl.ds(place + part * ROWS, 16), :] = half

    for group in range(ROWS // 16):
        x = jnp.concatenate([x_v[4 * group + i].astype(F32) for i in range(4)], axis=0)
        x = [x[:, q * QUARTER : (q + 1) * QUARTER] for q in range(4)]
        sums = x[0] + x[2], x[1] + x[3]
        put(even.at[0], 16 * group, sums[0] + sums[1])
        put(even.at[1], 16 * group, sums[0] - sums[1])
        put(odd, 16 * group, x[0] - x[2])
        put(odd, 16 * group + 2 * ROWS, x[1] - x[3])
    for step in range(STEPS):
        blocks[step].wait()
        if step % 2 == 0:
            raw = jnp.dot(even[step // 2], table_v[step], preferred_element_type=F32)
            raw = raw[:ROWS] + raw[ROWS:]
            real, imaginary = raw[:, :BLOCK], raw[:, BLOCK:]
        else:
            raw = jnp.dot(odd[...], table_v[step], preferred_element_type=F32)
            first = raw[:ROWS] + raw[ROWS : 2 * ROWS]
            second = raw[2 * ROWS : 3 * ROWS] + raw[3 * ROWS :]
            if step == 3:
                second = -second
            real = first[:, :BLOCK] + second[:, BLOCK:]
            imaginary = first[:, BLOCK:] - second[:, :BLOCK]
        scale = jnp.where(class_mask(kept, step), weight, 0.0)
        fourier = jnp.concatenate([real * scale, imaginary * scale], axis=0).astype(BF16)
        part = jnp.dot(fourier, slot_choice(order, step), preferred_element_type=F32)
        if step == 0:
            acc[...] = part
        else:
            acc[...] += part
    choice = row_choice(lat >= NORTH)
    moved = jnp.dot(choice, acc[...].astype(BF16), preferred_element_type=F32).astype(BF16)
    for b in range(LEVS):
        o_ref[b] = moved[:, b * LANES : (b + 1) * LANES]


def gather_kernel(y_ref, o_ref, rows):
    for j in range(BAND):
        block = jnp.concatenate([y_ref[b, 8 * j : 8 * j + 8, :].astype(F32) for b in range(LEVS)], axis=0)
        turned = block.T
        rows[:, j % 4, (j // 4) * LANES : (j // 4 + 1) * LANES] = jnp.concatenate(
            [turned[:LATS], turned[LATS:]], axis=1
        )
    o_ref[...] = rows[...].astype(BF16)


def scatter_kernel(z_ref, o_ref, rows):
    rows[...] = z_ref[...].astype(F32)
    for y in range(YS):
        for j in range(TILES):
            block = []
            for part in range(4):
                row, tile = (part * TILES + j) % 4, y * TILES + (part * TILES + j) // 4
                block.append(rows[:, row, tile * LANES : (tile + 1) * LANES])
            block = jnp.concatenate(block, axis=0)
            turned = jnp.concatenate([block[:, :LATS], block[:, LATS:]], axis=0).T
            for b in range(LEVS):
                o_ref[y * LEVS + b, 16 + 8 * j : 24 + 8 * j, :] = turned[8 * b : 8 * b + 8].astype(BF16)
    power = jnp.sum(rows[:, :, YS * DATA :], axis=0)
    power = jnp.concatenate([power[:, :LANES], power[:, LANES:]], axis=0)
    high = power.astype(BF16)
    both = jnp.concatenate([high.astype(F32), power - high.astype(F32)], axis=0).astype(BF16)
    for peer in range(YS * LEVS):
        o_ref[peer, :16, :] = both


def swap_lanes(even, odd, width):
    high = iota(even.shape, 1) // width % 2 == 1
    return (
        jnp.where(high, pltpu.roll(odd, width, 1), even),
        jnp.where(high, odd, pltpu.roll(even, LANES - width, 1)),
    )


def legendre_kernel(
    device_ref, slots_hbm, diffusion_hbm, z_ref, table_hbm, spectral_ref, o_ref, slots_s, diffusion_s, table_v, comb, sems
):
    copies = [
        pltpu.make_async_copy(slots_hbm, slots_s, sems.at[0]),
        pltpu.make_async_copy(diffusion_hbm, diffusion_s, sems.at[1]),
    ]
    tables = [
        [pltpu.make_async_copy(table_hbm.at[t, q], table_v.at[t, q], sems.at[2 + 2 * t + q]) for t in range(2)]
        for q in range(2)
    ]
    for copy in copies + tables[0] + tables[1]:
        copy.start()
    for group in range(NORTH * TILES // 4):
        north, south = [], []
        for u in range(4 * group, 4 * group + 4):
            a, tile = divmod(u, TILES)
            lanes = slice(tile * LANES, (tile + 1) * LANES)
            north.append(z_ref[a, :, lanes].astype(F32))
            south.append(z_ref[LATS - 1 - a, :, lanes].astype(F32))
        north = jnp.concatenate(north, axis=0)
        south = jnp.concatenate(south, axis=0)
        comb[0, 16 * group : 16 * group + 16, :] = north + south
        comb[1, 16 * group : 16 * group + 16, :] = north - south
    for copy in copies:
        copy.wait()
    column = iota((2 * LEVELS, HALF), 1)
    level = iota((2 * LEVELS, 1), 0) // 2
    diffusion = jnp.zeros((2 * LEVELS, 1), F32)
    for i in range(LEVELS):
        diffusion = jnp.where(level == i, diffusion_s[i], diffusion)
    power = [jnp.zeros((1, HALF), F32), jnp.zeros((1, HALF), F32)]
    halves = []
    for q in range(2):
        left = comb[q].T.astype(BF16)
        parts = []
        for t in range(2):
            tables[q][t].wait()
            wave = slots_s[device_ref[0] * 2 + t]
            raw = jnp.dot(left[64 * t : 64 * t + 64], table_v[t, q], preferred_element_type=F32)
            degree = wave + 2 * column + q
            spectral = jnp.where(degree < MM, raw, 0.0)
            for level in range(LEVELS):
                spectral_ref[t, q, level] = spectral[2 * level : 2 * level + 2]
            degree = degree.astype(F32)
            ratio = degree * (degree + 1.0) / (MM * (MM + 1.0))
            damped = (spectral / (1.0 + diffusion * ratio * ratio)).astype(BF16)
            parts.append(
                lax.dot_general(
                    table_v[t, q], damped, (((1,), (1,)), ((), ())), preferred_element_type=F32
                )
            )
            energy = jnp.sum(spectral * spectral, axis=0, keepdims=True)
            first = wave + q
            moved = pltpu.roll(jnp.broadcast_to(energy, (8, HALF)), first // 2 % HALF, 1)[:1]
            for odd in range(2):
                power[odd] += jnp.where(first % 2 == odd, moved, 0.0)
        halves.append(jnp.concatenate(parts, axis=1))
    source = iota((LANES, 2 * LANES), 0)
    to = iota((LANES, 2 * LANES), 1)
    natural = jnp.zeros((8, 2 * LANES), F32)
    for odd in range(2):
        quarters = [power[odd][:, i * LANES : (i + 1) * LANES] for i in range(4)]
        quarters = jnp.concatenate(quarters + quarters, axis=0).astype(BF16)
        choice = jnp.where(to == 2 * source + odd, 1.0, 0.0).astype(BF16)
        natural += jnp.dot(quarters, choice, preferred_element_type=F32)
    natural = natural[:4].astype(BF16)
    for z in range(ZS):
        o_ref[z, :, YS * DATA :] = natural
    for half, side in enumerate((halves[0] + halves[1], halves[0] - halves[1])):
        for u in range(NORTH * TILES):
            a, tile = divmod(u, TILES)
            y, z = divmod(LATS - 1 - a if half else a, ZS)
            place = (y * TILES + tile) * LANES
            o_ref[z, :, place : place + LANES] = side[4 * u : 4 * u + 4].astype(BF16)


def grid_kernel(lat_ref, kept_ref, order_ref, y_ref, table_ref, o_ref, spectrum_ref):
    kept = kept_ref[...]
    choice = row_choice(lat_ref[0] >= NORTH)
    back = []
    for b in range(LEVS):
        parts = [y_ref[y * LEVS + b, 16:, :].astype(F32) for y in range(YS)]
        parts[0], parts[1] = swap_lanes(parts[0], parts[1], ZS)
        parts[2], parts[3] = swap_lanes(parts[2], parts[3], ZS)
        parts[0], parts[2] = swap_lanes(parts[0], parts[2], 2 * ZS)
        parts[1], parts[3] = swap_lanes(parts[1], parts[3], 2 * ZS)
        back.append(jnp.concatenate(parts, axis=0).astype(BF16))
    back = jnp.concatenate(back, axis=1)
    rows = lax.dot_general(choice, back, (((0,), (0,)), ((), ())), preferred_element_type=F32).astype(BF16)
    parts = []
    for step in range(STEPS):
        numbered = lax.dot_general(
            rows, slot_choice(order_ref[...], step), (((1,), (1,)), ((), ())), preferred_element_type=F32
        )
        mask = class_mask(kept, step)
        real = jnp.where(mask, numbered[:ROWS], 0.0)
        imaginary = jnp.where(mask, numbered[ROWS:], 0.0)
        left = jnp.concatenate([real, imaginary], axis=1)
        if step == 1:
            left = jnp.concatenate([left, jnp.concatenate([-imaginary, real], axis=1)], axis=0)
        if step == 3:
            left = jnp.concatenate([left, jnp.concatenate([imaginary, -real], axis=1)], axis=0)
        parts.append(jnp.dot(left.astype(BF16), table_ref[step], preferred_element_type=F32))
    odd = parts[1] + parts[3]
    plus, minus = parts[0] + parts[2], parts[0] - parts[2]
    quarters = [plus + odd[:ROWS], minus + odd[ROWS:], plus - odd[:ROWS], minus - odd[ROWS:]]
    points = jnp.concatenate(quarters, axis=1) * math.sqrt(NLON / MM)
    for j in range(BAND):
        o_ref[j] = points[LEV * j : LEV * (j + 1), :]
    power = jnp.zeros((16, LANES), F32)
    for peer in range(YS * LEVS):
        power += y_ref[peer, :16, :].astype(F32)
    power = power[:8] + power[8:]
    power = jnp.concatenate([power[i // 2 + 4 * (i % 2)][None] for i in range(8)], axis=0)
    degree = (iota((8, LANES), 0) * LANES + iota((8, LANES), 1)).astype(F32)
    spectrum_ref[...] = power / (2.0 * LEVELS * (degree + 1.0))


def in_hbm(x):
    return pltpu.with_memory_space_constraint(x, pltpu.HBM)


def exchange(x, axes):
    return lax.all_to_all(x, axes, split_axis=0, concat_axis=0, tiled=True)


def body(grid_fields, legendre, weights, kept_waves, slot_wavenumber, diffusion):
    forward_table, inverse_table = dft_tables()
    lat = lax.axis_index(("y", "z")).astype(jnp.int32)
    lev = lax.axis_index(("x", "core")).astype(jnp.int32)
    lat_ref = lat.reshape(1)
    chunk = (ZS, 4, YS * DATA + 2 * LANES)

    sent, order, kept = pl.pallas_call(
        fourier_kernel,
        in_specs=[SMEM, HBM, HBM, HBM, HBM, HBM],
        out_specs=[VMEM, VMEM, VMEM],
        out_shape=[
            jax.ShapeDtypeStruct((LEVS, 2 * ROWS, LANES), BF16),
            jax.ShapeDtypeStruct((1, MM), jnp.int32),
            jax.ShapeDtypeStruct((ROWS, 1), jnp.int32),
        ],
        scratch_shapes=[
            pltpu.SMEM((BAND,), jnp.int32),
            pltpu.SMEM((NLAT // 2,), F32),
            pltpu.VMEM((8, LANES), jnp.int32),
            pltpu.VMEM((BAND, LEV, NLON), BF16),
            pltpu.VMEM((STEPS, QUARTER, 2 * BLOCK), BF16),
            pltpu.VMEM((2, 2 * ROWS, QUARTER), BF16),
            pltpu.VMEM((4 * ROWS, QUARTER), BF16),
            pltpu.VMEM((2 * ROWS, MM), F32),
            pltpu.SemaphoreType.DMA((4 + STEPS,)),
        ],
        compiler_params=PARAMS,
        name="fourier",
    )(
        lat_ref,
        in_hbm(kept_waves),
        in_hbm(weights),
        in_hbm(slot_wavenumber.reshape(8, LANES)),
        in_hbm(grid_fields.transpose(1, 0, 2)),
        in_hbm(jnp.asarray(forward_table)),
    )
    arrived = exchange(sent, ("x", "core"))
    gathered = pl.pallas_call(
        gather_kernel,
        in_specs=[VMEM],
        out_specs=VMEM,
        out_shape=jax.ShapeDtypeStruct((LATS, 4, DATA), BF16),
        scratch_shapes=[pltpu.VMEM((LATS, 4, DATA), F32)],
        compiler_params=PARAMS,
        name="gather",
    )(arrived)
    gathered = exchange(gathered, ("y", "z"))
    spectral, back = pl.pallas_call(
        legendre_kernel,
        in_specs=[SMEM, HBM, HBM, VMEM, HBM],
        out_specs=[VMEM, VMEM],
        out_shape=[
            jax.ShapeDtypeStruct((2, 2, LEVELS, 2, HALF), F32),
            jax.ShapeDtypeStruct(chunk, BF16),
        ],
        scratch_shapes=[
            pltpu.SMEM((MM,), jnp.int32),
            pltpu.SMEM((LEVELS,), F32),
            pltpu.VMEM((2, 2, NLAT // 2, HALF), BF16),
            pltpu.VMEM((2, NLAT // 2, LANES), F32),
            pltpu.SemaphoreType.DMA((6,)),
        ],
        compiler_params=PARAMS,
        name="legendre",
    )((lat * LEVS + lev).reshape(1), in_hbm(slot_wavenumber), in_hbm(diffusion), gathered, in_hbm(legendre))
    back = exchange(back, ("z",))
    scattered = pl.pallas_call(
        scatter_kernel,
        in_specs=[VMEM],
        out_specs=VMEM,
        out_shape=jax.ShapeDtypeStruct((YS * LEVS, 16 + 2 * ROWS // YS, LANES), BF16),
        scratch_shapes=[pltpu.VMEM(chunk, F32)],
        compiler_params=PARAMS,
        name="scatter",
    )(back)
    returned = exchange(scattered, ("y", "x", "core"))
    grid_out, spectrum = pl.pallas_call(
        grid_kernel,
        in_specs=[SMEM, VMEM, VMEM, VMEM, VMEM],
        out_specs=[VMEM, VMEM],
        out_shape=[
            jax.ShapeDtypeStruct((BAND, LEV, NLON), F32),
            jax.ShapeDtypeStruct((8, LANES), F32),
        ],
        compiler_params=PARAMS,
        name="grid",
    )(lat_ref, kept, order, returned, jnp.asarray(inverse_table))
    return (
        grid_out.transpose(1, 0, 2),
        spectral,
        spectrum.reshape(MM),
    )


def solution(mesh):
    fine = Mesh(mesh.devices.reshape(4, 16, 4, 2), ("y", "z", "x", "core"))
    lat, lev = ("y", "z"), ("x", "core")
    both = lat + lev
    in_specs = (P(lev, lat, None), P(both, None, None, None), P(), P(lat), P(), P())
    out_specs = (P(lev, lat, None), P(both, None, None, None, None), P())
    return jax.shard_map(body, mesh=fine, in_specs=in_specs, out_specs=out_specs, check_vma=False)
```

```python
import math

import jax
import jax.numpy as jnp
import ml_dtypes
import numpy as np
from jax import lax
from jax.experimental import pallas as pl
from jax.experimental.pallas import tpu as pltpu
from jax.sharding import Mesh
from jax.sharding import PartitionSpec as P

NLAT = 1280
NLON = 2688
MM = 1024
HALF = MM // 2
LEVELS = 32
BAND = 20
LEV = 4
ROWS = BAND * LEV
LATS = 64
LEVS = 8
YS = 4
ZS = 16
NORTH = LATS // 2
QUARTER = NLON // 4
STEPS = 4
BLOCK = MM // STEPS
TILES = BAND // 4
LANES = 128
DATA = TILES * LANES

BF16 = jnp.bfloat16
F32 = jnp.float32
VMEM = pl.BlockSpec(memory_space=pltpu.VMEM)
HBM = pl.BlockSpec(memory_space=pltpu.HBM)
SMEM = pl.BlockSpec(memory_space=pltpu.SMEM)
PARAMS = pltpu.CompilerParams(vmem_limit_bytes=20 * 1024 * 1024)


def dft_tables():
    sample = np.arange(QUARTER, dtype=np.int32)[:, None]
    number = np.arange(MM, dtype=np.int32)[None, :]
    angles = (sample * number % NLON).astype(np.float32) * np.float32(2.0 * math.pi / NLON)
    norm_scale = np.float32(1.0 / math.sqrt(NLON))
    cosine = (np.cos(angles) * norm_scale).astype(ml_dtypes.bfloat16)
    sine = (-np.sin(angles) * norm_scale).astype(ml_dtypes.bfloat16)
    both = np.stack([cosine, sine], axis=1).reshape(QUARTER, 2, BLOCK, STEPS)
    forward = np.ascontiguousarray(both.transpose(3, 0, 1, 2)).reshape(STEPS, QUARTER, 2 * BLOCK)
    inverse = np.ascontiguousarray(forward.transpose(0, 2, 1))
    return forward, inverse


def iota(shape, dim):
    return lax.broadcasted_iota(jnp.int32, shape, dim)


def slot_choice(order, step):
    number = iota((BLOCK, MM), 0) * STEPS + step
    return jnp.where(order == number, 1.0, 0.0).astype(BF16)


def slot_order(slots):
    digits = jnp.concatenate([slots // 32, slots % 32], axis=0).astype(F32).astype(BF16)
    source = iota((LANES, MM), 0)
    to = iota((LANES, MM), 1)
    choice = jnp.where(source == to % 8 * 16 + to // LANES * 2 + to // LATS % 2, 1.0, 0.0).astype(BF16)
    moved = jnp.dot(digits, choice, preferred_element_type=F32)
    row = iota((16, MM), 0)
    mine = row % 8 == iota((16, MM), 1) % LATS // 8
    value = jnp.where(mine, moved * jnp.where(row < 8, 32.0, 1.0), 0.0)
    return jnp.sum(value, axis=0, keepdims=True).astype(jnp.int32)


def latitude_column(scalars, zero):
    band = iota((ROWS, 1), 0) // LEV
    column = jnp.full((ROWS, 1), zero)
    for j in range(BAND):
        column = jnp.where(band == j, scalars[j], column)
    return column


def class_mask(kept, step):
    return iota((ROWS, BLOCK), 1) * STEPS + step < kept


def row_choice(southern):
    to = iota((2 * ROWS, 2 * ROWS), 0)
    source = iota((2 * ROWS, 2 * ROWS), 1)
    band = to // (2 * LEV)
    band = jnp.where(southern, BAND - 1 - band, band)
    wanted = (to % 2) * ROWS + band * LEV + to // 2 % LEV
    return jnp.where(source == wanted, 1.0, 0.0).astype(BF16)


def fourier_kernel(
    device_ref, kept_hbm, weights_hbm, slots_hbm, x_hbm, table_hbm, later_hbm, o_ref, order_ref, kept_ref, later_ref, kept_s, weights_s, slots_v, x_v,
    table_v, even, odd, acc, sems
):
    small = [
        pltpu.make_async_copy(slots_hbm, slots_v, sems.at[0]),
        pltpu.make_async_copy(x_hbm, x_v, sems.at[1]),
        pltpu.make_async_copy(kept_hbm, kept_s, sems.at[2]),
        pltpu.make_async_copy(weights_hbm, weights_s, sems.at[3]),
    ]
    blocks = [pltpu.make_async_copy(table_hbm.at[i], table_v.at[i], sems.at[4 + i]) for i in range(STEPS)]
    later = pltpu.make_async_copy(later_hbm, later_ref, sems.at[4 + STEPS])
    for copy in small + blocks + [later]:
        copy.start()
    lat = device_ref[0] // LEVS
    small[0].wait()
    order = slot_order(slots_v[...])
    order_ref[...] = order
    small[2].wait()
    small[3].wait()
    kept = latitude_column([kept_s[j] for j in range(BAND)], jnp.int32(0))
    kept_ref[...] = kept
    latitudes = [lat * BAND + j for j in range(BAND)]
    weight = latitude_column([weights_s[jnp.minimum(i, NLAT - 1 - i)] for i in latitudes], F32(0.0))
    small[1].wait()

    def put(ref, place, value):
        high = value.astype(BF16)
        low = (value - high.astype(F32)).astype(BF16)
        for part, half in enumerate((high, low)):
            ref[pl.ds(place + part * ROWS, 16), :] = half

    for group in range(ROWS // 16):
        x = jnp.concatenate([x_v[4 * group + i].astype(F32) for i in range(4)], axis=0)
        x = [x[:, q * QUARTER : (q + 1) * QUARTER] for q in range(4)]
        sums = x[0] + x[2], x[1] + x[3]
        put(even.at[0], 16 * group, sums[0] + sums[1])
        put(even.at[1], 16 * group, sums[0] - sums[1])
        put(odd, 16 * group, x[0] - x[2])
        put(odd, 16 * group + 2 * ROWS, x[1] - x[3])
    for step in range(STEPS):
        blocks[step].wait()
        if step % 2 == 0:
            raw = jnp.dot(even[step // 2], table_v[step], preferred_element_type=F32)
            raw = raw[:ROWS] + raw[ROWS:]
            real, imaginary = raw[:, :BLOCK], raw[:, BLOCK:]
        else:
            raw = jnp.dot(odd[...], table_v[step], preferred_element_type=F32)
            first = raw[:ROWS] + raw[ROWS : 2 * ROWS]
            second = raw[2 * ROWS : 3 * ROWS] + raw[3 * ROWS :]
            if step == 3:
                second = -second
            real = first[:, :BLOCK] + second[:, BLOCK:]
            imaginary = first[:, BLOCK:] - second[:, :BLOCK]
        scale = jnp.where(class_mask(kept, step), weight, 0.0)
        fourier = jnp.concatenate([real * scale, imaginary * scale], axis=0).astype(BF16)
        part = jnp.dot(fourier, slot_choice(order, step), preferred_element_type=F32)
        if step == 0:
            acc[...] = part
        else:
            acc[...] += part
    choice = row_choice(lat >= NORTH)
    moved = jnp.dot(choice, acc[...].astype(BF16), preferred_element_type=F32).astype(BF16)
    for b in range(LEVS):
        o_ref[b] = moved[:, b * LANES : (b + 1) * LANES]
    later.wait()


def gather_kernel(y_ref, o_ref, rows):
    for j in range(BAND):
        block = jnp.concatenate([y_ref[b, 8 * j : 8 * j + 8, :].astype(F32) for b in range(LEVS)], axis=0)
        turned = block.T
        rows[:, j % 4, (j // 4) * LANES : (j // 4 + 1) * LANES] = jnp.concatenate(
            [turned[:LATS], turned[LATS:]], axis=1
        )
    o_ref[...] = rows[...].astype(BF16)


def scatter_kernel(z_ref, o_ref, rows):
    rows[...] = z_ref[...].astype(F32)
    for y in range(YS):
        for j in range(TILES):
            block = []
            for part in range(4):
                row, tile = (part * TILES + j) % 4, y * TILES + (part * TILES + j) // 4
                block.append(rows[:, row, tile * LANES : (tile + 1) * LANES])
            block = jnp.concatenate(block, axis=0)
            turned = jnp.concatenate([block[:, :LATS], block[:, LATS:]], axis=0).T
            for b in range(LEVS):
                o_ref[y * LEVS + b, 16 + 8 * j : 24 + 8 * j, :] = turned[8 * b : 8 * b + 8].astype(BF16)
    power = jnp.sum(rows[:, :, YS * DATA :], axis=0)
    power = jnp.concatenate([power[:, :LANES], power[:, LANES:]], axis=0)
    high = power.astype(BF16)
    both = jnp.concatenate([high.astype(F32), power - high.astype(F32)], axis=0).astype(BF16)
    for peer in range(YS * LEVS):
        o_ref[peer, :16, :] = both


def swap_lanes(even, odd, width):
    high = iota(even.shape, 1) // width % 2 == 1
    return (
        jnp.where(high, pltpu.roll(odd, width, 1), even),
        jnp.where(high, odd, pltpu.roll(even, LANES - width, 1)),
    )


def legendre_kernel(
    device_ref, slots_hbm, diffusion_hbm, z_ref, table_ref, later_hbm, spectral_ref, o_ref, later_ref, slots_s, diffusion_s,
    comb, sems
):
    copies = [
        pltpu.make_async_copy(slots_hbm, slots_s, sems.at[0]),
        pltpu.make_async_copy(diffusion_hbm, diffusion_s, sems.at[1]),
    ]
    later = pltpu.make_async_copy(later_hbm, later_ref, sems.at[2])
    for copy in copies + [later]:
        copy.start()
    for group in range(NORTH * TILES // 4):
        north, south = [], []
        for u in range(4 * group, 4 * group + 4):
            a, tile = divmod(u, TILES)
            lanes = slice(tile * LANES, (tile + 1) * LANES)
            north.append(z_ref[a, :, lanes].astype(F32))
            south.append(z_ref[LATS - 1 - a, :, lanes].astype(F32))
        north = jnp.concatenate(north, axis=0)
        south = jnp.concatenate(south, axis=0)
        comb[0, 16 * group : 16 * group + 16, :] = north + south
        comb[1, 16 * group : 16 * group + 16, :] = north - south
    for copy in copies:
        copy.wait()
    column = iota((2 * LEVELS, HALF), 1)
    level = iota((2 * LEVELS, 1), 0) // 2
    diffusion = jnp.zeros((2 * LEVELS, 1), F32)
    for i in range(LEVELS):
        diffusion = jnp.where(level == i, diffusion_s[i], diffusion)
    power = [jnp.zeros((1, HALF), F32), jnp.zeros((1, HALF), F32)]
    halves = []
    for q in range(2):
        left = comb[q].T.astype(BF16)
        parts = []
        for t in range(2):
            wave = slots_s[device_ref[0] * 2 + t]
            raw = jnp.dot(left[64 * t : 64 * t + 64], table_ref[t, q], preferred_element_type=F32)
            degree = wave + 2 * column + q
            spectral = jnp.where(degree < MM, raw, 0.0)
            for level in range(LEVELS):
                spectral_ref[t, q, level] = spectral[2 * level : 2 * level + 2]
            degree = degree.astype(F32)
            ratio = degree * (degree + 1.0) / (MM * (MM + 1.0))
            damped = (spectral / (1.0 + diffusion * ratio * ratio)).astype(BF16)
            parts.append(
                lax.dot_general(
                    table_ref[t, q], damped, (((1,), (1,)), ((), ())), preferred_element_type=F32
                )
            )
            energy = jnp.sum(spectral * spectral, axis=0, keepdims=True)
            first = wave + q
            moved = pltpu.roll(jnp.broadcast_to(energy, (8, HALF)), first // 2 % HALF, 1)[:1]
            for odd in range(2):
                power[odd] += jnp.where(first % 2 == odd, moved, 0.0)
        halves.append(jnp.concatenate(parts, axis=1))
    source = iota((LANES, 2 * LANES), 0)
    to = iota((LANES, 2 * LANES), 1)
    natural = jnp.zeros((8, 2 * LANES), F32)
    for odd in range(2):
        quarters = [power[odd][:, i * LANES : (i + 1) * LANES] for i in range(4)]
        quarters = jnp.concatenate(quarters + quarters, axis=0).astype(BF16)
        choice = jnp.where(to == 2 * source + odd, 1.0, 0.0).astype(BF16)
        natural += jnp.dot(quarters, choice, preferred_element_type=F32)
    natural = natural[:4].astype(BF16)
    for z in range(ZS):
        o_ref[z, :, YS * DATA :] = natural
    for half, side in enumerate((halves[0] + halves[1], halves[0] - halves[1])):
        for u in range(NORTH * TILES):
            a, tile = divmod(u, TILES)
            y, z = divmod(LATS - 1 - a if half else a, ZS)
            place = (y * TILES + tile) * LANES
            o_ref[z, :, place : place + LANES] = side[4 * u : 4 * u + 4].astype(BF16)
    later.wait()


def grid_kernel(device_ref, kept_ref, order_ref, y_ref, table_ref, o_ref, spectrum_ref):
    kept = kept_ref[...]
    choice = row_choice(device_ref[0] >= NORTH * LEVS)
    back = []
    for b in range(LEVS):
        parts = [y_ref[y * LEVS + b, 16:, :].astype(F32) for y in range(YS)]
        parts[0], parts[1] = swap_lanes(parts[0], parts[1], ZS)
        parts[2], parts[3] = swap_lanes(parts[2], parts[3], ZS)
        parts[0], parts[2] = swap_lanes(parts[0], parts[2], 2 * ZS)
        parts[1], parts[3] = swap_lanes(parts[1], parts[3], 2 * ZS)
        back.append(jnp.concatenate(parts, axis=0).astype(BF16))
    back = jnp.concatenate(back, axis=1)
    rows = lax.dot_general(choice, back, (((0,), (0,)), ((), ())), preferred_element_type=F32).astype(BF16)
    parts = []
    for step in range(STEPS):
        numbered = lax.dot_general(
            rows, slot_choice(order_ref[...], step), (((1,), (1,)), ((), ())), preferred_element_type=F32
        )
        mask = class_mask(kept, step)
        real = jnp.where(mask, numbered[:ROWS], 0.0)
        imaginary = jnp.where(mask, numbered[ROWS:], 0.0)
        left = jnp.concatenate([real, imaginary], axis=1)
        if step == 1:
            left = jnp.concatenate([left, jnp.concatenate([-imaginary, real], axis=1)], axis=0)
        if step == 3:
            left = jnp.concatenate([left, jnp.concatenate([imaginary, -real], axis=1)], axis=0)
        parts.append(jnp.dot(left.astype(BF16), table_ref[step], preferred_element_type=F32))
    odd = parts[1] + parts[3]
    plus, minus = parts[0] + parts[2], parts[0] - parts[2]
    quarters = [plus + odd[:ROWS], minus + odd[ROWS:], plus - odd[:ROWS], minus - odd[ROWS:]]
    points = jnp.concatenate(quarters, axis=1) * math.sqrt(NLON / MM)
    for j in range(BAND):
        o_ref[j] = points[LEV * j : LEV * (j + 1), :]
    power = jnp.zeros((16, LANES), F32)
    for peer in range(YS * LEVS):
        power += y_ref[peer, :16, :].astype(F32)
    power = power[:8] + power[8:]
    power = jnp.concatenate([power[i // 2 + 4 * (i % 2)][None] for i in range(8)], axis=0)
    degree = (iota((8, LANES), 0) * LANES + iota((8, LANES), 1)).astype(F32)
    spectrum_ref[...] = power / (2.0 * LEVELS * (degree + 1.0))


def in_hbm(x):
    return pltpu.with_memory_space_constraint(x, pltpu.HBM)


def in_vmem(x):
    return pltpu.with_memory_space_constraint(x, pltpu.VMEM)


def exchange(x, axes):
    return lax.all_to_all(x, axes, split_axis=0, concat_axis=0, tiled=True)


def body(grid_fields, legendre, weights, kept_waves, slot_wavenumber, diffusion):
    forward_table, inverse_table = dft_tables()
    device = lax.axis_index(("y", "z", "x", "core")).astype(jnp.int32).reshape(1)
    chunk = (ZS, 4, YS * DATA + 2 * LANES)

    sent, order, kept, legendre = pl.pallas_call(
        fourier_kernel,
        in_specs=[SMEM, HBM, HBM, HBM, HBM, HBM, HBM],
        out_specs=[VMEM, VMEM, VMEM, VMEM],
        out_shape=[
            jax.ShapeDtypeStruct((LEVS, 2 * ROWS, LANES), BF16),
            jax.ShapeDtypeStruct((1, MM), jnp.int32),
            jax.ShapeDtypeStruct((ROWS, 1), jnp.int32),
            pltpu.VMEM(legendre.shape, BF16),
        ],
        scratch_shapes=[
            pltpu.SMEM((BAND,), jnp.int32),
            pltpu.SMEM((NLAT // 2,), F32),
            pltpu.VMEM((8, LANES), jnp.int32),
            pltpu.VMEM((BAND, LEV, NLON), BF16),
            pltpu.VMEM((STEPS, QUARTER, 2 * BLOCK), BF16),
            pltpu.VMEM((2, 2 * ROWS, QUARTER), BF16),
            pltpu.VMEM((4 * ROWS, QUARTER), BF16),
            pltpu.VMEM((2 * ROWS, MM), F32),
            pltpu.SemaphoreType.DMA((5 + STEPS,)),
        ],
        compiler_params=PARAMS,
        name="fourier",
    )(
        device,
        in_hbm(kept_waves),
        in_hbm(weights),
        in_hbm(slot_wavenumber.reshape(8, LANES)),
        in_hbm(grid_fields.transpose(1, 0, 2)),
        in_hbm(jnp.asarray(forward_table)),
        in_hbm(legendre),
    )
    arrived = exchange(sent, ("x", "core"))
    gathered = pl.pallas_call(
        gather_kernel,
        in_specs=[VMEM],
        out_specs=VMEM,
        out_shape=jax.ShapeDtypeStruct((LATS, 4, DATA), BF16),
        scratch_shapes=[pltpu.VMEM((LATS, 4, DATA), F32)],
        compiler_params=PARAMS,
        name="gather",
    )(arrived)
    gathered = exchange(gathered, ("y", "z"))
    spectral, back, table = pl.pallas_call(
        legendre_kernel,
        in_specs=[SMEM, HBM, HBM, VMEM, VMEM, HBM],
        out_specs=[VMEM, VMEM, VMEM],
        out_shape=[
            jax.ShapeDtypeStruct((2, 2, LEVELS, 2, HALF), F32),
            jax.ShapeDtypeStruct(chunk, BF16),
            pltpu.VMEM((STEPS, 2 * BLOCK, QUARTER), BF16),
        ],
        scratch_shapes=[
            pltpu.SMEM((MM,), jnp.int32),
            pltpu.SMEM((LEVELS,), F32),
            pltpu.VMEM((2, NLAT // 2, LANES), F32),
            pltpu.SemaphoreType.DMA((3,)),
        ],
        compiler_params=PARAMS,
        name="legendre",
    )(device, in_hbm(slot_wavenumber), in_hbm(diffusion), gathered, in_vmem(legendre), in_hbm(jnp.asarray(inverse_table)))
    back = exchange(back, ("z",))
    scattered = pl.pallas_call(
        scatter_kernel,
        in_specs=[VMEM],
        out_specs=VMEM,
        out_shape=jax.ShapeDtypeStruct((YS * LEVS, 16 + 2 * ROWS // YS, LANES), BF16),
        scratch_shapes=[pltpu.VMEM(chunk, F32)],
        compiler_params=PARAMS,
        name="scatter",
    )(back)
    returned = exchange(scattered, ("y", "x", "core"))
    grid_out, spectrum = pl.pallas_call(
        grid_kernel,
        in_specs=[SMEM, VMEM, VMEM, VMEM, VMEM],
        out_specs=[VMEM, VMEM],
        out_shape=[
            jax.ShapeDtypeStruct((BAND, LEV, NLON), F32),
            jax.ShapeDtypeStruct((8, LANES), F32),
        ],
        compiler_params=PARAMS,
        name="grid",
    )(device, kept, order, returned, in_vmem(table))
    return (
        grid_out.transpose(1, 0, 2),
        spectral,
        spectrum.reshape(MM),
    )


def solution(mesh):
    fine = Mesh(mesh.devices.reshape(4, 16, 4, 2), ("y", "z", "x", "core"))
    lat, lev = ("y", "z"), ("x", "core")
    both = lat + lev
    in_specs = (P(lev, lat, None), P(both, None, None, None), P(), P(lat), P(), P())
    out_specs = (P(lev, lat, None), P(both, None, None, None, None), P())
    return jax.shard_map(body, mesh=fine, in_specs=in_specs, out_specs=out_specs, check_vma=False)
```

```python
import math

import jax
import jax.numpy as jnp
import ml_dtypes
import numpy as np
from jax import lax
from jax.experimental import pallas as pl
from jax.experimental.pallas import tpu as pltpu
from jax.sharding import Mesh
from jax.sharding import PartitionSpec as P

NLAT = 1280
NLON = 2688
MM = 1024
HALF = MM // 2
LEVELS = 32
BAND = 20
LEV = 4
ROWS = BAND * LEV
LATS = 64
LEVS = 8
YS = 4
ZS = 16
CHUNK = 2 * ROWS // YS
NORTH = LATS // 2
QUARTER = NLON // 4
STEPS = 4
BLOCK = MM // STEPS
TILES = BAND // 4
LANES = 128
DATA = TILES * LANES

BF16 = jnp.bfloat16
F32 = jnp.float32
VMEM = pl.BlockSpec(memory_space=pltpu.VMEM)
HBM = pl.BlockSpec(memory_space=pltpu.HBM)
SMEM = pl.BlockSpec(memory_space=pltpu.SMEM)
PARAMS = pltpu.CompilerParams(vmem_limit_bytes=20 * 1024 * 1024)


def dft_tables():
    sample = np.arange(QUARTER, dtype=np.int32)[:, None]
    number = np.arange(MM, dtype=np.int32)[None, :]
    angles = (sample * number % NLON).astype(np.float32) * np.float32(2.0 * math.pi / NLON)
    norm_scale = np.float32(1.0 / math.sqrt(NLON))
    cosine = (np.cos(angles) * norm_scale).astype(ml_dtypes.bfloat16)
    sine = (-np.sin(angles) * norm_scale).astype(ml_dtypes.bfloat16)
    both = np.stack([cosine, sine], axis=1).reshape(QUARTER, 2, BLOCK, STEPS)
    forward = np.ascontiguousarray(both.transpose(3, 0, 1, 2)).reshape(STEPS, QUARTER, 2 * BLOCK)
    inverse = np.ascontiguousarray(forward.transpose(0, 2, 1))
    return forward, inverse


def iota(shape, dim):
    return lax.broadcasted_iota(jnp.int32, shape, dim)


def slot_choice(order, step):
    number = iota((BLOCK, MM), 0) * STEPS + step
    return jnp.where(order == number, 1.0, 0.0).astype(BF16)


def slot_order(slots):
    digits = jnp.concatenate([slots // 32, slots % 32], axis=0).astype(F32).astype(BF16)
    source = iota((LANES, MM), 0)
    to = iota((LANES, MM), 1)
    choice = jnp.where(source == to % 8 * 16 + to // LANES * 2 + to // LATS % 2, 1.0, 0.0).astype(BF16)
    moved = jnp.dot(digits, choice, preferred_element_type=F32)
    row = iota((16, MM), 0)
    mine = row % 8 == iota((16, MM), 1) % LATS // 8
    value = jnp.where(mine, moved * jnp.where(row < 8, 32.0, 1.0), 0.0)
    return jnp.sum(value, axis=0, keepdims=True).astype(jnp.int32)


def latitude_column(scalars, zero):
    band = iota((ROWS, 1), 0) // LEV
    column = jnp.full((ROWS, 1), zero)
    for j in range(BAND):
        column = jnp.where(band == j, scalars[j], column)
    return column


def class_mask(kept, step):
    return iota((ROWS, BLOCK), 1) * STEPS + step < kept


def row_choice(southern):
    to = iota((2 * ROWS, 2 * ROWS), 0)
    source = iota((2 * ROWS, 2 * ROWS), 1)
    band = to // (2 * LEV)
    band = jnp.where(southern, BAND - 1 - band, band)
    wanted = (to % 2) * ROWS + band * LEV + to // 2 % LEV
    return jnp.where(source == wanted, 1.0, 0.0).astype(BF16)


def swap_lanes(even, odd, width):
    high = iota(even.shape, 1) // width % 2 == 1
    return (
        jnp.where(high, pltpu.roll(odd, width, 1), even),
        jnp.where(high, odd, pltpu.roll(even, LANES - width, 1)),
    )


def swap_parts(parts):
    parts = list(parts)
    parts[0], parts[1] = swap_lanes(parts[0], parts[1], ZS)
    parts[2], parts[3] = swap_lanes(parts[2], parts[3], ZS)
    parts[0], parts[2] = swap_lanes(parts[0], parts[2], 2 * ZS)
    parts[1], parts[3] = swap_lanes(parts[1], parts[3], 2 * ZS)
    return parts


def fourier_kernel(
    device_ref, kept_hbm, weights_hbm, slots_hbm, x_hbm, table_hbm, later_hbm, o_ref, order_ref, kept_ref, later_ref, kept_s, weights_s, slots_v, x_v,
    table_v, even, odd, acc, sems
):
    small = [
        pltpu.make_async_copy(slots_hbm, slots_v, sems.at[0]),
        pltpu.make_async_copy(x_hbm, x_v, sems.at[1]),
        pltpu.make_async_copy(kept_hbm, kept_s, sems.at[2]),
        pltpu.make_async_copy(weights_hbm, weights_s, sems.at[3]),
    ]
    blocks = [pltpu.make_async_copy(table_hbm.at[i], table_v.at[i], sems.at[4 + i]) for i in range(STEPS)]
    later = pltpu.make_async_copy(later_hbm, later_ref, sems.at[4 + STEPS])
    for copy in small + blocks + [later]:
        copy.start()
    lat = device_ref[0] // LEVS
    small[0].wait()
    order = slot_order(slots_v[...])
    order_ref[...] = jnp.concatenate([order[:, b * LANES : (b + 1) * LANES] for b in range(LEVS)], axis=0).T
    small[2].wait()
    small[3].wait()
    kept = latitude_column([kept_s[j] for j in range(BAND)], jnp.int32(0))
    kept_ref[...] = kept
    latitudes = [lat * BAND + j for j in range(BAND)]
    weight = latitude_column([weights_s[jnp.minimum(i, NLAT - 1 - i)] for i in latitudes], F32(0.0))
    small[1].wait()

    def put(ref, place, value):
        high = value.astype(BF16)
        low = (value - high.astype(F32)).astype(BF16)
        for part, half in enumerate((high, low)):
            ref[pl.ds(place + part * ROWS, 16), :] = half

    for group in range(ROWS // 16):
        x = jnp.concatenate([x_v[4 * group + i].astype(F32) for i in range(4)], axis=0)
        x = [x[:, q * QUARTER : (q + 1) * QUARTER] for q in range(4)]
        sums = x[0] + x[2], x[1] + x[3]
        put(even.at[0], 16 * group, sums[0] + sums[1])
        put(even.at[1], 16 * group, sums[0] - sums[1])
        put(odd, 16 * group, x[0] - x[2])
        put(odd, 16 * group + 2 * ROWS, x[1] - x[3])
    for step in range(STEPS):
        blocks[step].wait()
        if step % 2 == 0:
            raw = jnp.dot(even[step // 2], table_v[step], preferred_element_type=F32)
            raw = raw[:ROWS] + raw[ROWS:]
            real, imaginary = raw[:, :BLOCK], raw[:, BLOCK:]
        else:
            raw = jnp.dot(odd[...], table_v[step], preferred_element_type=F32)
            first = raw[:ROWS] + raw[ROWS : 2 * ROWS]
            second = raw[2 * ROWS : 3 * ROWS] + raw[3 * ROWS :]
            if step == 3:
                second = -second
            real = first[:, :BLOCK] + second[:, BLOCK:]
            imaginary = first[:, BLOCK:] - second[:, :BLOCK]
        scale = jnp.where(class_mask(kept, step), weight, 0.0)
        fourier = jnp.concatenate([real * scale, imaginary * scale], axis=0).astype(BF16)
        part = jnp.dot(fourier, slot_choice(order, step), preferred_element_type=F32)
        if step == 0:
            acc[...] = part
        else:
            acc[...] += part
    choice = row_choice(lat >= NORTH)
    moved = jnp.dot(choice, acc[...].astype(BF16), preferred_element_type=F32)
    for b in range(LEVS):
        block = moved[:, b * LANES : (b + 1) * LANES]
        parts = swap_parts([block[i * CHUNK : (i + 1) * CHUNK] for i in range(YS)])
        for y in range(YS):
            o_ref[y * LEVS + b] = parts[y].astype(BF16)
    later.wait()


def gather_kernel(y_ref, o_ref, rows):
    for y in range(YS):
        for j in range(TILES):
            block = [y_ref[y * LEVS + b, 8 * j : 8 * j + 8, :].astype(F32) for b in range(LEVS)]
            turned = jnp.concatenate(block, axis=0).T
            turned = jnp.concatenate([turned[:LATS], turned[LATS:]], axis=1)
            for part in range(4):
                row, tile = (part * TILES + j) % 4, y * TILES + (part * TILES + j) // 4
                rows[:, row, tile * LANES : (tile + 1) * LANES] = turned[part * ZS : (part + 1) * ZS]
    o_ref[...] = rows[...].astype(BF16)


def scatter_kernel(z_ref, o_ref, rows):
    rows[...] = z_ref[...].astype(F32)
    for y in range(YS):
        for j in range(TILES):
            block = []
            for part in range(4):
                row, tile = (part * TILES + j) % 4, y * TILES + (part * TILES + j) // 4
                block.append(rows[:, row, tile * LANES : (tile + 1) * LANES])
            block = jnp.concatenate(block, axis=0)
            turned = jnp.concatenate([block[:, :LATS], block[:, LATS:]], axis=0).T
            for b in range(LEVS):
                o_ref[y * LEVS + b, 8 + 8 * j : 16 + 8 * j, :] = turned[8 * b : 8 * b + 8].astype(BF16)
    power = jnp.sum(rows[:, :, YS * DATA :], axis=0)
    power = jnp.concatenate([power[:, :LANES], power[:, LANES:]], axis=0)
    for peer in range(YS * LEVS):
        o_ref[peer, :8, :] = power.astype(BF16)


def legendre_kernel(
    device_ref, slots_hbm, diffusion_hbm, z_ref, table_ref, later_hbm, spectral_hbm, o_ref, later_ref, slots_s, diffusion_s,
    spectral_v, comb, sems
):
    copies = [
        pltpu.make_async_copy(slots_hbm, slots_s, sems.at[0]),
        pltpu.make_async_copy(diffusion_hbm, diffusion_s, sems.at[1]),
    ]
    later = pltpu.make_async_copy(later_hbm, later_ref, sems.at[2])
    for copy in copies + [later]:
        copy.start()
    for group in range(NORTH * TILES // 4):
        north, south = [], []
        for u in range(4 * group, 4 * group + 4):
            a, tile = divmod(u, TILES)
            for side, lat in (north, a), (south, LATS - 1 - a):
                y, z = divmod(lat, ZS)
                place = (y * TILES + tile) * LANES
                side.append(z_ref[z, :, place : place + LANES].astype(F32))
        north = jnp.concatenate(north, axis=0)
        south = jnp.concatenate(south, axis=0)
        comb[0, 16 * group : 16 * group + 16, :] = north + south
        comb[1, 16 * group : 16 * group + 16, :] = north - south
    for copy in copies:
        copy.wait()
    copies = [later]
    column = iota((2 * LEVELS, HALF), 1)
    level = iota((2 * LEVELS, 1), 0) // 2
    diffusion = jnp.zeros((2 * LEVELS, 1), F32)
    for i in range(LEVELS):
        diffusion = jnp.where(level == i, diffusion_s[i], diffusion)
    power = [jnp.zeros((1, HALF), F32), jnp.zeros((1, HALF), F32)]
    halves = []
    for q in range(2):
        left = comb[q].T.astype(BF16)
        parts = []
        for t in range(2):
            wave = slots_s[device_ref[0] * 2 + t]
            raw = jnp.dot(left[64 * t : 64 * t + 64], table_ref[t, q], preferred_element_type=F32)
            degree = wave + 2 * column + q
            spectral = jnp.where(degree < MM, raw, 0.0)
            for level in range(LEVELS):
                spectral_v[t, q, level] = spectral[2 * level : 2 * level + 2]
            copies.append(pltpu.make_async_copy(spectral_v.at[t, q], spectral_hbm.at[t, q], sems.at[3 + 2 * t + q]))
            copies[-1].start()
            degree = degree.astype(F32)
            ratio = degree * (degree + 1.0) / (MM * (MM + 1.0))
            damped = (spectral / (1.0 + diffusion * ratio * ratio)).astype(BF16)
            parts.append(
                lax.dot_general(
                    table_ref[t, q], damped, (((1,), (1,)), ((), ())), preferred_element_type=F32
                )
            )
            energy = jnp.sum(spectral * spectral, axis=0, keepdims=True)
            first = wave + q
            moved = pltpu.roll(jnp.broadcast_to(energy, (8, HALF)), first // 2 % HALF, 1)[:1]
            for odd in range(2):
                power[odd] += jnp.where(first % 2 == odd, moved, 0.0)
        halves.append(jnp.concatenate(parts, axis=1))
    source = iota((LANES, 2 * LANES), 0)
    to = iota((LANES, 2 * LANES), 1)
    natural = jnp.zeros((8, 2 * LANES), F32)
    for odd in range(2):
        quarters = [power[odd][:, i * LANES : (i + 1) * LANES] for i in range(4)]
        quarters = jnp.concatenate(quarters + quarters, axis=0).astype(BF16)
        choice = jnp.where(to == 2 * source + odd, 1.0, 0.0).astype(BF16)
        natural += jnp.dot(quarters, choice, preferred_element_type=F32)
    natural = natural[:4].astype(BF16)
    for z in range(ZS):
        o_ref[z, :, YS * DATA :] = natural
    for half, side in enumerate((halves[0] + halves[1], halves[0] - halves[1])):
        for u in range(NORTH * TILES):
            a, tile = divmod(u, TILES)
            y, z = divmod(LATS - 1 - a if half else a, ZS)
            place = (y * TILES + tile) * LANES
            o_ref[z, :, place : place + LANES] = side[4 * u : 4 * u + 4].astype(BF16)
    for copy in copies:
        copy.wait()


def grid_kernel(device_ref, kept_ref, order_ref, y_ref, table_ref, o_hbm, spectrum_ref, points_v, sems):
    kept = kept_ref[...]
    choice = row_choice(device_ref[0] >= NORTH * LEVS)
    back = []
    for b in range(LEVS):
        parts = swap_parts([y_ref[y * LEVS + b, 8:, :].astype(F32) for y in range(YS)])
        back.append(jnp.concatenate(parts, axis=0).astype(BF16))
    back = jnp.concatenate(back, axis=1)
    rows = lax.dot_general(choice, back, (((0,), (0,)), ((), ())), preferred_element_type=F32).astype(BF16)
    numbers = [jnp.broadcast_to(order_ref[:, b : b + 1], (LANES, BLOCK)) for b in range(LEVS)]
    parts = []
    for step in range(STEPS):
        number = iota((LANES, BLOCK), 1) * STEPS + step
        choice = jnp.concatenate([jnp.where(n == number, 1.0, 0.0).astype(BF16) for n in numbers], axis=0)
        numbered = jnp.dot(rows, choice, preferred_element_type=F32)
        mask = class_mask(kept, step)
        real = jnp.where(mask, numbered[:ROWS], 0.0)
        imaginary = jnp.where(mask, numbered[ROWS:], 0.0)
        left = jnp.concatenate([real, imaginary], axis=1)
        if step == 1:
            left = jnp.concatenate([left, jnp.concatenate([-imaginary, real], axis=1)], axis=0)
        if step == 3:
            left = jnp.concatenate([left, jnp.concatenate([imaginary, -real], axis=1)], axis=0)
        parts.append(jnp.dot(left.astype(BF16), table_ref[step], preferred_element_type=F32))
    odd = parts[1] + parts[3]
    plus, minus = parts[0] + parts[2], parts[0] - parts[2]
    copies = []
    for group in range(ROWS // 16):
        place = slice(16 * group, 16 * group + 16)
        turned = slice(ROWS + 16 * group, ROWS + 16 * group + 16)
        quarters = [plus[place] + odd[place], minus[place] + odd[turned], plus[place] - odd[place], minus[place] - odd[turned]]
        points = jnp.concatenate(quarters, axis=1) * math.sqrt(NLON / MM)
        bands = pl.ds(4 * group, 4)
        for i in range(4):
            points_v[4 * group + i] = points[LEV * i : LEV * (i + 1)]
        copies.append(pltpu.make_async_copy(points_v.at[bands], o_hbm.at[bands], sems.at[group]))
        copies[-1].start()
    power = jnp.zeros((8, LANES), F32)
    for peer in range(YS * LEVS):
        power += y_ref[peer, :8, :].astype(F32)
    power = jnp.concatenate([power[i // 2 + 4 * (i % 2)][None] for i in range(8)], axis=0)
    degree = (iota((8, LANES), 0) * LANES + iota((8, LANES), 1)).astype(F32)
    spectrum_ref[...] = power / (2.0 * LEVELS * (degree + 1.0))
    for copy in copies:
        copy.wait()


def in_hbm(x):
    return pltpu.with_memory_space_constraint(x, pltpu.HBM)


def in_vmem(x):
    return pltpu.with_memory_space_constraint(x, pltpu.VMEM)


def exchange(x, axes):
    return lax.all_to_all(x, axes, split_axis=0, concat_axis=0, tiled=True)


def body(grid_fields, legendre, weights, kept_waves, slot_wavenumber, diffusion):
    forward_table, inverse_table = dft_tables()
    device = lax.axis_index(("y", "z", "x", "core")).astype(jnp.int32).reshape(1)
    chunk = (ZS, 4, YS * DATA + 2 * LANES)

    sent, order, kept, legendre = pl.pallas_call(
        fourier_kernel,
        in_specs=[SMEM, HBM, HBM, HBM, HBM, HBM, HBM],
        out_specs=[VMEM, VMEM, VMEM, VMEM],
        out_shape=[
            jax.ShapeDtypeStruct((YS * LEVS, CHUNK, LANES), BF16),
            jax.ShapeDtypeStruct((LANES, LEVS), jnp.int32),
            jax.ShapeDtypeStruct((ROWS, 1), jnp.int32),
            pltpu.VMEM(legendre.shape, BF16),
        ],
        scratch_shapes=[
            pltpu.SMEM((BAND,), jnp.int32),
            pltpu.SMEM((NLAT // 2,), F32),
            pltpu.VMEM((8, LANES), jnp.int32),
            pltpu.VMEM((BAND, LEV, NLON), BF16),
            pltpu.VMEM((STEPS, QUARTER, 2 * BLOCK), BF16),
            pltpu.VMEM((2, 2 * ROWS, QUARTER), BF16),
            pltpu.VMEM((4 * ROWS, QUARTER), BF16),
            pltpu.VMEM((2 * ROWS, MM), F32),
            pltpu.SemaphoreType.DMA((5 + STEPS,)),
        ],
        compiler_params=PARAMS,
        name="fourier",
    )(
        device,
        in_hbm(kept_waves),
        in_hbm(weights),
        in_hbm(slot_wavenumber.reshape(8, LANES)),
        in_hbm(grid_fields.transpose(1, 0, 2)),
        in_hbm(jnp.asarray(forward_table)),
        in_hbm(legendre),
    )
    arrived = exchange(sent, ("y", "x", "core"))
    gathered = pl.pallas_call(
        gather_kernel,
        in_specs=[VMEM],
        out_specs=VMEM,
        out_shape=jax.ShapeDtypeStruct((ZS, 4, YS * DATA), BF16),
        scratch_shapes=[pltpu.VMEM((ZS, 4, YS * DATA), F32)],
        compiler_params=PARAMS,
        name="gather",
    )(arrived)
    gathered = exchange(gathered, ("z",))
    spectral, back, table = pl.pallas_call(
        legendre_kernel,
        in_specs=[SMEM, HBM, HBM, VMEM, VMEM, HBM],
        out_specs=[HBM, VMEM, VMEM],
        out_shape=[
            jax.ShapeDtypeStruct((2, 2, LEVELS, 2, HALF), F32),
            jax.ShapeDtypeStruct(chunk, BF16),
            pltpu.VMEM((STEPS, 2 * BLOCK, QUARTER), BF16),
        ],
        scratch_shapes=[
            pltpu.SMEM((MM,), jnp.int32),
            pltpu.SMEM((LEVELS,), F32),
            pltpu.VMEM((2, 2, LEVELS, 2, HALF), F32),
            pltpu.VMEM((2, NLAT // 2, LANES), F32),
            pltpu.SemaphoreType.DMA((7,)),
        ],
        compiler_params=PARAMS,
        name="legendre",
    )(device, in_hbm(slot_wavenumber), in_hbm(diffusion), gathered, in_vmem(legendre), in_hbm(jnp.asarray(inverse_table)))
    back = exchange(back, ("z",))
    scattered = pl.pallas_call(
        scatter_kernel,
        in_specs=[VMEM],
        out_specs=VMEM,
        out_shape=jax.ShapeDtypeStruct((YS * LEVS, 8 + CHUNK, LANES), BF16),
        scratch_shapes=[pltpu.VMEM(chunk, F32)],
        compiler_params=PARAMS,
        name="scatter",
    )(back)
    returned = exchange(scattered, ("y", "x", "core"))
    grid_out, spectrum = pl.pallas_call(
        grid_kernel,
        in_specs=[SMEM, VMEM, VMEM, VMEM, VMEM],
        out_specs=[HBM, VMEM],
        out_shape=[
            jax.ShapeDtypeStruct((BAND, LEV, NLON), F32),
            jax.ShapeDtypeStruct((8, LANES), F32),
        ],
        scratch_shapes=[
            pltpu.VMEM((BAND, LEV, NLON), F32),
            pltpu.SemaphoreType.DMA((ROWS // 16,)),
        ],
        compiler_params=PARAMS,
        name="grid",
    )(device, kept, order, returned, in_vmem(table))
    return (
        grid_out.transpose(1, 0, 2),
        spectral,
        spectrum.reshape(MM),
    )


def solution(mesh):
    fine = Mesh(mesh.devices.reshape(4, 16, 4, 2), ("y", "z", "x", "core"))
    lat, lev = ("y", "z"), ("x", "core")
    both = lat + lev
    in_specs = (P(lev, lat, None), P(both, None, None, None), P(), P(lat), P(), P())
    out_specs = (P(lev, lat, None), P(both, None, None, None, None), P())
    return jax.shard_map(body, mesh=fine, in_specs=in_specs, out_specs=out_specs, check_vma=False)
```

```python
import math

import jax
import jax.numpy as jnp
import ml_dtypes
import numpy as np
from jax import lax
from jax.experimental import pallas as pl
from jax.experimental.pallas import tpu as pltpu
from jax.sharding import Mesh
from jax.sharding import PartitionSpec as P

NLAT = 1280
NLON = 2688
MM = 1024
HALF = MM // 2
LEVELS = 32
BAND = 20
LEV = 4
ROWS = BAND * LEV
LATS = 64
LEVS = 8
YS = 4
ZS = 16
CHUNK = 2 * ROWS // YS
NORTH = LATS // 2
QUARTER = NLON // 4
STEPS = 4
BLOCK = MM // STEPS
TILES = BAND // 4
LANES = 128
DATA = TILES * LANES

BF16 = jnp.bfloat16
F32 = jnp.float32
VMEM = pl.BlockSpec(memory_space=pltpu.VMEM)
HBM = pl.BlockSpec(memory_space=pltpu.HBM)
SMEM = pl.BlockSpec(memory_space=pltpu.SMEM)
PARAMS = pltpu.CompilerParams(vmem_limit_bytes=20 * 1024 * 1024)


def dft_tables():
    sample = np.arange(QUARTER, dtype=np.int32)[:, None]
    number = np.arange(MM, dtype=np.int32)[None, :]
    angles = (sample * number % NLON).astype(np.float32) * np.float32(2.0 * math.pi / NLON)
    norm_scale = np.float32(1.0 / math.sqrt(NLON))
    cosine = (np.cos(angles) * norm_scale).astype(ml_dtypes.bfloat16)
    sine = (-np.sin(angles) * norm_scale).astype(ml_dtypes.bfloat16)
    rising = np.arange(LANES)
    places = np.concatenate([rising, BLOCK - 1 - rising])
    numbers = places[None, :] * STEPS + np.arange(STEPS)[:, None]
    forward = np.stack([cosine[:, numbers], sine[:, numbers]], axis=2)
    forward = np.ascontiguousarray(forward.transpose(1, 0, 2, 3)).reshape(STEPS, QUARTER, 2 * BLOCK)
    inverse = np.ascontiguousarray(forward.transpose(0, 2, 1))
    return forward, inverse


def iota(shape, dim):
    return lax.broadcasted_iota(jnp.int32, shape, dim)


def pair_number(shape, dim):
    place = iota(shape, dim)
    return place % LANES * STEPS + place // LANES


def slot_order(slots):
    digits = jnp.concatenate([slots // 32, slots % 32], axis=0).astype(F32).astype(BF16)
    source = iota((LANES, HALF), 0)
    to = iota((LANES, HALF), 1)
    choice = jnp.where(source == to % 8 * 16 + to // LATS * 2, 1.0, 0.0).astype(BF16)
    moved = jnp.dot(digits, choice, preferred_element_type=F32)
    row = iota((16, HALF), 0)
    mine = row % 8 == iota((16, HALF), 1) % LATS // 8
    value = jnp.where(mine, moved * jnp.where(row < 8, 32.0, 1.0), 0.0)
    return jnp.sum(value, axis=0, keepdims=True).astype(jnp.int32)


def latitude_column(scalars, zero):
    band = iota((ROWS, 1), 0) // LEV
    column = jnp.full((ROWS, 1), zero)
    for j in range(BAND):
        column = jnp.where(band == j, scalars[j], column)
    return column


def class_mask(kept, step):
    place = iota((ROWS, BLOCK), 1)
    place = jnp.where(place < LANES, place, BLOCK + LANES - 1 - place)
    return place * STEPS + step < kept


def lower_of_pair(wave):
    return jnp.minimum(wave, MM - 1 - wave)


def row_choice(southern):
    to = iota((2 * ROWS, 2 * ROWS), 0)
    source = iota((2 * ROWS, 2 * ROWS), 1)
    band = to // (2 * LEV)
    band = jnp.where(southern, BAND - 1 - band, band)
    wanted = (to % 2) * ROWS + band * LEV + to // 2 % LEV
    return jnp.where(source == wanted, 1.0, 0.0).astype(BF16)


def swap_lanes(even, odd, width):
    high = iota(even.shape, 1) // width % 2 == 1
    return (
        jnp.where(high, pltpu.roll(odd, width, 1), even),
        jnp.where(high, odd, pltpu.roll(even, LANES - width, 1)),
    )


def sort_pair(order, first, second):
    flip = jnp.broadcast_to(order >= HALF, first.shape)
    return jnp.where(flip, second, first), jnp.where(flip, first, second)


def swap_parts(parts):
    parts = list(parts)
    parts[0], parts[1] = swap_lanes(parts[0], parts[1], ZS)
    parts[2], parts[3] = swap_lanes(parts[2], parts[3], ZS)
    parts[0], parts[2] = swap_lanes(parts[0], parts[2], 2 * ZS)
    parts[1], parts[3] = swap_lanes(parts[1], parts[3], 2 * ZS)
    return parts


def fourier_kernel(
    device_ref, kept_hbm, weights_hbm, slots_hbm, x_hbm, table_hbm, later_hbm, o_ref, order_ref, column_ref, kept_ref, later_ref, kept_s, weights_s, slots_v, x_v,
    table_v, even, odd, both, sems
):
    small = [
        pltpu.make_async_copy(slots_hbm, slots_v, sems.at[0]),
        pltpu.make_async_copy(x_hbm, x_v, sems.at[1]),
        pltpu.make_async_copy(kept_hbm, kept_s, sems.at[2]),
        pltpu.make_async_copy(weights_hbm, weights_s, sems.at[3]),
    ]
    blocks = [pltpu.make_async_copy(table_hbm.at[i], table_v.at[i], sems.at[4 + i]) for i in range(STEPS)]
    later = pltpu.make_async_copy(later_hbm, later_ref, sems.at[4 + STEPS])
    for copy in small + blocks + [later]:
        copy.start()
    lat = device_ref[0] // LEVS
    small[0].wait()
    order = slot_order(slots_v[...])
    order_ref[...] = order
    lower = lower_of_pair(order)
    columns = [lower[:, i * LANES : (i + 1) * LANES] for i in range(4)]
    column_ref[...] = jnp.concatenate(columns + columns, axis=0).T
    small[2].wait()
    small[3].wait()
    kept = latitude_column([kept_s[j] for j in range(BAND)], jnp.int32(0))
    kept_ref[...] = kept
    latitudes = [lat * BAND + j for j in range(BAND)]
    weight = latitude_column([weights_s[jnp.minimum(i, NLAT - 1 - i)] for i in latitudes], F32(0.0))
    small[1].wait()

    def put(ref, place, value):
        high = value.astype(BF16)
        low = (value - high.astype(F32)).astype(BF16)
        for part, half in enumerate((high, low)):
            ref[pl.ds(place + part * ROWS, 16), :] = half

    for group in range(ROWS // 16):
        x = jnp.concatenate([x_v[4 * group + i].astype(F32) for i in range(4)], axis=0)
        x = [x[:, q * QUARTER : (q + 1) * QUARTER] for q in range(4)]
        sums = x[0] + x[2], x[1] + x[3]
        put(even.at[0], 16 * group, sums[0] + sums[1])
        put(even.at[1], 16 * group, sums[0] - sums[1])
        put(odd, 16 * group, x[0] - x[2])
        put(odd, 16 * group + 2 * ROWS, x[1] - x[3])
    for step in range(STEPS):
        blocks[step].wait()
        if step % 2 == 0:
            raw = jnp.dot(even[step // 2], table_v[step], preferred_element_type=F32)
            raw = raw[:ROWS] + raw[ROWS:]
            real, imaginary = raw[:, :BLOCK], raw[:, BLOCK:]
        else:
            raw = jnp.dot(odd[...], table_v[step], preferred_element_type=F32)
            first = raw[:ROWS] + raw[ROWS : 2 * ROWS]
            second = raw[2 * ROWS : 3 * ROWS] + raw[3 * ROWS :]
            if step == 3:
                second = -second
            real = first[:, :BLOCK] + second[:, BLOCK:]
            imaginary = first[:, BLOCK:] - second[:, :BLOCK]
        scale = jnp.where(class_mask(kept, step), weight, 0.0)
        fourier = jnp.concatenate([real * scale, imaginary * scale], axis=0).astype(BF16)
        both[: 2 * ROWS, step * LANES : (step + 1) * LANES] = fourier[:, :LANES]
        both[2 * ROWS :, (3 - step) * LANES : (4 - step) * LANES] = fourier[:, LANES:]
    choice = jnp.where(lower == pair_number((HALF, HALF), 0), 1.0, 0.0).astype(BF16)
    moved = jnp.dot(both[...], choice, preferred_element_type=F32)
    moved = sort_pair(order, moved[: 2 * ROWS], moved[2 * ROWS :])
    choice = row_choice(lat >= NORTH)
    moved = jnp.concatenate([half.astype(BF16) for half in moved], axis=1)
    moved = jnp.dot(choice, moved, preferred_element_type=F32)
    for i in range(LEVS // 2):
        place = i * LANES
        pair = swap_lanes(moved[:, place : place + LANES], moved[:, HALF + place : HALF + place + LANES], LATS)
        for b, block in zip((2 * i, 2 * i + 1), pair):
            parts = swap_parts([block[k * CHUNK : (k + 1) * CHUNK] for k in range(YS)])
            for y in range(YS):
                o_ref[y * LEVS + b] = parts[y].astype(BF16)
    later.wait()


def gather_kernel(y_ref, o_ref, rows):
    for y in range(YS):
        for j in range(TILES):
            block = [y_ref[y * LEVS + b, 8 * j : 8 * j + 8, :].astype(F32) for b in range(LEVS)]
            turned = jnp.concatenate(block, axis=0).T
            turned = jnp.concatenate([turned[:LATS], turned[LATS:]], axis=1)
            for part in range(4):
                row, tile = (part * TILES + j) % 4, y * TILES + (part * TILES + j) // 4
                rows[:, row, tile * LANES : (tile + 1) * LANES] = turned[part * ZS : (part + 1) * ZS]
    o_ref[...] = rows[...].astype(BF16)


def scatter_kernel(z_ref, o_ref, rows):
    rows[...] = z_ref[...].astype(F32)
    for y in range(YS):
        for j in range(TILES):
            block = []
            for part in range(4):
                row, tile = (part * TILES + j) % 4, y * TILES + (part * TILES + j) // 4
                block.append(rows[:, row, tile * LANES : (tile + 1) * LANES])
            block = jnp.concatenate(block, axis=0)
            turned = jnp.concatenate([block[:, :LATS], block[:, LATS:]], axis=0).T
            for b in range(LEVS):
                o_ref[y * LEVS + b, 8 + 8 * j : 16 + 8 * j, :] = turned[8 * b : 8 * b + 8].astype(BF16)
    power = jnp.sum(rows[:, :, YS * DATA :], axis=0)
    power = jnp.concatenate([power[:, :LANES], power[:, LANES:]], axis=0)
    for peer in range(YS * LEVS):
        o_ref[peer, :8, :] = power.astype(BF16)


def legendre_kernel(
    device_ref, slots_hbm, diffusion_hbm, z_ref, table_ref, later_hbm, spectral_hbm, o_ref, later_ref, slots_s, diffusion_s,
    spectral_v, comb, sems
):
    copies = [
        pltpu.make_async_copy(slots_hbm, slots_s, sems.at[0]),
        pltpu.make_async_copy(diffusion_hbm, diffusion_s, sems.at[1]),
    ]
    later = pltpu.make_async_copy(later_hbm, later_ref, sems.at[2])
    for copy in copies + [later]:
        copy.start()
    for group in range(NORTH * TILES // 4):
        north, south = [], []
        for u in range(4 * group, 4 * group + 4):
            a, tile = divmod(u, TILES)
            for side, lat in (north, a), (south, LATS - 1 - a):
                y, z = divmod(lat, ZS)
                place = (y * TILES + tile) * LANES
                side.append(z_ref[z, :, place : place + LANES].astype(F32))
        north = jnp.concatenate(north, axis=0)
        south = jnp.concatenate(south, axis=0)
        comb[0, 16 * group : 16 * group + 16, :] = north + south
        comb[1, 16 * group : 16 * group + 16, :] = north - south
    for copy in copies:
        copy.wait()
    copies = [later]
    column = iota((2 * LEVELS, HALF), 1)
    level = iota((2 * LEVELS, 1), 0) // 2
    diffusion = jnp.zeros((2 * LEVELS, 1), F32)
    for i in range(LEVELS):
        diffusion = jnp.where(level == i, diffusion_s[i], diffusion)
    power = [jnp.zeros((1, HALF), F32), jnp.zeros((1, HALF), F32)]
    halves = []
    for q in range(2):
        left = comb[q].T.astype(BF16)
        parts = []
        for t in range(2):
            wave = slots_s[device_ref[0] * 2 + t]
            raw = jnp.dot(left[64 * t : 64 * t + 64], table_ref[t, q], preferred_element_type=F32)
            degree = wave + 2 * column + q
            spectral = jnp.where(degree < MM, raw, 0.0)
            for level in range(LEVELS):
                spectral_v[t, q, level] = spectral[2 * level : 2 * level + 2]
            copies.append(pltpu.make_async_copy(spectral_v.at[t, q], spectral_hbm.at[t, q], sems.at[3 + 2 * t + q]))
            copies[-1].start()
            degree = degree.astype(F32)
            ratio = degree * (degree + 1.0) / (MM * (MM + 1.0))
            damped = (spectral / (1.0 + diffusion * ratio * ratio)).astype(BF16)
            parts.append(
                lax.dot_general(
                    table_ref[t, q], damped, (((1,), (1,)), ((), ())), preferred_element_type=F32
                )
            )
            energy = jnp.sum(spectral * spectral, axis=0, keepdims=True)
            first = wave + q
            moved = pltpu.roll(jnp.broadcast_to(energy, (8, HALF)), first // 2 % HALF, 1)[:1]
            for odd in range(2):
                power[odd] += jnp.where(first % 2 == odd, moved, 0.0)
        halves.append(jnp.concatenate(parts, axis=1))
    source = iota((LANES, 2 * LANES), 0)
    to = iota((LANES, 2 * LANES), 1)
    natural = jnp.zeros((8, 2 * LANES), F32)
    for odd in range(2):
        quarters = [power[odd][:, i * LANES : (i + 1) * LANES] for i in range(4)]
        quarters = jnp.concatenate(quarters + quarters, axis=0).astype(BF16)
        choice = jnp.where(to == 2 * source + odd, 1.0, 0.0).astype(BF16)
        natural += jnp.dot(quarters, choice, preferred_element_type=F32)
    natural = natural[:4].astype(BF16)
    for z in range(ZS):
        o_ref[z, :, YS * DATA :] = natural
    for half, side in enumerate((halves[0] + halves[1], halves[0] - halves[1])):
        for u in range(NORTH * TILES):
            a, tile = divmod(u, TILES)
            y, z = divmod(LATS - 1 - a if half else a, ZS)
            place = (y * TILES + tile) * LANES
            o_ref[z, :, place : place + LANES] = side[4 * u : 4 * u + 4].astype(BF16)
    for copy in copies:
        copy.wait()


def grid_kernel(device_ref, kept_ref, order_ref, column_ref, y_ref, table_ref, o_ref, spectrum_ref):
    kept = kept_ref[...]
    choice = row_choice(device_ref[0] >= NORTH * LEVS)
    firsts, seconds = [], []
    for i in range(LEVS // 2):
        pair = []
        for b in (2 * i, 2 * i + 1):
            parts = swap_parts([y_ref[y * LEVS + b, 8:, :].astype(F32) for y in range(YS)])
            pair.append(jnp.concatenate(parts, axis=0))
        first, second = swap_lanes(pair[0], pair[1], LATS)
        firsts.append(first)
        seconds.append(second)
    back = sort_pair(order_ref[...], jnp.concatenate(firsts, axis=1), jnp.concatenate(seconds, axis=1))
    back = jnp.concatenate([half.astype(BF16) for half in back], axis=1)
    rows = lax.dot_general(choice, back, (((0,), (0,)), ((), ())), preferred_element_type=F32).astype(BF16)
    rows = jnp.concatenate([rows[:, :HALF], rows[:, HALF:]], axis=0)
    number = pair_number((LANES, HALF), 1)
    choice = [jnp.where(column_ref[:, i : i + 1] == number, 1.0, 0.0).astype(BF16) for i in range(HALF // LANES)]
    numbered = jnp.dot(rows, jnp.concatenate(choice, axis=0), preferred_element_type=F32)
    parts = []
    for step in range(STEPS):
        low = numbered[: 2 * ROWS, step * LANES : (step + 1) * LANES]
        high = numbered[2 * ROWS :, (3 - step) * LANES : (4 - step) * LANES]
        found = jnp.concatenate([low, high], axis=1)
        mask = class_mask(kept, step)
        real = jnp.where(mask, found[:ROWS], 0.0)
        imaginary = jnp.where(mask, found[ROWS:], 0.0)
        left = jnp.concatenate([real, imaginary], axis=1)
        if step == 1:
            left = jnp.concatenate([left, jnp.concatenate([-imaginary, real], axis=1)], axis=0)
        if step == 3:
            left = jnp.concatenate([left, jnp.concatenate([imaginary, -real], axis=1)], axis=0)
        parts.append(jnp.dot(left.astype(BF16), table_ref[step], preferred_element_type=F32))
    odd = parts[1] + parts[3]
    plus, minus = parts[0] + parts[2], parts[0] - parts[2]
    for group in range(ROWS // 16):
        place = slice(16 * group, 16 * group + 16)
        turned = slice(ROWS + 16 * group, ROWS + 16 * group + 16)
        quarters = [plus[place] + odd[place], minus[place] + odd[turned], plus[place] - odd[place], minus[place] - odd[turned]]
        points = jnp.concatenate(quarters, axis=1) * math.sqrt(NLON / MM)
        for i in range(4):
            o_ref[4 * group + i] = points[LEV * i : LEV * (i + 1)]
    power = jnp.zeros((8, LANES), F32)
    for peer in range(YS * LEVS):
        power += y_ref[peer, :8, :].astype(F32)
    power = jnp.concatenate([power[i // 2 + 4 * (i % 2)][None] for i in range(8)], axis=0)
    degree = (iota((8, LANES), 0) * LANES + iota((8, LANES), 1)).astype(F32)
    spectrum_ref[...] = power / (2.0 * LEVELS * (degree + 1.0))


def in_hbm(x):
    return pltpu.with_memory_space_constraint(x, pltpu.HBM)


def in_vmem(x):
    return pltpu.with_memory_space_constraint(x, pltpu.VMEM)


def exchange(x, axes):
    return lax.all_to_all(x, axes, split_axis=0, concat_axis=0, tiled=True)


def body(grid_fields, legendre, weights, kept_waves, slot_wavenumber, diffusion):
    forward_table, inverse_table = dft_tables()
    device = lax.axis_index(("y", "z", "x", "core")).astype(jnp.int32).reshape(1)
    chunk = (ZS, 4, YS * DATA + 2 * LANES)

    sent, order, column, kept, legendre = pl.pallas_call(
        fourier_kernel,
        in_specs=[SMEM, HBM, HBM, HBM, HBM, HBM, HBM],
        out_specs=[VMEM, VMEM, VMEM, VMEM, VMEM],
        out_shape=[
            jax.ShapeDtypeStruct((YS * LEVS, CHUNK, LANES), BF16),
            jax.ShapeDtypeStruct((1, HALF), jnp.int32),
            jax.ShapeDtypeStruct((LANES, 8), jnp.int32),
            jax.ShapeDtypeStruct((ROWS, 1), jnp.int32),
            pltpu.VMEM(legendre.shape, BF16),
        ],
        scratch_shapes=[
            pltpu.SMEM((BAND,), jnp.int32),
            pltpu.SMEM((NLAT // 2,), F32),
            pltpu.VMEM((8, LANES), jnp.int32),
            pltpu.VMEM((BAND, LEV, NLON), BF16),
            pltpu.VMEM((STEPS, QUARTER, 2 * BLOCK), BF16),
            pltpu.VMEM((2, 2 * ROWS, QUARTER), BF16),
            pltpu.VMEM((4 * ROWS, QUARTER), BF16),
            pltpu.VMEM((4 * ROWS, HALF), BF16),
            pltpu.SemaphoreType.DMA((5 + STEPS,)),
        ],
        compiler_params=PARAMS,
        name="fourier",
    )(
        device,
        in_hbm(kept_waves),
        in_hbm(weights),
        in_hbm(slot_wavenumber.reshape(8, LANES)),
        in_hbm(grid_fields.transpose(1, 0, 2)),
        in_hbm(jnp.asarray(forward_table)),
        in_hbm(legendre),
    )
    arrived = exchange(sent, ("y", "x", "core"))
    gathered = pl.pallas_call(
        gather_kernel,
        in_specs=[VMEM],
        out_specs=VMEM,
        out_shape=jax.ShapeDtypeStruct((ZS, 4, YS * DATA), BF16),
        scratch_shapes=[pltpu.VMEM((ZS, 4, YS * DATA), F32)],
        compiler_params=PARAMS,
        name="gather",
    )(arrived)
    gathered = exchange(gathered, ("z",))
    spectral, back, table = pl.pallas_call(
        legendre_kernel,
        in_specs=[SMEM, HBM, HBM, VMEM, VMEM, HBM],
        out_specs=[HBM, VMEM, VMEM],
        out_shape=[
            jax.ShapeDtypeStruct((2, 2, LEVELS, 2, HALF), F32),
            jax.ShapeDtypeStruct(chunk, BF16),
            pltpu.VMEM((STEPS, 2 * BLOCK, QUARTER), BF16),
        ],
        scratch_shapes=[
            pltpu.SMEM((MM,), jnp.int32),
            pltpu.SMEM((LEVELS,), F32),
            pltpu.VMEM((2, 2, LEVELS, 2, HALF), F32),
            pltpu.VMEM((2, NLAT // 2, LANES), F32),
            pltpu.SemaphoreType.DMA((7,)),
        ],
        compiler_params=PARAMS,
        name="legendre",
    )(device, in_hbm(slot_wavenumber), in_hbm(diffusion), gathered, in_vmem(legendre), in_hbm(jnp.asarray(inverse_table)))
    back = exchange(back, ("z",))
    scattered = pl.pallas_call(
        scatter_kernel,
        in_specs=[VMEM],
        out_specs=VMEM,
        out_shape=jax.ShapeDtypeStruct((YS * LEVS, 8 + CHUNK, LANES), BF16),
        scratch_shapes=[pltpu.VMEM(chunk, F32)],
        compiler_params=PARAMS,
        name="scatter",
    )(back)
    returned = exchange(scattered, ("y", "x", "core"))
    grid_out, spectrum = pl.pallas_call(
        grid_kernel,
        in_specs=[SMEM, VMEM, VMEM, VMEM, VMEM, VMEM],
        out_specs=[VMEM, VMEM],
        out_shape=[
            jax.ShapeDtypeStruct((BAND, LEV, NLON), F32),
            jax.ShapeDtypeStruct((8, LANES), F32),
        ],
        compiler_params=PARAMS,
        name="grid",
    )(device, kept, order, column, returned, in_vmem(table))
    return (
        grid_out.transpose(1, 0, 2),
        spectral,
        spectrum.reshape(MM),
    )


def solution(mesh):
    fine = Mesh(mesh.devices.reshape(4, 16, 4, 2), ("y", "z", "x", "core"))
    lat, lev = ("y", "z"), ("x", "core")
    both = lat + lev
    in_specs = (P(lev, lat, None), P(both, None, None, None), P(), P(lat), P(), P())
    out_specs = (P(lev, lat, None), P(both, None, None, None, None), P())
    return jax.shard_map(body, mesh=fine, in_specs=in_specs, out_specs=out_specs, check_vma=False)
```

```python
import math

import jax
import jax.numpy as jnp
import ml_dtypes
import numpy as np
from jax import lax
from jax.experimental import pallas as pl
from jax.experimental.pallas import tpu as pltpu
from jax.sharding import Mesh
from jax.sharding import PartitionSpec as P

NLAT = 1280
NLON = 2688
MM = 1024
HALF = MM // 2
LEVELS = 32
BAND = 20
LEV = 4
ROWS = BAND * LEV
LATS = 64
LEVS = 8
YS = 4
ZS = 16
CHUNK = 2 * ROWS // YS
NORTH = LATS // 2
QUARTER = NLON // 4
STEPS = 4
BLOCK = MM // STEPS
TILES = BAND // 4
LANES = 128
DATA = TILES * LANES

BF16 = jnp.bfloat16
F32 = jnp.float32
VMEM = pl.BlockSpec(memory_space=pltpu.VMEM)
HBM = pl.BlockSpec(memory_space=pltpu.HBM)
SMEM = pl.BlockSpec(memory_space=pltpu.SMEM)
PARAMS = pltpu.CompilerParams(vmem_limit_bytes=20 * 1024 * 1024)


def dft_tables():
    sample = np.arange(QUARTER, dtype=np.int32)[:, None]
    number = np.arange(MM, dtype=np.int32)[None, :]
    angles = (sample * number % NLON).astype(np.float32) * np.float32(2.0 * math.pi / NLON)
    norm_scale = np.float32(1.0 / math.sqrt(NLON))
    cosine = (np.cos(angles) * norm_scale).astype(ml_dtypes.bfloat16)
    sine = (-np.sin(angles) * norm_scale).astype(ml_dtypes.bfloat16)
    rising = np.arange(LANES)
    places = np.concatenate([rising, BLOCK - 1 - rising])
    numbers = places[None, :] * STEPS + np.arange(STEPS)[:, None]
    forward = np.stack([cosine[:, numbers], sine[:, numbers]], axis=2)
    forward = np.ascontiguousarray(forward.transpose(1, 0, 2, 3)).reshape(STEPS, QUARTER, 2 * BLOCK)
    inverse = np.ascontiguousarray(forward.transpose(0, 2, 1))
    return forward, inverse


def iota(shape, dim):
    return lax.broadcasted_iota(jnp.int32, shape, dim)


def pair_number(shape, dim):
    place = iota(shape, dim)
    return place % LANES * STEPS + place // LANES


def slot_order(slots):
    digits = jnp.concatenate([slots // 32, slots % 32], axis=0).astype(F32).astype(BF16)
    source = iota((LANES, HALF), 0)
    to = iota((LANES, HALF), 1)
    choice = jnp.where(source == to % 8 * 16 + to // LATS * 2, 1.0, 0.0).astype(BF16)
    moved = jnp.dot(digits, choice, preferred_element_type=F32)
    row = iota((16, HALF), 0)
    mine = row % 8 == iota((16, HALF), 1) % LATS // 8
    value = jnp.where(mine, moved * jnp.where(row < 8, 32.0, 1.0), 0.0)
    return jnp.sum(value, axis=0, keepdims=True).astype(jnp.int32)


def latitude_column(scalars, zero):
    band = iota((ROWS, 1), 0) // LEV
    column = jnp.full((ROWS, 1), zero)
    for j in range(BAND):
        column = jnp.where(band == j, scalars[j], column)
    return column


def class_mask(kept, step):
    place = iota((ROWS, BLOCK), 1)
    place = jnp.where(place < LANES, place, BLOCK + LANES - 1 - place)
    return place * STEPS + step < kept


def lower_of_pair(wave):
    return jnp.minimum(wave, MM - 1 - wave)


def row_choice(southern):
    to = iota((2 * ROWS, 2 * ROWS), 0)
    source = iota((2 * ROWS, 2 * ROWS), 1)
    band = to // (2 * LEV)
    band = jnp.where(southern, BAND - 1 - band, band)
    wanted = (to % 2) * ROWS + band * LEV + to // 2 % LEV
    return jnp.where(source == wanted, 1.0, 0.0).astype(BF16)


def swap_lanes(even, odd, width):
    high = iota(even.shape, 1) // width % 2 == 1
    return (
        jnp.where(high, pltpu.roll(odd, width, 1), even),
        jnp.where(high, odd, pltpu.roll(even, LANES - width, 1)),
    )


def sort_pair(order, first, second):
    flip = jnp.broadcast_to(order >= HALF, first.shape)
    return jnp.where(flip, second, first), jnp.where(flip, first, second)


def swap_parts(parts):
    parts = list(parts)
    parts[0], parts[1] = swap_lanes(parts[0], parts[1], ZS)
    parts[2], parts[3] = swap_lanes(parts[2], parts[3], ZS)
    parts[0], parts[2] = swap_lanes(parts[0], parts[2], 2 * ZS)
    parts[1], parts[3] = swap_lanes(parts[1], parts[3], 2 * ZS)
    return parts


def fourier_kernel(
    device_ref, kept_hbm, weights_hbm, diffusion_hbm, slots_hbm, x_hbm, table_hbm, o_ref, order_ref, column_ref,
    kept_ref, wave_ref, diffusion_ref, kept_s, weights_s, diffusion_s, slots_v, x_v,
    table_v, even, odd, both, sems
):
    small = [
        pltpu.make_async_copy(slots_hbm, slots_v, sems.at[0]),
        pltpu.make_async_copy(x_hbm, x_v, sems.at[1]),
        pltpu.make_async_copy(kept_hbm, kept_s, sems.at[2]),
        pltpu.make_async_copy(weights_hbm, weights_s, sems.at[3]),
        pltpu.make_async_copy(diffusion_hbm, diffusion_s, sems.at[4 + STEPS]),
    ]
    blocks = [pltpu.make_async_copy(table_hbm.at[i], table_v.at[i], sems.at[4 + i]) for i in range(STEPS)]
    for copy in small + blocks:
        copy.start()
    lat = device_ref[0] // LEVS
    small[0].wait()
    slots = slots_v[...]
    mine = iota((8, LANES), 0) * LANES + iota((8, LANES), 1) == device_ref[0] * 2
    mine = jnp.sum(jnp.where(mine, slots.astype(F32), 0.0), axis=0, keepdims=True)
    wave_ref[...] = jnp.broadcast_to(jnp.sum(mine, axis=1, keepdims=True).astype(jnp.int32), (1, LANES))
    order = slot_order(slots)
    order_ref[...] = order
    lower = lower_of_pair(order)
    columns = [lower[:, i * LANES : (i + 1) * LANES] for i in range(4)]
    column_ref[...] = jnp.concatenate(columns + columns, axis=0).T
    small[2].wait()
    small[3].wait()
    small[4].wait()
    level = iota((2 * LEVELS, 1), 0) // 2
    diffusion = jnp.zeros((2 * LEVELS, 1), F32)
    for i in range(LEVELS):
        diffusion = jnp.where(level == i, diffusion_s[i], diffusion)
    diffusion_ref[...] = diffusion
    kept = latitude_column([kept_s[j] for j in range(BAND)], jnp.int32(0))
    kept_ref[...] = kept
    latitudes = [lat * BAND + j for j in range(BAND)]
    weight = latitude_column([weights_s[jnp.minimum(i, NLAT - 1 - i)] for i in latitudes], F32(0.0))
    small[1].wait()

    def put(ref, place, value):
        high = value.astype(BF16)
        low = (value - high.astype(F32)).astype(BF16)
        for part, half in enumerate((high, low)):
            ref[pl.ds(place + part * ROWS, 16), :] = half

    for group in range(ROWS // 16):
        x = jnp.concatenate([x_v[4 * group + i].astype(F32) for i in range(4)], axis=0)
        x = [x[:, q * QUARTER : (q + 1) * QUARTER] for q in range(4)]
        sums = x[0] + x[2], x[1] + x[3]
        put(even.at[0], 16 * group, sums[0] + sums[1])
        put(even.at[1], 16 * group, sums[0] - sums[1])
        put(odd, 16 * group, x[0] - x[2])
        put(odd, 16 * group + 2 * ROWS, x[1] - x[3])
    for step in range(STEPS):
        blocks[step].wait()
        if step % 2 == 0:
            raw = jnp.dot(even[step // 2], table_v[step], preferred_element_type=F32)
            raw = raw[:ROWS] + raw[ROWS:]
            real, imaginary = raw[:, :BLOCK], raw[:, BLOCK:]
        else:
            raw = jnp.dot(odd[...], table_v[step], preferred_element_type=F32)
            first = raw[:ROWS] + raw[ROWS : 2 * ROWS]
            second = raw[2 * ROWS : 3 * ROWS] + raw[3 * ROWS :]
            if step == 3:
                second = -second
            real = first[:, :BLOCK] + second[:, BLOCK:]
            imaginary = first[:, BLOCK:] - second[:, :BLOCK]
        scale = jnp.where(class_mask(kept, step), weight, 0.0)
        fourier = jnp.concatenate([real * scale, imaginary * scale], axis=0).astype(BF16)
        both[: 2 * ROWS, step * LANES : (step + 1) * LANES] = fourier[:, :LANES]
        both[2 * ROWS :, (3 - step) * LANES : (4 - step) * LANES] = fourier[:, LANES:]
    choice = jnp.where(lower == pair_number((HALF, HALF), 0), 1.0, 0.0).astype(BF16)
    moved = jnp.dot(both[...], choice, preferred_element_type=F32)
    moved = sort_pair(order, moved[: 2 * ROWS], moved[2 * ROWS :])
    choice = row_choice(lat >= NORTH)
    moved = jnp.concatenate([half.astype(BF16) for half in moved], axis=1)
    moved = jnp.dot(choice, moved, preferred_element_type=F32)
    for i in range(LEVS // 2):
        place = i * LANES
        pair = swap_lanes(moved[:, place : place + LANES], moved[:, HALF + place : HALF + place + LANES], LATS)
        for b, block in zip((2 * i, 2 * i + 1), pair):
            parts = swap_parts([block[k * CHUNK : (k + 1) * CHUNK] for k in range(YS)])
            for y in range(YS):
                o_ref[y * LEVS + b] = parts[y].astype(BF16)


def gather_kernel(y_ref, o_ref, rows):
    for y in range(YS):
        for j in range(TILES):
            block = [y_ref[y * LEVS + b, 8 * j : 8 * j + 8, :].astype(F32) for b in range(LEVS)]
            turned = jnp.concatenate(block, axis=0).T
            turned = jnp.concatenate([turned[:LATS], turned[LATS:]], axis=1)
            for part in range(4):
                row, tile = (part * TILES + j) % 4, y * TILES + (part * TILES + j) // 4
                rows[:, row, tile * LANES : (tile + 1) * LANES] = turned[part * ZS : (part + 1) * ZS]
    o_ref[...] = rows[...].astype(BF16)


def scatter_kernel(z_ref, o_ref, rows):
    rows[...] = z_ref[...].astype(F32)
    for y in range(YS):
        for j in range(TILES):
            block = []
            for part in range(4):
                row, tile = (part * TILES + j) % 4, y * TILES + (part * TILES + j) // 4
                block.append(rows[:, row, tile * LANES : (tile + 1) * LANES])
            block = jnp.concatenate(block, axis=0)
            turned = jnp.concatenate([block[:, :LATS], block[:, LATS:]], axis=0).T
            for b in range(LEVS):
                o_ref[y * LEVS + b, 8 + 8 * j : 16 + 8 * j, :] = turned[8 * b : 8 * b + 8].astype(BF16)
    power = jnp.sum(rows[:, :, YS * DATA :], axis=0)
    power = jnp.concatenate([power[:, :LANES], power[:, LANES:]], axis=0)
    for peer in range(YS * LEVS):
        o_ref[peer, :8, :] = power.astype(BF16)


def legendre_kernel(
    wave_ref, diffusion_ref, z_ref, table_ref, spectral_hbm, o_ref, spectral_v, comb, sems
):
    copies = []
    for group in range(NORTH * TILES // 4):
        north, south = [], []
        for u in range(4 * group, 4 * group + 4):
            a, tile = divmod(u, TILES)
            for side, lat in (north, a), (south, LATS - 1 - a):
                y, z = divmod(lat, ZS)
                place = (y * TILES + tile) * LANES
                side.append(z_ref[z, :, place : place + LANES].astype(F32))
        north = jnp.concatenate(north, axis=0)
        south = jnp.concatenate(south, axis=0)
        comb[0, 16 * group : 16 * group + 16, :] = north + south
        comb[1, 16 * group : 16 * group + 16, :] = north - south
    column = iota((2 * LEVELS, HALF), 1)
    diffusion = diffusion_ref[...]
    waves = [wave_ref[...], MM - 1 - wave_ref[...]]
    waves = [jnp.concatenate([wave] * (HALF // LANES), axis=1) for wave in waves]
    power = [jnp.zeros((1, HALF), F32), jnp.zeros((1, HALF), F32)]
    halves = []
    for q in range(2):
        left = comb[q].T.astype(BF16)
        parts = []
        for t in range(2):
            wave = waves[t]
            raw = jnp.dot(left[64 * t : 64 * t + 64], table_ref[t, q], preferred_element_type=F32)
            degree = wave + 2 * column + q
            spectral = jnp.where(degree < MM, raw, 0.0)
            for level in range(LEVELS):
                spectral_v[t, q, level] = spectral[2 * level : 2 * level + 2]
            copies.append(pltpu.make_async_copy(spectral_v.at[t, q], spectral_hbm.at[t, q], sems.at[2 * t + q]))
            copies[-1].start()
            degree = degree.astype(F32)
            ratio = degree * (degree + 1.0) / (MM * (MM + 1.0))
            damped = (spectral / (1.0 + diffusion * ratio * ratio)).astype(BF16)
            parts.append(
                lax.dot_general(
                    table_ref[t, q], damped, (((1,), (1,)), ((), ())), preferred_element_type=F32
                )
            )
            energy = jnp.sum(spectral * spectral, axis=0, keepdims=True)
            first = wave + q
            moved = jnp.broadcast_to(energy, (8, HALF))
            for bit in range(9):
                moved = jnp.where(first // 2**bit // 2 % 2 == 1, pltpu.roll(moved, 2**bit, 1), moved)
            moved = moved[:1]
            for odd in range(2):
                power[odd] += jnp.where(first % 2 == odd, moved, 0.0)
        halves.append(jnp.concatenate(parts, axis=1))
    source = iota((LANES, 2 * LANES), 0)
    to = iota((LANES, 2 * LANES), 1)
    natural = jnp.zeros((8, 2 * LANES), F32)
    for odd in range(2):
        quarters = [power[odd][:, i * LANES : (i + 1) * LANES] for i in range(4)]
        quarters = jnp.concatenate(quarters + quarters, axis=0).astype(BF16)
        choice = jnp.where(to == 2 * source + odd, 1.0, 0.0).astype(BF16)
        natural += jnp.dot(quarters, choice, preferred_element_type=F32)
    natural = natural[:4].astype(BF16)
    for z in range(ZS):
        o_ref[z, :, YS * DATA :] = natural
    for half, side in enumerate((halves[0] + halves[1], halves[0] - halves[1])):
        for u in range(NORTH * TILES):
            a, tile = divmod(u, TILES)
            y, z = divmod(LATS - 1 - a if half else a, ZS)
            place = (y * TILES + tile) * LANES
            o_ref[z, :, place : place + LANES] = side[4 * u : 4 * u + 4].astype(BF16)
    for copy in copies:
        copy.wait()


def grid_kernel(device_ref, kept_ref, order_ref, column_ref, y_ref, table_ref, o_ref, spectrum_ref):
    kept = kept_ref[...]
    choice = row_choice(device_ref[0] >= NORTH * LEVS)
    firsts, seconds = [], []
    for i in range(LEVS // 2):
        pair = []
        for b in (2 * i, 2 * i + 1):
            parts = swap_parts([y_ref[y * LEVS + b, 8:, :].astype(F32) for y in range(YS)])
            pair.append(jnp.concatenate(parts, axis=0))
        first, second = swap_lanes(pair[0], pair[1], LATS)
        firsts.append(first)
        seconds.append(second)
    back = sort_pair(order_ref[...], jnp.concatenate(firsts, axis=1), jnp.concatenate(seconds, axis=1))
    back = jnp.concatenate([half.astype(BF16) for half in back], axis=1)
    rows = lax.dot_general(choice, back, (((0,), (0,)), ((), ())), preferred_element_type=F32).astype(BF16)
    rows = jnp.concatenate([rows[:, :HALF], rows[:, HALF:]], axis=0)
    number = pair_number((LANES, HALF), 1)
    choice = [jnp.where(column_ref[:, i : i + 1] == number, 1.0, 0.0).astype(BF16) for i in range(HALF // LANES)]
    numbered = jnp.dot(rows, jnp.concatenate(choice, axis=0), preferred_element_type=F32)
    parts = []
    for step in range(STEPS):
        low = numbered[: 2 * ROWS, step * LANES : (step + 1) * LANES]
        high = numbered[2 * ROWS :, (3 - step) * LANES : (4 - step) * LANES]
        found = jnp.concatenate([low, high], axis=1)
        mask = class_mask(kept, step)
        real = jnp.where(mask, found[:ROWS], 0.0)
        imaginary = jnp.where(mask, found[ROWS:], 0.0)
        left = jnp.concatenate([real, imaginary], axis=1)
        if step == 1:
            left = jnp.concatenate([left, jnp.concatenate([-imaginary, real], axis=1)], axis=0)
        if step == 3:
            left = jnp.concatenate([left, jnp.concatenate([imaginary, -real], axis=1)], axis=0)
        parts.append(jnp.dot(left.astype(BF16), table_ref[step], preferred_element_type=F32))
    odd = parts[1] + parts[3]
    plus, minus = parts[0] + parts[2], parts[0] - parts[2]
    for group in range(ROWS // 16):
        place = slice(16 * group, 16 * group + 16)
        turned = slice(ROWS + 16 * group, ROWS + 16 * group + 16)
        quarters = [plus[place] + odd[place], minus[place] + odd[turned], plus[place] - odd[place], minus[place] - odd[turned]]
        points = jnp.concatenate(quarters, axis=1) * math.sqrt(NLON / MM)
        for i in range(4):
            o_ref[4 * group + i] = points[LEV * i : LEV * (i + 1)]
    power = jnp.zeros((8, LANES), F32)
    for peer in range(YS * LEVS):
        power += y_ref[peer, :8, :].astype(F32)
    power = jnp.concatenate([power[i // 2 + 4 * (i % 2)][None] for i in range(8)], axis=0)
    degree = (iota((8, LANES), 0) * LANES + iota((8, LANES), 1)).astype(F32)
    spectrum_ref[...] = power / (2.0 * LEVELS * (degree + 1.0))


def in_hbm(x):
    return pltpu.with_memory_space_constraint(x, pltpu.HBM)


def exchange(x, axes):
    return lax.all_to_all(x, axes, split_axis=0, concat_axis=0, tiled=True)


def body(grid_fields, legendre, weights, kept_waves, slot_wavenumber, diffusion):
    forward_table, inverse_table = dft_tables()
    device = lax.axis_index(("y", "z", "x", "core")).astype(jnp.int32).reshape(1)
    chunk = (ZS, 4, YS * DATA + 2 * LANES)

    sent, order, column, kept, wave, diffusion = pl.pallas_call(
        fourier_kernel,
        in_specs=[SMEM, HBM, HBM, HBM, HBM, HBM, HBM],
        out_specs=[VMEM] * 6,
        out_shape=[
            jax.ShapeDtypeStruct((YS * LEVS, CHUNK, LANES), BF16),
            jax.ShapeDtypeStruct((1, HALF), jnp.int32),
            jax.ShapeDtypeStruct((LANES, 8), jnp.int32),
            jax.ShapeDtypeStruct((ROWS, 1), jnp.int32),
            jax.ShapeDtypeStruct((1, LANES), jnp.int32),
            jax.ShapeDtypeStruct((2 * LEVELS, 1), F32),
        ],
        scratch_shapes=[
            pltpu.SMEM((BAND,), jnp.int32),
            pltpu.SMEM((NLAT // 2,), F32),
            pltpu.SMEM((LEVELS,), F32),
            pltpu.VMEM((8, LANES), jnp.int32),
            pltpu.VMEM((BAND, LEV, NLON), BF16),
            pltpu.VMEM((STEPS, QUARTER, 2 * BLOCK), BF16),
            pltpu.VMEM((2, 2 * ROWS, QUARTER), BF16),
            pltpu.VMEM((4 * ROWS, QUARTER), BF16),
            pltpu.VMEM((4 * ROWS, HALF), BF16),
            pltpu.SemaphoreType.DMA((5 + STEPS,)),
        ],
        compiler_params=PARAMS,
        name="fourier",
    )(
        device,
        in_hbm(kept_waves),
        in_hbm(weights),
        in_hbm(diffusion),
        in_hbm(slot_wavenumber.reshape(8, LANES)),
        in_hbm(grid_fields.transpose(1, 0, 2)),
        in_hbm(jnp.asarray(forward_table)),
    )
    arrived = exchange(sent, ("y", "x", "core"))
    gathered = pl.pallas_call(
        gather_kernel,
        in_specs=[VMEM],
        out_specs=VMEM,
        out_shape=jax.ShapeDtypeStruct((ZS, 4, YS * DATA), BF16),
        scratch_shapes=[pltpu.VMEM((ZS, 4, YS * DATA), F32)],
        compiler_params=PARAMS,
        name="gather",
    )(arrived)
    gathered = exchange(gathered, ("z",))
    spectral, back = pl.pallas_call(
        legendre_kernel,
        in_specs=[VMEM, VMEM, VMEM, VMEM],
        out_specs=[HBM, VMEM],
        out_shape=[
            jax.ShapeDtypeStruct((2, 2, LEVELS, 2, HALF), F32),
            jax.ShapeDtypeStruct(chunk, BF16),
        ],
        scratch_shapes=[
            pltpu.VMEM((2, 2, LEVELS, 2, HALF), F32),
            pltpu.VMEM((2, NLAT // 2, LANES), F32),
            pltpu.SemaphoreType.DMA((4,)),
        ],
        compiler_params=PARAMS,
        name="legendre",
    )(wave, diffusion, gathered, legendre)
    back = exchange(back, ("z",))
    scattered = pl.pallas_call(
        scatter_kernel,
        in_specs=[VMEM],
        out_specs=VMEM,
        out_shape=jax.ShapeDtypeStruct((YS * LEVS, 8 + CHUNK, LANES), BF16),
        scratch_shapes=[pltpu.VMEM(chunk, F32)],
        compiler_params=PARAMS,
        name="scatter",
    )(back)
    returned = exchange(scattered, ("y", "x", "core"))
    grid_out, spectrum = pl.pallas_call(
        grid_kernel,
        in_specs=[SMEM, VMEM, VMEM, VMEM, VMEM, VMEM],
        out_specs=[VMEM, VMEM],
        out_shape=[
            jax.ShapeDtypeStruct((BAND, LEV, NLON), F32),
            jax.ShapeDtypeStruct((8, LANES), F32),
        ],
        compiler_params=PARAMS,
        name="grid",
    )(device, kept, order, column, returned, jnp.asarray(inverse_table))
    return (
        grid_out.transpose(1, 0, 2),
        spectral,
        spectrum.reshape(MM),
    )


def solution(mesh):
    fine = Mesh(mesh.devices.reshape(4, 16, 4, 2), ("y", "z", "x", "core"))
    lat, lev = ("y", "z"), ("x", "core")
    both = lat + lev
    in_specs = (P(lev, lat, None), P(both, None, None, None), P(), P(lat), P(), P())
    out_specs = (P(lev, lat, None), P(both, None, None, None, None), P())
    return jax.shard_map(body, mesh=fine, in_specs=in_specs, out_specs=out_specs, check_vma=False)
```

```python
import math

import jax
import jax.numpy as jnp
import ml_dtypes
import numpy as np
from jax import lax
from jax.experimental import pallas as pl
from jax.experimental.pallas import tpu as pltpu
from jax.sharding import Mesh
from jax.sharding import PartitionSpec as P

NLAT = 1280
NLON = 2688
MM = 1024
HALF = MM // 2
LEVELS = 32
BAND = 20
LEV = 4
ROWS = BAND * LEV
LATS = 64
LEVS = 8
YS = 4
ZS = 16
CHUNK = 2 * ROWS // YS
NORTH = LATS // 2
QUARTER = NLON // 4
STEPS = 4
BLOCK = MM // STEPS
TILES = BAND // 4
LANES = 128
DATA = TILES * LANES

BF16 = jnp.bfloat16
F32 = jnp.float32
VMEM = pl.BlockSpec(memory_space=pltpu.VMEM)
HBM = pl.BlockSpec(memory_space=pltpu.HBM)
SMEM = pl.BlockSpec(memory_space=pltpu.SMEM)
PARAMS = pltpu.CompilerParams(vmem_limit_bytes=20 * 1024 * 1024)


def dft_tables():
    sample = np.arange(QUARTER, dtype=np.int32)[:, None]
    number = np.arange(MM, dtype=np.int32)[None, :]
    angles = (sample * number % NLON).astype(np.float32) * np.float32(2.0 * math.pi / NLON)
    norm_scale = np.float32(1.0 / math.sqrt(NLON))
    cosine = (np.cos(angles) * norm_scale).astype(ml_dtypes.bfloat16)
    sine = (-np.sin(angles) * norm_scale).astype(ml_dtypes.bfloat16)
    rising = np.arange(LANES)
    places = np.concatenate([rising, BLOCK - 1 - rising])
    numbers = places[None, :] * STEPS + np.arange(STEPS)[:, None]
    forward = np.stack([cosine[:, numbers], sine[:, numbers]], axis=2)
    forward = np.ascontiguousarray(forward.transpose(1, 0, 2, 3)).reshape(STEPS, QUARTER, 2 * BLOCK)
    inverse = np.ascontiguousarray(forward.transpose(0, 2, 1))
    return forward, inverse


def iota(shape, dim):
    return lax.broadcasted_iota(jnp.int32, shape, dim)


def pair_number(shape, dim):
    place = iota(shape, dim)
    return place % LANES * STEPS + place // LANES


def slot_order(slots):
    digits = jnp.concatenate([slots // 32, slots % 32], axis=0).astype(F32).astype(BF16)
    source = iota((LANES, HALF), 0)
    to = iota((LANES, HALF), 1)
    choice = jnp.where(source == to // YS % 8 * 16 + to // LATS * 2, 1.0, 0.0).astype(BF16)
    moved = jnp.dot(digits, choice, preferred_element_type=F32)
    row = iota((16, HALF), 0)
    lane = iota((16, HALF), 1)
    mine = row % 8 == lane % YS * 2 + lane // 32 % 2
    value = jnp.where(mine, moved * jnp.where(row < 8, 32.0, 1.0), 0.0)
    return jnp.sum(value, axis=0, keepdims=True).astype(jnp.int32)


def latitude_column(scalars, zero):
    band = iota((ROWS, 1), 0) // LEV
    column = jnp.full((ROWS, 1), zero)
    for j in range(BAND):
        column = jnp.where(band == j, scalars[j], column)
    return column


def class_mask(kept, step):
    place = iota((ROWS, BLOCK), 1)
    place = jnp.where(place < LANES, place, BLOCK + LANES - 1 - place)
    return place * STEPS + step < kept


def lower_of_pair(wave):
    return jnp.minimum(wave, MM - 1 - wave)


def row_choice(southern):
    to = iota((2 * ROWS, 2 * ROWS), 0)
    source = iota((2 * ROWS, 2 * ROWS), 1)
    band = to % CHUNK // (2 * LEV) * YS + to // CHUNK
    band = jnp.where(southern, BAND - 1 - band, band)
    wanted = (to % 2) * ROWS + band * LEV + to // 2 % LEV
    return jnp.where(source == wanted, 1.0, 0.0).astype(BF16)


def swap_lanes(even, odd, width):
    high = iota(even.shape, 1) // width % 2 == 1
    return (
        jnp.where(high, pltpu.roll(odd, width, 1), even),
        jnp.where(high, odd, pltpu.roll(even, LANES - width, 1)),
    )


def sort_pair(order, first, second):
    flip = jnp.broadcast_to(order >= HALF, first.shape)
    return jnp.where(flip, second, first), jnp.where(flip, first, second)


def swap_parts(parts):
    parts = list(parts)
    parts[0], parts[1] = swap_lanes(parts[0], parts[1], 1)
    parts[2], parts[3] = swap_lanes(parts[2], parts[3], 1)
    parts[0], parts[2] = swap_lanes(parts[0], parts[2], 2)
    parts[1], parts[3] = swap_lanes(parts[1], parts[3], 2)
    return parts


def fourier_kernel(
    device_ref, kept_hbm, weights_hbm, diffusion_hbm, slots_hbm, x_hbm, table_hbm, o_ref, order_ref, column_ref,
    kept_ref, wave_ref, diffusion_ref, kept_s, weights_s, diffusion_s, slots_v, x_v,
    table_v, even, odd, both, sems
):
    small = [
        pltpu.make_async_copy(slots_hbm, slots_v, sems.at[0]),
        pltpu.make_async_copy(x_hbm, x_v, sems.at[1]),
        pltpu.make_async_copy(kept_hbm, kept_s, sems.at[2]),
        pltpu.make_async_copy(weights_hbm, weights_s, sems.at[3]),
        pltpu.make_async_copy(diffusion_hbm, diffusion_s, sems.at[4 + STEPS]),
    ]
    blocks = [pltpu.make_async_copy(table_hbm.at[i], table_v.at[i], sems.at[4 + i]) for i in range(STEPS)]
    for copy in small + blocks:
        copy.start()
    lat = device_ref[0] // LEVS
    small[0].wait()
    slots = slots_v[...]
    mine = iota((8, LANES), 0) * LANES + iota((8, LANES), 1) == device_ref[0] * 2
    mine = jnp.sum(jnp.where(mine, slots.astype(F32), 0.0), axis=0, keepdims=True)
    wave_ref[...] = jnp.broadcast_to(jnp.sum(mine, axis=1, keepdims=True).astype(jnp.int32), (1, LANES))
    order = slot_order(slots)
    order_ref[...] = order
    lower = lower_of_pair(order)
    columns = [lower[:, i * LANES : (i + 1) * LANES] for i in range(4)]
    column_ref[...] = jnp.concatenate(columns + columns, axis=0).T
    small[2].wait()
    small[3].wait()
    small[4].wait()
    level = iota((2 * LEVELS, 1), 0) // 2
    diffusion = jnp.zeros((2 * LEVELS, 1), F32)
    for i in range(LEVELS):
        diffusion = jnp.where(level == i, diffusion_s[i], diffusion)
    diffusion_ref[...] = diffusion
    kept = latitude_column([kept_s[j] for j in range(BAND)], jnp.int32(0))
    kept_ref[...] = kept
    latitudes = [lat * BAND + j for j in range(BAND)]
    weight = latitude_column([weights_s[jnp.minimum(i, NLAT - 1 - i)] for i in latitudes], F32(0.0))
    small[1].wait()

    def put(ref, place, value):
        high = value.astype(BF16)
        low = (value - high.astype(F32)).astype(BF16)
        for part, half in enumerate((high, low)):
            ref[pl.ds(place + part * ROWS, 16), :] = half

    for group in range(ROWS // 16):
        x = jnp.concatenate([x_v[4 * group + i].astype(F32) for i in range(4)], axis=0)
        x = [x[:, q * QUARTER : (q + 1) * QUARTER] for q in range(4)]
        sums = x[0] + x[2], x[1] + x[3]
        put(even.at[0], 16 * group, sums[0] + sums[1])
        put(even.at[1], 16 * group, sums[0] - sums[1])
        put(odd, 16 * group, x[0] - x[2])
        put(odd, 16 * group + 2 * ROWS, x[1] - x[3])
    for step in range(STEPS):
        blocks[step].wait()
        if step % 2 == 0:
            raw = jnp.dot(even[step // 2], table_v[step], preferred_element_type=F32)
            raw = raw[:ROWS] + raw[ROWS:]
            real, imaginary = raw[:, :BLOCK], raw[:, BLOCK:]
        else:
            raw = jnp.dot(odd[...], table_v[step], preferred_element_type=F32)
            first = raw[:ROWS] + raw[ROWS : 2 * ROWS]
            second = raw[2 * ROWS : 3 * ROWS] + raw[3 * ROWS :]
            if step == 3:
                second = -second
            real = first[:, :BLOCK] + second[:, BLOCK:]
            imaginary = first[:, BLOCK:] - second[:, :BLOCK]
        scale = jnp.where(class_mask(kept, step), weight, 0.0)
        fourier = jnp.concatenate([real * scale, imaginary * scale], axis=0).astype(BF16)
        both[: 2 * ROWS, step * LANES : (step + 1) * LANES] = fourier[:, :LANES]
        both[2 * ROWS :, (3 - step) * LANES : (4 - step) * LANES] = fourier[:, LANES:]
    choice = jnp.where(lower == pair_number((HALF, HALF), 0), 1.0, 0.0).astype(BF16)
    moved = jnp.dot(both[...], choice, preferred_element_type=F32)
    moved = sort_pair(order, moved[: 2 * ROWS], moved[2 * ROWS :])
    choice = row_choice(lat >= NORTH)
    moved = jnp.concatenate([half.astype(BF16) for half in moved], axis=1)
    moved = jnp.dot(choice, moved, preferred_element_type=F32)
    for i in range(LEVS // 2):
        place = i * LANES
        pair = swap_lanes(moved[:, place : place + LANES], moved[:, HALF + place : HALF + place + LANES], LATS)
        for b, block in zip((2 * i, 2 * i + 1), pair):
            parts = swap_parts([block[k * CHUNK : (k + 1) * CHUNK] for k in range(YS)])
            for y in range(YS):
                o_ref[y * LEVS + b] = parts[y].astype(BF16)


def gather_kernel(y_ref, o_ref):
    for y in range(YS):
        for j in range(TILES):
            block = [y_ref[y * LEVS + b, 8 * j : 8 * j + 8, :].astype(F32) for b in range(LEVS)]
            turned = jnp.concatenate(block, axis=0).astype(BF16).T.astype(F32)
            turned = jnp.concatenate([turned[:LATS], turned[LATS:]], axis=1)
            place = (y * TILES + j) * LANES
            o_ref[:, :, place : place + LANES] = turned.reshape(ZS, 4, LANES).astype(BF16)


def scatter_kernel(z_ref, o_ref):
    for y in range(YS):
        for j in range(TILES):
            place = (y * TILES + j) * LANES
            block = z_ref[:, :, place : place + LANES].astype(F32).reshape(LATS, LANES)
            turned = jnp.concatenate([block[:, :LATS], block[:, LATS:]], axis=0).astype(BF16).T.astype(F32)
            for b in range(LEVS):
                o_ref[y * LEVS + b, 8 + 8 * j : 16 + 8 * j, :] = turned[8 * b : 8 * b + 8].astype(BF16)
    power = jnp.sum(z_ref[:, :, YS * DATA :].astype(F32), axis=0)
    power = jnp.concatenate([power[:, :LANES], power[:, LANES:]], axis=0)
    for peer in range(YS * LEVS):
        o_ref[peer, :8, :] = power.astype(BF16)


def legendre_kernel(
    wave_ref, diffusion_ref, z_ref, table_ref, spectral_hbm, o_ref, spectral_v, comb, sems
):
    copies = []
    for group in range(NORTH * TILES // 4):
        north, south = [], []
        for u in range(4 * group, 4 * group + 4):
            a, tile = divmod(u, TILES)
            for side, lat in (north, a), (south, LATS - 1 - a):
                y, z = divmod(lat, ZS)
                place = (y * TILES + tile) * LANES
                side.append(z_ref[z, :, place : place + LANES].astype(F32))
        north = jnp.concatenate(north, axis=0)
        south = jnp.concatenate(south, axis=0)
        comb[0, 16 * group : 16 * group + 16, :] = north + south
        comb[1, 16 * group : 16 * group + 16, :] = north - south
    column = iota((2 * LEVELS, HALF), 1)
    diffusion = diffusion_ref[...]
    waves = [wave_ref[...], MM - 1 - wave_ref[...]]
    waves = [jnp.concatenate([wave] * (HALF // LANES), axis=1) for wave in waves]
    power = [jnp.zeros((1, HALF), F32), jnp.zeros((1, HALF), F32)]
    halves = []
    for q in range(2):
        left = comb[q].T.astype(BF16)
        parts = []
        for t in range(2):
            wave = waves[t]
            raw = jnp.dot(left[64 * t : 64 * t + 64], table_ref[t, q], preferred_element_type=F32)
            degree = wave + 2 * column + q
            spectral = jnp.where(degree < MM, raw, 0.0)
            for level in range(LEVELS):
                spectral_v[t, q, level] = spectral[2 * level : 2 * level + 2]
            copies.append(pltpu.make_async_copy(spectral_v.at[t, q], spectral_hbm.at[t, q], sems.at[2 * t + q]))
            copies[-1].start()
            degree = degree.astype(F32)
            ratio = degree * (degree + 1.0) / (MM * (MM + 1.0))
            damped = (spectral / (1.0 + diffusion * ratio * ratio)).astype(BF16)
            parts.append(
                lax.dot_general(
                    table_ref[t, q], damped, (((1,), (1,)), ((), ())), preferred_element_type=F32
                )
            )
            energy = jnp.sum(spectral * spectral, axis=0, keepdims=True)
            first = wave + q
            moved = jnp.broadcast_to(energy, (8, HALF))
            for bit in range(9):
                moved = jnp.where(first // 2**bit // 2 % 2 == 1, pltpu.roll(moved, 2**bit, 1), moved)
            moved = moved[:1]
            for odd in range(2):
                power[odd] += jnp.where(first % 2 == odd, moved, 0.0)
        halves.append(jnp.concatenate(parts, axis=1))
    source = iota((LANES, 2 * LANES), 0)
    to = iota((LANES, 2 * LANES), 1)
    natural = jnp.zeros((8, 2 * LANES), F32)
    for odd in range(2):
        quarters = [power[odd][:, i * LANES : (i + 1) * LANES] for i in range(4)]
        quarters = jnp.concatenate(quarters + quarters, axis=0).astype(BF16)
        choice = jnp.where(to == 2 * source + odd, 1.0, 0.0).astype(BF16)
        natural += jnp.dot(quarters, choice, preferred_element_type=F32)
    natural = natural[:4].astype(BF16)
    for z in range(ZS):
        o_ref[z, :, YS * DATA :] = natural
    for half, side in enumerate((halves[0] + halves[1], halves[0] - halves[1])):
        for u in range(NORTH * TILES):
            a, tile = divmod(u, TILES)
            y, z = divmod(LATS - 1 - a if half else a, ZS)
            place = (y * TILES + tile) * LANES
            o_ref[z, :, place : place + LANES] = side[4 * u : 4 * u + 4].astype(BF16)
    for copy in copies:
        copy.wait()


def grid_kernel(device_ref, kept_ref, order_ref, column_ref, y_ref, table_ref, o_ref, spectrum_ref):
    kept = kept_ref[...]
    choice = row_choice(device_ref[0] >= NORTH * LEVS)
    firsts, seconds = [], []
    for i in range(LEVS // 2):
        pair = []
        for b in (2 * i, 2 * i + 1):
            parts = swap_parts([y_ref[y * LEVS + b, 8:, :].astype(F32) for y in range(YS)])
            pair.append(jnp.concatenate(parts, axis=0))
        first, second = swap_lanes(pair[0], pair[1], LATS)
        firsts.append(first)
        seconds.append(second)
    back = sort_pair(order_ref[...], jnp.concatenate(firsts, axis=1), jnp.concatenate(seconds, axis=1))
    back = jnp.concatenate([half.astype(BF16) for half in back], axis=1)
    rows = lax.dot_general(choice, back, (((0,), (0,)), ((), ())), preferred_element_type=F32).astype(BF16)
    rows = jnp.concatenate([rows[:, :HALF], rows[:, HALF:]], axis=0)
    number = pair_number((LANES, HALF), 1)
    choice = [jnp.where(column_ref[:, i : i + 1] == number, 1.0, 0.0).astype(BF16) for i in range(HALF // LANES)]
    numbered = jnp.dot(rows, jnp.concatenate(choice, axis=0), preferred_element_type=F32)
    parts = []
    for step in range(STEPS):
        low = numbered[: 2 * ROWS, step * LANES : (step + 1) * LANES]
        high = numbered[2 * ROWS :, (3 - step) * LANES : (4 - step) * LANES]
        found = jnp.concatenate([low, high], axis=1)
        mask = class_mask(kept, step)
        real = jnp.where(mask, found[:ROWS], 0.0)
        imaginary = jnp.where(mask, found[ROWS:], 0.0)
        left = jnp.concatenate([real, imaginary], axis=1)
        if step == 1:
            left = jnp.concatenate([left, jnp.concatenate([-imaginary, real], axis=1)], axis=0)
        if step == 3:
            left = jnp.concatenate([left, jnp.concatenate([imaginary, -real], axis=1)], axis=0)
        parts.append(jnp.dot(left.astype(BF16), table_ref[step], preferred_element_type=F32))
    odd = parts[1] + parts[3]
    plus, minus = parts[0] + parts[2], parts[0] - parts[2]
    for group in range(ROWS // 16):
        place = slice(16 * group, 16 * group + 16)
        turned = slice(ROWS + 16 * group, ROWS + 16 * group + 16)
        quarters = [plus[place] + odd[place], minus[place] + odd[turned], plus[place] - odd[place], minus[place] - odd[turned]]
        points = jnp.concatenate(quarters, axis=1) * math.sqrt(NLON / MM)
        for i in range(4):
            o_ref[4 * group + i] = points[LEV * i : LEV * (i + 1)]
    power = jnp.zeros((8, LANES), F32)
    for peer in range(YS * LEVS):
        power += y_ref[peer, :8, :].astype(F32)
    power = jnp.concatenate([power[i // 2 + 4 * (i % 2)][None] for i in range(8)], axis=0)
    degree = (iota((8, LANES), 0) * LANES + iota((8, LANES), 1)).astype(F32)
    spectrum_ref[...] = power / (2.0 * LEVELS * (degree + 1.0))


def in_hbm(x):
    return pltpu.with_memory_space_constraint(x, pltpu.HBM)


def exchange(x, axes):
    return lax.all_to_all(x, axes, split_axis=0, concat_axis=0, tiled=True)


def body(grid_fields, legendre, weights, kept_waves, slot_wavenumber, diffusion):
    forward_table, inverse_table = dft_tables()
    device = lax.axis_index(("y", "z", "x", "core")).astype(jnp.int32).reshape(1)
    chunk = (ZS, 4, YS * DATA + 2 * LANES)

    sent, order, column, kept, wave, diffusion = pl.pallas_call(
        fourier_kernel,
        in_specs=[SMEM, HBM, HBM, HBM, HBM, HBM, HBM],
        out_specs=[VMEM] * 6,
        out_shape=[
            jax.ShapeDtypeStruct((YS * LEVS, CHUNK, LANES), BF16),
            jax.ShapeDtypeStruct((1, HALF), jnp.int32),
            jax.ShapeDtypeStruct((LANES, 8), jnp.int32),
            jax.ShapeDtypeStruct((ROWS, 1), jnp.int32),
            jax.ShapeDtypeStruct((1, LANES), jnp.int32),
            jax.ShapeDtypeStruct((2 * LEVELS, 1), F32),
        ],
        scratch_shapes=[
            pltpu.SMEM((BAND,), jnp.int32),
            pltpu.SMEM((NLAT // 2,), F32),
            pltpu.SMEM((LEVELS,), F32),
            pltpu.VMEM((8, LANES), jnp.int32),
            pltpu.VMEM((BAND, LEV, NLON), BF16),
            pltpu.VMEM((STEPS, QUARTER, 2 * BLOCK), BF16),
            pltpu.VMEM((2, 2 * ROWS, QUARTER), BF16),
            pltpu.VMEM((4 * ROWS, QUARTER), BF16),
            pltpu.VMEM((4 * ROWS, HALF), BF16),
            pltpu.SemaphoreType.DMA((5 + STEPS,)),
        ],
        compiler_params=PARAMS,
        name="fourier",
    )(
        device,
        in_hbm(kept_waves),
        in_hbm(weights),
        in_hbm(diffusion),
        in_hbm(slot_wavenumber.reshape(8, LANES)),
        in_hbm(grid_fields.transpose(1, 0, 2)),
        in_hbm(jnp.asarray(forward_table)),
    )
    arrived = exchange(sent, ("y", "x", "core"))
    gathered = pl.pallas_call(
        gather_kernel,
        in_specs=[VMEM],
        out_specs=VMEM,
        out_shape=jax.ShapeDtypeStruct((ZS, 4, YS * DATA), BF16),
        compiler_params=PARAMS,
        name="gather",
    )(arrived)
    gathered = exchange(gathered, ("z",))
    spectral, back = pl.pallas_call(
        legendre_kernel,
        in_specs=[VMEM, VMEM, VMEM, VMEM],
        out_specs=[HBM, VMEM],
        out_shape=[
            jax.ShapeDtypeStruct((2, 2, LEVELS, 2, HALF), F32),
            jax.ShapeDtypeStruct(chunk, BF16),
        ],
        scratch_shapes=[
            pltpu.VMEM((2, 2, LEVELS, 2, HALF), F32),
            pltpu.VMEM((2, NLAT // 2, LANES), F32),
            pltpu.SemaphoreType.DMA((4,)),
        ],
        compiler_params=PARAMS,
        name="legendre",
    )(wave, diffusion, gathered, legendre)
    back = exchange(back, ("z",))
    scattered = pl.pallas_call(
        scatter_kernel,
        in_specs=[VMEM],
        out_specs=VMEM,
        out_shape=jax.ShapeDtypeStruct((YS * LEVS, 8 + CHUNK, LANES), BF16),
        compiler_params=PARAMS,
        name="scatter",
    )(back)
    returned = exchange(scattered, ("y", "x", "core"))
    grid_out, spectrum = pl.pallas_call(
        grid_kernel,
        in_specs=[SMEM, VMEM, VMEM, VMEM, VMEM, VMEM],
        out_specs=[VMEM, VMEM],
        out_shape=[
            jax.ShapeDtypeStruct((BAND, LEV, NLON), F32),
            jax.ShapeDtypeStruct((8, LANES), F32),
        ],
        compiler_params=PARAMS,
        name="grid",
    )(device, kept, order, column, returned, jnp.asarray(inverse_table))
    return (
        grid_out.transpose(1, 0, 2),
        spectral,
        spectrum.reshape(MM),
    )


def solution(mesh):
    fine = Mesh(mesh.devices.reshape(4, 16, 4, 2), ("y", "z", "x", "core"))
    lat, lev = ("y", "z"), ("x", "core")
    both = lat + lev
    in_specs = (P(lev, lat, None), P(both, None, None, None), P(), P(lat), P(), P())
    out_specs = (P(lev, lat, None), P(both, None, None, None, None), P())
    return jax.shard_map(body, mesh=fine, in_specs=in_specs, out_specs=out_specs, check_vma=False)
```

```python
import math

import jax
import jax.numpy as jnp
import ml_dtypes
import numpy as np
from jax import lax
from jax.experimental import pallas as pl
from jax.experimental.pallas import tpu as pltpu
from jax.sharding import Mesh
from jax.sharding import PartitionSpec as P

NLAT = 1280
NLON = 2688
MM = 1024
HALF = MM // 2
LEVELS = 32
BAND = 20
LEV = 4
ROWS = BAND * LEV
LATS = 64
LEVS = 8
YS = 4
ZS = 16
CHUNK = 2 * ROWS // YS
NORTH = LATS // 2
QUARTER = NLON // 4
STEPS = 4
BLOCK = MM // STEPS
TILES = BAND // 4
LANES = 128
DATA = TILES * LANES

BF16 = jnp.bfloat16
F32 = jnp.float32
VMEM = pl.BlockSpec(memory_space=pltpu.VMEM)
HBM = pl.BlockSpec(memory_space=pltpu.HBM)
SMEM = pl.BlockSpec(memory_space=pltpu.SMEM)
PARAMS = pltpu.CompilerParams(vmem_limit_bytes=20 * 1024 * 1024)


def dft_tables():
    sample = np.arange(QUARTER, dtype=np.int32)[:, None]
    number = np.arange(MM, dtype=np.int32)[None, :]
    angles = (sample * number % NLON).astype(np.float32) * np.float32(2.0 * math.pi / NLON)
    norm_scale = np.float32(1.0 / math.sqrt(NLON))
    cosine = (np.cos(angles) * norm_scale).astype(ml_dtypes.bfloat16)
    sine = (-np.sin(angles) * norm_scale).astype(ml_dtypes.bfloat16)
    rising = np.arange(LANES)
    places = np.concatenate([rising, BLOCK - 1 - rising])
    numbers = places[None, :] * STEPS + np.arange(STEPS)[:, None]
    forward = np.stack([cosine[:, numbers], sine[:, numbers]], axis=2)
    forward = np.ascontiguousarray(forward.transpose(1, 0, 2, 3)).reshape(STEPS, QUARTER, 2 * BLOCK)
    inverse = np.ascontiguousarray(forward.transpose(0, 2, 1))
    return forward, inverse


def iota(shape, dim):
    return lax.broadcasted_iota(jnp.int32, shape, dim)


def pair_number(shape, dim):
    place = iota(shape, dim)
    return place % LANES * STEPS + place // LANES


def slot_moves():
    source = iota((LANES, HALF), 0)
    to = iota((LANES, HALF), 1)
    choice = jnp.where(source == to // YS % 8 * 16 + to // LATS * 2, 1.0, 0.0).astype(BF16)
    row = iota((16, HALF), 0)
    lane = iota((16, HALF), 1)
    mine = row % 8 == lane % YS * 2 + lane // 32 % 2
    return choice, jnp.where(mine, jnp.where(row < 8, 32.0, 1.0), 0.0)


def slot_order(slots, choice, digit):
    digits = jnp.concatenate([slots // 32, slots % 32], axis=0).astype(F32).astype(BF16)
    moved = jnp.dot(digits, choice, preferred_element_type=F32)
    return jnp.sum(moved * digit, axis=0, keepdims=True).astype(jnp.int32)


def latitude_column(scalars, zero):
    band = iota((ROWS, 1), 0) // LEV
    column = jnp.full((ROWS, 1), zero)
    for j in range(BAND):
        column = jnp.where(band == j, scalars[j], column)
    return column


def class_mask(kept, step):
    place = iota((ROWS, BLOCK), 1)
    place = jnp.where(place < LANES, place, BLOCK + LANES - 1 - place)
    return place * STEPS + step < kept


def lower_of_pair(wave):
    return jnp.minimum(wave, MM - 1 - wave)


def row_choice(southern, side):
    to = iota((2 * ROWS, 2 * ROWS), side)
    source = iota((2 * ROWS, 2 * ROWS), 1 - side)
    band = to % CHUNK // (2 * LEV) * YS + to // CHUNK
    band = jnp.where(southern, BAND - 1 - band, band)
    wanted = (to % 2) * ROWS + band * LEV + to // 2 % LEV
    return jnp.where(source == wanted, 1.0, 0.0).astype(BF16)


def swap_lanes(even, odd, width):
    high = iota(even.shape, 1) // width % 2 == 1
    return (
        jnp.where(high, pltpu.roll(odd, width, 1), even),
        jnp.where(high, odd, pltpu.roll(even, LANES - width, 1)),
    )


def sort_pair(order, first, second):
    flip = jnp.broadcast_to(order >= HALF, first.shape)
    return jnp.where(flip, second, first), jnp.where(flip, first, second)


def swap_parts(parts):
    parts = list(parts)
    parts[0], parts[1] = swap_lanes(parts[0], parts[1], 1)
    parts[2], parts[3] = swap_lanes(parts[2], parts[3], 1)
    parts[0], parts[2] = swap_lanes(parts[0], parts[2], 2)
    parts[1], parts[3] = swap_lanes(parts[1], parts[3], 2)
    return parts


def fourier_kernel(
    device_ref, kept_hbm, weights_hbm, diffusion_hbm, slots_hbm, x_hbm, table_hbm, o_ref, order_ref, column_ref,
    kept_ref, wave_ref, diffusion_ref, kept_s, weights_s, diffusion_s, slots_v, x_v,
    table_v, even, odd, both, row_moves, moves, digit, sems
):
    small = [
        pltpu.make_async_copy(slots_hbm, slots_v, sems.at[0]),
        pltpu.make_async_copy(x_hbm, x_v, sems.at[1]),
        pltpu.make_async_copy(kept_hbm, kept_s, sems.at[2]),
        pltpu.make_async_copy(weights_hbm, weights_s, sems.at[3]),
        pltpu.make_async_copy(diffusion_hbm, diffusion_s, sems.at[4 + STEPS]),
    ]
    blocks = [pltpu.make_async_copy(table_hbm.at[i], table_v.at[i], sems.at[4 + i]) for i in range(STEPS)]
    for copy in small + blocks:
        copy.start()
    lat = device_ref[0] // LEVS
    row_moves[...] = row_choice(lat >= NORTH, 0)
    moves[...], digit[...] = slot_moves()
    small[1].wait()

    def put(ref, place, value):
        high = value.astype(BF16)
        low = (value - high.astype(F32)).astype(BF16)
        for part, half in enumerate((high, low)):
            ref[pl.ds(place + part * ROWS, 16), :] = half

    for group in range(ROWS // 16):
        x = jnp.concatenate([x_v[4 * group + i].astype(F32) for i in range(4)], axis=0)
        x = [x[:, q * QUARTER : (q + 1) * QUARTER] for q in range(4)]
        sums = x[0] + x[2], x[1] + x[3]
        put(even.at[0], 16 * group, sums[0] + sums[1])
        put(even.at[1], 16 * group, sums[0] - sums[1])
        put(odd, 16 * group, x[0] - x[2])
        put(odd, 16 * group + 2 * ROWS, x[1] - x[3])
    for copy in small[:1] + small[2:] + blocks:
        copy.wait()
    kept = latitude_column([kept_s[j] for j in range(BAND)], jnp.int32(0))
    kept_ref[...] = kept
    latitudes = [lat * BAND + j for j in range(BAND)]
    weight = latitude_column([weights_s[jnp.minimum(i, NLAT - 1 - i)] for i in latitudes], F32(0.0))
    for step in range(STEPS):
        if step % 2 == 0:
            raw = jnp.dot(even[step // 2], table_v[step], preferred_element_type=F32)
            raw = raw[:ROWS] + raw[ROWS:]
            real, imaginary = raw[:, :BLOCK], raw[:, BLOCK:]
        else:
            raw = jnp.dot(odd[...], table_v[step], preferred_element_type=F32)
            first = raw[:ROWS] + raw[ROWS : 2 * ROWS]
            second = raw[2 * ROWS : 3 * ROWS] + raw[3 * ROWS :]
            if step == 3:
                second = -second
            real = first[:, :BLOCK] + second[:, BLOCK:]
            imaginary = first[:, BLOCK:] - second[:, :BLOCK]
        scale = jnp.where(class_mask(kept, step), weight, 0.0)
        fourier = jnp.concatenate([real * scale, imaginary * scale], axis=0).astype(BF16)
        both[: 2 * ROWS, step * LANES : (step + 1) * LANES] = fourier[:, :LANES]
        both[2 * ROWS :, (3 - step) * LANES : (4 - step) * LANES] = fourier[:, LANES:]
    level = iota((2 * LEVELS, 1), 0) // 2
    diffusion = jnp.zeros((2 * LEVELS, 1), F32)
    for i in range(LEVELS):
        diffusion = jnp.where(level == i, diffusion_s[i], diffusion)
    diffusion_ref[...] = diffusion
    slots = slots_v[...]
    mine = iota((8, LANES), 0) * LANES + iota((8, LANES), 1) == device_ref[0] * 2
    mine = jnp.sum(jnp.where(mine, slots.astype(F32), 0.0), axis=0, keepdims=True)
    wave_ref[...] = jnp.broadcast_to(jnp.sum(mine, axis=1, keepdims=True).astype(jnp.int32), (1, LANES))
    order = slot_order(slots, moves[...], digit[...])
    order_ref[...] = order
    lower = lower_of_pair(order)
    columns = [lower[:, i * LANES : (i + 1) * LANES] for i in range(4)]
    column_ref[...] = jnp.concatenate(columns + columns, axis=0).T
    choice = jnp.where(lower == pair_number((HALF, HALF), 0), 1.0, 0.0).astype(BF16)
    moved = jnp.dot(both[...], choice, preferred_element_type=F32)
    moved = sort_pair(order, moved[: 2 * ROWS], moved[2 * ROWS :])
    moved = jnp.concatenate([half.astype(BF16) for half in moved], axis=1)
    moved = jnp.dot(row_moves[...], moved, preferred_element_type=F32)
    for i in range(LEVS // 2):
        place = i * LANES
        pair = swap_lanes(moved[:, place : place + LANES], moved[:, HALF + place : HALF + place + LANES], LATS)
        for b, block in zip((2 * i, 2 * i + 1), pair):
            parts = swap_parts([block[k * CHUNK : (k + 1) * CHUNK] for k in range(YS)])
            for y in range(YS):
                o_ref[y * LEVS + b] = parts[y].astype(BF16)


def gather_kernel(y_ref, o_ref):
    for y in range(YS):
        for j in range(TILES):
            block = [y_ref[y * LEVS + b, 8 * j : 8 * j + 8, :].astype(F32) for b in range(LEVS)]
            turned = jnp.concatenate(block, axis=0).astype(BF16).T.astype(F32)
            turned = jnp.concatenate([turned[:LATS], turned[LATS:]], axis=1)
            place = (y * TILES + j) * LANES
            o_ref[:, :, place : place + LANES] = turned.reshape(ZS, 4, LANES).astype(BF16)


def scatter_kernel(z_ref, o_ref):
    for y in range(YS):
        for j in range(TILES):
            place = (y * TILES + j) * LANES
            block = z_ref[:, :, place : place + LANES].astype(F32).reshape(LATS, LANES)
            turned = jnp.concatenate([block[:, :LATS], block[:, LATS:]], axis=0).T
            for b in range(LEVS):
                o_ref[y * LEVS + b, 8 + 8 * j : 16 + 8 * j, :] = turned[8 * b : 8 * b + 8].astype(BF16)
    power = jnp.sum(z_ref[:, :, YS * DATA :].astype(F32), axis=0)
    power = jnp.concatenate([power[:, :LANES], power[:, LANES:]], axis=0)
    for peer in range(YS * LEVS):
        o_ref[peer, :8, :] = power.astype(BF16)


def legendre_kernel(
    wave_ref, diffusion_ref, z_ref, table_ref, spectral_hbm, o_ref, spectral_v, comb, sems
):
    copies = []
    for group in range(NORTH * TILES // 4):
        north, south = [], []
        for u in range(4 * group, 4 * group + 4):
            a, tile = divmod(u, TILES)
            for side, lat in (north, a), (south, LATS - 1 - a):
                y, z = divmod(lat, ZS)
                place = (y * TILES + tile) * LANES
                side.append(z_ref[z, :, place : place + LANES].astype(F32))
        north = jnp.concatenate(north, axis=0)
        south = jnp.concatenate(south, axis=0)
        comb[0, 16 * group : 16 * group + 16, :] = north + south
        comb[1, 16 * group : 16 * group + 16, :] = north - south
    column = iota((2 * LEVELS, HALF), 1)
    diffusion = diffusion_ref[...]
    waves = [wave_ref[...], MM - 1 - wave_ref[...]]
    waves = [jnp.concatenate([wave] * (HALF // LANES), axis=1) for wave in waves]
    power = [jnp.zeros((1, HALF), F32), jnp.zeros((1, HALF), F32)]
    halves = []
    for q in range(2):
        left = comb[q].astype(BF16).T
        parts = []
        for t in range(2):
            wave = waves[t]
            raw = jnp.dot(left[64 * t : 64 * t + 64], table_ref[t, q], preferred_element_type=F32)
            degree = wave + 2 * column + q
            spectral = jnp.where(degree < MM, raw, 0.0)
            for level in range(LEVELS):
                spectral_v[t, q, level] = spectral[2 * level : 2 * level + 2]
            copies.append(pltpu.make_async_copy(spectral_v.at[t, q], spectral_hbm.at[t, q], sems.at[2 * t + q]))
            copies[-1].start()
            degree = degree.astype(F32)
            ratio = degree * (degree + 1.0) / (MM * (MM + 1.0))
            damped = (spectral / (1.0 + diffusion * ratio * ratio)).astype(BF16)
            parts.append(
                lax.dot_general(
                    table_ref[t, q], damped, (((1,), (1,)), ((), ())), preferred_element_type=F32
                )
            )
            energy = jnp.sum(spectral * spectral, axis=0, keepdims=True)
            first = wave + q
            moved = jnp.broadcast_to(energy, (8, HALF))
            for bit in range(9):
                moved = jnp.where(first // 2**bit // 2 % 2 == 1, pltpu.roll(moved, 2**bit, 1), moved)
            moved = moved[:1]
            for odd in range(2):
                power[odd] += jnp.where(first % 2 == odd, moved, 0.0)
        halves.append(jnp.concatenate(parts, axis=1))
    source = iota((LANES, 2 * LANES), 0)
    to = iota((LANES, 2 * LANES), 1)
    natural = jnp.zeros((8, 2 * LANES), F32)
    for odd in range(2):
        quarters = [power[odd][:, i * LANES : (i + 1) * LANES] for i in range(4)]
        quarters = jnp.concatenate(quarters + quarters, axis=0).astype(BF16)
        choice = jnp.where(to == 2 * source + odd, 1.0, 0.0).astype(BF16)
        natural += jnp.dot(quarters, choice, preferred_element_type=F32)
    natural = natural[:4].astype(BF16)
    for z in range(ZS):
        o_ref[z, :, YS * DATA :] = natural
    for half, side in enumerate((halves[0] + halves[1], halves[0] - halves[1])):
        for u in range(NORTH * TILES):
            a, tile = divmod(u, TILES)
            y, z = divmod(LATS - 1 - a if half else a, ZS)
            place = (y * TILES + tile) * LANES
            o_ref[z, :, place : place + LANES] = side[4 * u : 4 * u + 4].astype(BF16)
    for copy in copies:
        copy.wait()


def grid_kernel(device_ref, kept_ref, order_ref, column_ref, y_ref, table_ref, o_ref, spectrum_ref):
    kept = kept_ref[...]
    choice = row_choice(device_ref[0] >= NORTH * LEVS, 1)
    firsts, seconds = [], []
    for i in range(LEVS // 2):
        pair = []
        for b in (2 * i, 2 * i + 1):
            parts = swap_parts([y_ref[y * LEVS + b, 8:, :].astype(F32) for y in range(YS)])
            pair.append(jnp.concatenate(parts, axis=0))
        first, second = swap_lanes(pair[0], pair[1], LATS)
        firsts.append(first)
        seconds.append(second)
    back = sort_pair(order_ref[...], jnp.concatenate(firsts, axis=1), jnp.concatenate(seconds, axis=1))
    back = jnp.concatenate([half.astype(BF16) for half in back], axis=1)
    rows = jnp.dot(choice, back, preferred_element_type=F32).astype(BF16)
    rows = jnp.concatenate([rows[:, :HALF], rows[:, HALF:]], axis=0)
    number = pair_number((LANES, HALF), 1)
    choice = [jnp.where(column_ref[:, i : i + 1] == number, 1.0, 0.0).astype(BF16) for i in range(HALF // LANES)]
    numbered = jnp.dot(rows, jnp.concatenate(choice, axis=0), preferred_element_type=F32)
    parts = []
    for step in range(STEPS):
        low = numbered[: 2 * ROWS, step * LANES : (step + 1) * LANES]
        high = numbered[2 * ROWS :, (3 - step) * LANES : (4 - step) * LANES]
        found = jnp.concatenate([low, high], axis=1)
        mask = class_mask(kept, step)
        real = jnp.where(mask, found[:ROWS], 0.0)
        imaginary = jnp.where(mask, found[ROWS:], 0.0)
        left = jnp.concatenate([real, imaginary], axis=1)
        if step == 1:
            left = jnp.concatenate([left, jnp.concatenate([-imaginary, real], axis=1)], axis=0)
        if step == 3:
            left = jnp.concatenate([left, jnp.concatenate([imaginary, -real], axis=1)], axis=0)
        parts.append(jnp.dot(left.astype(BF16), table_ref[step], preferred_element_type=F32))
    odd = parts[1] + parts[3]
    plus, minus = parts[0] + parts[2], parts[0] - parts[2]
    for group in range(ROWS // 16):
        place = slice(16 * group, 16 * group + 16)
        turned = slice(ROWS + 16 * group, ROWS + 16 * group + 16)
        quarters = [plus[place] + odd[place], minus[place] + odd[turned], plus[place] - odd[place], minus[place] - odd[turned]]
        points = jnp.concatenate(quarters, axis=1) * math.sqrt(NLON / MM)
        for i in range(4):
            o_ref[4 * group + i] = points[LEV * i : LEV * (i + 1)]
    power = jnp.zeros((8, LANES), F32)
    for peer in range(YS * LEVS):
        power += y_ref[peer, :8, :].astype(F32)
    power = jnp.concatenate([power[i // 2 + 4 * (i % 2)][None] for i in range(8)], axis=0)
    degree = (iota((8, LANES), 0) * LANES + iota((8, LANES), 1)).astype(F32)
    spectrum_ref[...] = power / (2.0 * LEVELS * (degree + 1.0))


def in_hbm(x):
    return pltpu.with_memory_space_constraint(x, pltpu.HBM)


def exchange(x, axes):
    return lax.all_to_all(x, axes, split_axis=0, concat_axis=0, tiled=True)


def body(grid_fields, legendre, weights, kept_waves, slot_wavenumber, diffusion):
    forward_table, inverse_table = dft_tables()
    device = lax.axis_index(("y", "z", "x", "core")).astype(jnp.int32).reshape(1)
    chunk = (ZS, 4, YS * DATA + 2 * LANES)

    sent, order, column, kept, wave, diffusion = pl.pallas_call(
        fourier_kernel,
        in_specs=[SMEM, HBM, HBM, HBM, HBM, HBM, HBM],
        out_specs=[VMEM] * 6,
        out_shape=[
            jax.ShapeDtypeStruct((YS * LEVS, CHUNK, LANES), BF16),
            jax.ShapeDtypeStruct((1, HALF), jnp.int32),
            jax.ShapeDtypeStruct((LANES, 8), jnp.int32),
            jax.ShapeDtypeStruct((ROWS, 1), jnp.int32),
            jax.ShapeDtypeStruct((1, LANES), jnp.int32),
            jax.ShapeDtypeStruct((2 * LEVELS, 1), F32),
        ],
        scratch_shapes=[
            pltpu.SMEM((BAND,), jnp.int32),
            pltpu.SMEM((NLAT // 2,), F32),
            pltpu.SMEM((LEVELS,), F32),
            pltpu.VMEM((8, LANES), jnp.int32),
            pltpu.VMEM((BAND, LEV, NLON), BF16),
            pltpu.VMEM((STEPS, QUARTER, 2 * BLOCK), BF16),
            pltpu.VMEM((2, 2 * ROWS, QUARTER), BF16),
            pltpu.VMEM((4 * ROWS, QUARTER), BF16),
            pltpu.VMEM((4 * ROWS, HALF), BF16),
            pltpu.VMEM((2 * ROWS, 2 * ROWS), BF16),
            pltpu.VMEM((LANES, HALF), BF16),
            pltpu.VMEM((16, HALF), F32),
            pltpu.SemaphoreType.DMA((5 + STEPS,)),
        ],
        compiler_params=PARAMS,
        name="fourier",
    )(
        device,
        in_hbm(kept_waves),
        in_hbm(weights),
        in_hbm(diffusion),
        in_hbm(slot_wavenumber.reshape(8, LANES)),
        in_hbm(grid_fields.transpose(1, 0, 2)),
        in_hbm(jnp.asarray(forward_table)),
    )
    arrived = exchange(sent, ("y", "x", "core"))
    gathered = pl.pallas_call(
        gather_kernel,
        in_specs=[VMEM],
        out_specs=VMEM,
        out_shape=jax.ShapeDtypeStruct((ZS, 4, YS * DATA), BF16),
        compiler_params=PARAMS,
        name="gather",
    )(arrived)
    gathered = exchange(gathered, ("z",))
    spectral, back = pl.pallas_call(
        legendre_kernel,
        in_specs=[VMEM, VMEM, VMEM, VMEM],
        out_specs=[HBM, VMEM],
        out_shape=[
            jax.ShapeDtypeStruct((2, 2, LEVELS, 2, HALF), F32),
            jax.ShapeDtypeStruct(chunk, BF16),
        ],
        scratch_shapes=[
            pltpu.VMEM((2, 2, LEVELS, 2, HALF), F32),
            pltpu.VMEM((2, NLAT // 2, LANES), F32),
            pltpu.SemaphoreType.DMA((4,)),
        ],
        compiler_params=PARAMS,
        name="legendre",
    )(wave, diffusion, gathered, legendre)
    back = exchange(back, ("z",))
    scattered = pl.pallas_call(
        scatter_kernel,
        in_specs=[VMEM],
        out_specs=VMEM,
        out_shape=jax.ShapeDtypeStruct((YS * LEVS, 8 + CHUNK, LANES), BF16),
        compiler_params=PARAMS,
        name="scatter",
    )(back)
    returned = exchange(scattered, ("y", "x", "core"))
    grid_out, spectrum = pl.pallas_call(
        grid_kernel,
        in_specs=[SMEM, VMEM, VMEM, VMEM, VMEM, VMEM],
        out_specs=[VMEM, VMEM],
        out_shape=[
            jax.ShapeDtypeStruct((BAND, LEV, NLON), F32),
            jax.ShapeDtypeStruct((8, LANES), F32),
        ],
        compiler_params=PARAMS,
        name="grid",
    )(device, kept, order, column, returned, jnp.asarray(inverse_table))
    return (
        grid_out.transpose(1, 0, 2),
        spectral,
        spectrum.reshape(MM),
    )


def solution(mesh):
    fine = Mesh(mesh.devices.reshape(4, 16, 4, 2), ("y", "z", "x", "core"))
    lat, lev = ("y", "z"), ("x", "core")
    both = lat + lev
    in_specs = (P(lev, lat, None), P(both, None, None, None), P(), P(lat), P(), P())
    out_specs = (P(lev, lat, None), P(both, None, None, None, None), P())
    return jax.shard_map(body, mesh=fine, in_specs=in_specs, out_specs=out_specs, check_vma=False)
```

```python
import math

import jax
import jax.numpy as jnp
import ml_dtypes
import numpy as np
from jax import lax
from jax.experimental import pallas as pl
from jax.experimental.pallas import tpu as pltpu
from jax.sharding import Mesh
from jax.sharding import PartitionSpec as P

NLAT = 1280
NLON = 2688
MM = 1024
HALF = MM // 2
LEVELS = 32
BAND = 20
LEV = 4
ROWS = BAND * LEV
LATS = 64
LEVS = 8
YS = 4
ZS = 16
CHUNK = 2 * ROWS // YS
NORTH = LATS // 2
QUARTER = NLON // 4
STEPS = 4
BLOCK = MM // STEPS
TILES = BAND // 4
LANES = 128
DATA = TILES * LANES

BF16 = jnp.bfloat16
F32 = jnp.float32
VMEM = pl.BlockSpec(memory_space=pltpu.VMEM)
HBM = pl.BlockSpec(memory_space=pltpu.HBM)
SMEM = pl.BlockSpec(memory_space=pltpu.SMEM)
PARAMS = pltpu.CompilerParams(vmem_limit_bytes=20 * 1024 * 1024)


def dft_tables():
    sample = np.arange(QUARTER, dtype=np.int32)[:, None]
    number = np.arange(MM, dtype=np.int32)[None, :]
    angles = (sample * number % NLON).astype(np.float32) * np.float32(2.0 * math.pi / NLON)
    norm_scale = np.float32(1.0 / math.sqrt(NLON))
    cosine = (np.cos(angles) * norm_scale).astype(ml_dtypes.bfloat16)
    sine = (-np.sin(angles) * norm_scale).astype(ml_dtypes.bfloat16)
    rising = np.arange(LANES)
    places = np.concatenate([rising, BLOCK - 1 - rising])
    numbers = places[None, :] * STEPS + np.arange(STEPS)[:, None]
    forward = np.stack([cosine[:, numbers], sine[:, numbers]], axis=2)
    forward = np.ascontiguousarray(forward.transpose(1, 0, 2, 3)).reshape(STEPS, QUARTER, 2 * BLOCK)
    inverse = np.ascontiguousarray(forward.transpose(0, 2, 1)[[0, 2, 1, 3]])
    return forward, inverse


def iota(shape, dim):
    return lax.broadcasted_iota(jnp.int32, shape, dim)


def pair_number(shape, dim):
    place = iota(shape, dim)
    return place % LANES * STEPS + place // LANES


def slot_moves():
    source = iota((LANES, HALF), 0)
    to = iota((LANES, HALF), 1)
    choice = jnp.where(source == to // YS % 8 * 16 + to // LATS * 2, 1.0, 0.0).astype(BF16)
    row = iota((16, HALF), 0)
    lane = iota((16, HALF), 1)
    mine = row % 8 == lane % YS * 2 + lane // 32 % 2
    return choice, jnp.where(mine, jnp.where(row < 8, 32.0, 1.0), 0.0)


def slot_order(slots, choice, digit):
    digits = jnp.concatenate([slots // 32, slots % 32], axis=0).astype(F32).astype(BF16)
    moved = jnp.dot(digits, choice, preferred_element_type=F32)
    return jnp.sum(moved * digit, axis=0, keepdims=True).astype(jnp.int32)


def latitude_column(scalars, zero):
    band = iota((ROWS, 1), 0) // LEV
    column = jnp.full((ROWS, 1), zero)
    for j in range(BAND):
        column = jnp.where(band == j, scalars[j], column)
    return column


def class_mask(kept, step):
    place = iota((ROWS, BLOCK), 1)
    place = jnp.where(place < LANES, place, BLOCK + LANES - 1 - place)
    return place * STEPS + step < kept


def lower_of_pair(wave):
    return jnp.minimum(wave, MM - 1 - wave)


def row_choice(southern, side):
    to = iota((2 * ROWS, 2 * ROWS), side)
    source = iota((2 * ROWS, 2 * ROWS), 1 - side)
    band = to % CHUNK // (2 * LEV) * YS + to // CHUNK
    band = jnp.where(southern, BAND - 1 - band, band)
    wanted = (to % 2) * ROWS + band * LEV + to // 2 % LEV
    return jnp.where(source == wanted, 1.0, 0.0).astype(BF16)


def swap_lanes(even, odd, width):
    high = iota(even.shape, 1) // width % 2 == 1
    return (
        jnp.where(high, pltpu.roll(odd, width, 1), even),
        jnp.where(high, odd, pltpu.roll(even, LANES - width, 1)),
    )


def sort_pair(order, first, second):
    flip = jnp.broadcast_to(order >= HALF, first.shape)
    return jnp.where(flip, second, first), jnp.where(flip, first, second)


def swap_parts(parts):
    parts = list(parts)
    parts[0], parts[1] = swap_lanes(parts[0], parts[1], 1)
    parts[2], parts[3] = swap_lanes(parts[2], parts[3], 1)
    parts[0], parts[2] = swap_lanes(parts[0], parts[2], 2)
    parts[1], parts[3] = swap_lanes(parts[1], parts[3], 2)
    return parts


def fourier_kernel(
    device_ref, kept_hbm, weights_hbm, diffusion_hbm, slots_hbm, x_hbm, table_hbm, o_ref, order_ref, column_ref,
    kept_ref, wave_ref, diffusion_ref, kept_s, weights_s, diffusion_s, slots_v, x_v,
    table_v, even, odd, both, row_moves, moves, digit, sems
):
    small = [
        pltpu.make_async_copy(slots_hbm, slots_v, sems.at[0]),
        pltpu.make_async_copy(x_hbm, x_v, sems.at[1]),
        pltpu.make_async_copy(kept_hbm, kept_s, sems.at[2]),
        pltpu.make_async_copy(weights_hbm, weights_s, sems.at[3]),
        pltpu.make_async_copy(diffusion_hbm, diffusion_s, sems.at[4 + STEPS]),
    ]
    blocks = [pltpu.make_async_copy(table_hbm.at[i], table_v.at[i], sems.at[4 + i]) for i in range(STEPS)]
    for copy in small + blocks:
        copy.start()
    lat = device_ref[0] // LEVS
    row_moves[...] = row_choice(lat >= NORTH, 0)
    moves[...], digit[...] = slot_moves()
    small[1].wait()

    def put(ref, place, value):
        high = value.astype(BF16)
        low = (value - high.astype(F32)).astype(BF16)
        for part, half in enumerate((high, low)):
            ref[pl.ds(place + part * ROWS, 16), :] = half

    for group in range(ROWS // 16):
        x = jnp.concatenate([x_v[4 * group + i].astype(F32) for i in range(4)], axis=0)
        x = [x[:, q * QUARTER : (q + 1) * QUARTER] for q in range(4)]
        sums = x[0] + x[2], x[1] + x[3]
        put(even.at[0], 16 * group, sums[0] + sums[1])
        put(even.at[1], 16 * group, sums[0] - sums[1])
        put(odd, 16 * group, x[0] - x[2])
        put(odd, 16 * group + 2 * ROWS, x[1] - x[3])
    for copy in small[:1] + small[2:] + blocks:
        copy.wait()
    kept = latitude_column([kept_s[j] for j in range(BAND)], jnp.int32(0))
    kept_ref[...] = kept
    latitudes = [lat * BAND + j for j in range(BAND)]
    weight = latitude_column([weights_s[jnp.minimum(i, NLAT - 1 - i)] for i in latitudes], F32(0.0))
    for step in range(STEPS):
        if step % 2 == 0:
            raw = jnp.dot(even[step // 2], table_v[step], preferred_element_type=F32)
            raw = raw[:ROWS] + raw[ROWS:]
            real, imaginary = raw[:, :BLOCK], raw[:, BLOCK:]
        else:
            raw = jnp.dot(odd[...], table_v[step], preferred_element_type=F32)
            first = raw[:ROWS] + raw[ROWS : 2 * ROWS]
            second = raw[2 * ROWS : 3 * ROWS] + raw[3 * ROWS :]
            if step == 3:
                second = -second
            real = first[:, :BLOCK] + second[:, BLOCK:]
            imaginary = first[:, BLOCK:] - second[:, :BLOCK]
        scale = jnp.where(class_mask(kept, step), weight, 0.0)
        fourier = jnp.concatenate([real * scale, imaginary * scale], axis=0).astype(BF16)
        both[: 2 * ROWS, step * LANES : (step + 1) * LANES] = fourier[:, :LANES]
        both[2 * ROWS :, (3 - step) * LANES : (4 - step) * LANES] = fourier[:, LANES:]
    level = iota((2 * LEVELS, 1), 0) // 2
    diffusion = jnp.zeros((2 * LEVELS, 1), F32)
    for i in range(LEVELS):
        diffusion = jnp.where(level == i, diffusion_s[i], diffusion)
    diffusion_ref[...] = diffusion
    slots = slots_v[...]
    mine = iota((8, LANES), 0) * LANES + iota((8, LANES), 1) == device_ref[0] * 2
    mine = jnp.sum(jnp.where(mine, slots.astype(F32), 0.0), axis=0, keepdims=True)
    wave_ref[...] = jnp.broadcast_to(jnp.sum(mine, axis=1, keepdims=True).astype(jnp.int32), (1, LANES))
    order = slot_order(slots, moves[...], digit[...])
    order_ref[...] = order
    lower = lower_of_pair(order)
    columns = [lower[:, i * LANES : (i + 1) * LANES] for i in range(4)]
    column_ref[...] = jnp.concatenate(columns + columns, axis=0).T
    choice = jnp.where(lower == pair_number((HALF, HALF), 0), 1.0, 0.0).astype(BF16)
    moved = jnp.dot(both[...], choice, preferred_element_type=F32)
    moved = sort_pair(order, moved[: 2 * ROWS], moved[2 * ROWS :])
    moved = jnp.concatenate([half.astype(BF16) for half in moved], axis=1)
    moved = jnp.dot(row_moves[...], moved, preferred_element_type=F32)
    for i in range(LEVS // 2):
        place = i * LANES
        pair = swap_lanes(moved[:, place : place + LANES], moved[:, HALF + place : HALF + place + LANES], LATS)
        for b, block in zip((2 * i, 2 * i + 1), pair):
            parts = swap_parts([block[k * CHUNK : (k + 1) * CHUNK] for k in range(YS)])
            for y in range(YS):
                o_ref[y * LEVS + b] = parts[y].astype(BF16)


def gather_kernel(y_ref, o_ref):
    for y in range(YS):
        for j in range(TILES):
            block = [y_ref[y * LEVS + b, 8 * j : 8 * j + 8, :].astype(F32) for b in range(LEVS)]
            turned = jnp.concatenate(block, axis=0).astype(BF16).T.astype(F32)
            turned = jnp.concatenate([turned[:LATS], turned[LATS:]], axis=1)
            place = (y * TILES + j) * LANES
            o_ref[:, :, place : place + LANES] = turned.reshape(ZS, 4, LANES).astype(BF16)


def scatter_kernel(z_ref, o_ref):
    for y in range(YS):
        for j in range(TILES):
            place = (y * TILES + j) * LANES
            block = z_ref[:, :, place : place + LANES].astype(F32).reshape(LATS, LANES)
            turned = jnp.concatenate([block[:, :LATS], block[:, LATS:]], axis=0).T
            for b in range(LEVS):
                o_ref[y * LEVS + b, 8 + 8 * j : 16 + 8 * j, :] = turned[8 * b : 8 * b + 8].astype(BF16)
    power = jnp.sum(z_ref[:, :, YS * DATA :].astype(F32), axis=0)
    power = jnp.concatenate([power[:, :LANES], power[:, LANES:]], axis=0)
    for peer in range(YS * LEVS):
        o_ref[peer, :8, :] = power.astype(BF16)


def legendre_kernel(
    wave_ref, diffusion_ref, z_ref, table_ref, spectral_hbm, o_ref, spectral_v, comb, sems
):
    copies = []
    for group in range(NORTH * TILES // 4):
        north, south = [], []
        for u in range(4 * group, 4 * group + 4):
            a, tile = divmod(u, TILES)
            for side, lat in (north, a), (south, LATS - 1 - a):
                y, z = divmod(lat, ZS)
                place = (y * TILES + tile) * LANES
                side.append(z_ref[z, :, place : place + LANES].astype(F32))
        north = jnp.concatenate(north, axis=0)
        south = jnp.concatenate(south, axis=0)
        comb[0, 16 * group : 16 * group + 16, :] = north + south
        comb[1, 16 * group : 16 * group + 16, :] = north - south
    column = iota((2 * LEVELS, HALF), 1)
    diffusion = diffusion_ref[...]
    waves = [wave_ref[...], MM - 1 - wave_ref[...]]
    waves = [jnp.concatenate([wave] * (HALF // LANES), axis=1) for wave in waves]
    power = [jnp.zeros((1, HALF), F32), jnp.zeros((1, HALF), F32)]
    halves = []
    for q in range(2):
        left = comb[q].astype(BF16).T
        parts = []
        for t in range(2):
            wave = waves[t]
            raw = jnp.dot(left[64 * t : 64 * t + 64], table_ref[t, q], preferred_element_type=F32)
            degree = wave + 2 * column + q
            spectral = jnp.where(degree < MM, raw, 0.0)
            for level in range(LEVELS):
                spectral_v[t, q, level] = spectral[2 * level : 2 * level + 2]
            copies.append(pltpu.make_async_copy(spectral_v.at[t, q], spectral_hbm.at[t, q], sems.at[2 * t + q]))
            copies[-1].start()
            degree = degree.astype(F32)
            ratio = degree * (degree + 1.0) / (MM * (MM + 1.0))
            damped = (spectral / (1.0 + diffusion * ratio * ratio)).astype(BF16)
            parts.append(
                lax.dot_general(
                    table_ref[t, q], damped, (((1,), (1,)), ((), ())), preferred_element_type=F32
                )
            )
            energy = jnp.sum(spectral * spectral, axis=0, keepdims=True)
            first = wave + q
            moved = jnp.broadcast_to(energy, (8, HALF))
            for bit in range(9):
                moved = jnp.where(first // 2**bit // 2 % 2 == 1, pltpu.roll(moved, 2**bit, 1), moved)
            moved = moved[:1]
            for odd in range(2):
                power[odd] += jnp.where(first % 2 == odd, moved, 0.0)
        halves.append(jnp.concatenate(parts, axis=1))
    source = iota((LANES, 2 * LANES), 0)
    to = iota((LANES, 2 * LANES), 1)
    natural = jnp.zeros((8, 2 * LANES), F32)
    for odd in range(2):
        quarters = [power[odd][:, i * LANES : (i + 1) * LANES] for i in range(4)]
        quarters = jnp.concatenate(quarters + quarters, axis=0).astype(BF16)
        choice = jnp.where(to == 2 * source + odd, 1.0, 0.0).astype(BF16)
        natural += jnp.dot(quarters, choice, preferred_element_type=F32)
    natural = natural[:4].astype(BF16)
    for z in range(ZS):
        o_ref[z, :, YS * DATA :] = natural
    for half, side in enumerate((halves[0] + halves[1], halves[0] - halves[1])):
        for u in range(NORTH * TILES):
            a, tile = divmod(u, TILES)
            y, z = divmod(LATS - 1 - a if half else a, ZS)
            place = (y * TILES + tile) * LANES
            o_ref[z, :, place : place + LANES] = side[4 * u : 4 * u + 4].astype(BF16)
    for copy in copies:
        copy.wait()


def grid_kernel(device_ref, kept_ref, order_ref, column_ref, y_ref, table_ref, o_ref, spectrum_ref):
    kept = kept_ref[...]
    choice = row_choice(device_ref[0] >= NORTH * LEVS, 1)
    firsts, seconds = [], []
    for i in range(LEVS // 2):
        pair = []
        for b in (2 * i, 2 * i + 1):
            parts = swap_parts([y_ref[y * LEVS + b, 8:, :].astype(F32) for y in range(YS)])
            pair.append(jnp.concatenate(parts, axis=0))
        first, second = swap_lanes(pair[0], pair[1], LATS)
        firsts.append(first)
        seconds.append(second)
    back = sort_pair(order_ref[...], jnp.concatenate(firsts, axis=1), jnp.concatenate(seconds, axis=1))
    back = jnp.concatenate([half.astype(BF16) for half in back], axis=1)
    rows = jnp.dot(choice, back, preferred_element_type=F32).astype(BF16)
    rows = jnp.concatenate([rows[:, :HALF], rows[:, HALF:]], axis=0)
    number = pair_number((LANES, HALF), 1)
    choice = [jnp.where(column_ref[:, i : i + 1] == number, 1.0, 0.0).astype(BF16) for i in range(HALF // LANES)]
    numbered = jnp.dot(rows, jnp.concatenate(choice, axis=0), preferred_element_type=F32)
    lefts = []
    for step in range(STEPS):
        low = numbered[: 2 * ROWS, step * LANES : (step + 1) * LANES]
        high = numbered[2 * ROWS :, (3 - step) * LANES : (4 - step) * LANES]
        found = jnp.concatenate([low, high], axis=1)
        mask = class_mask(kept, step)
        real = jnp.where(mask, found[:ROWS], 0.0)
        imaginary = jnp.where(mask, found[ROWS:], 0.0)
        left = jnp.concatenate([real, imaginary], axis=1)
        if step == 1:
            left = jnp.concatenate([left, jnp.concatenate([-imaginary, real], axis=1)], axis=0)
        if step == 3:
            left = jnp.concatenate([left, jnp.concatenate([imaginary, -real], axis=1)], axis=0)
        lefts.append(left.astype(BF16))
    table = table_ref[2:].reshape(4 * BLOCK, QUARTER)
    odd = jnp.dot(jnp.concatenate([lefts[1], lefts[3]], axis=1), table, preferred_element_type=F32)
    first = jnp.dot(lefts[0], table_ref[0], preferred_element_type=F32)
    second = jnp.dot(lefts[2], table_ref[1], preferred_element_type=F32)
    plus, minus = first + second, first - second
    for group in range(ROWS // 16):
        place = slice(16 * group, 16 * group + 16)
        turned = slice(ROWS + 16 * group, ROWS + 16 * group + 16)
        quarters = [plus[place] + odd[place], minus[place] + odd[turned], plus[place] - odd[place], minus[place] - odd[turned]]
        points = jnp.concatenate(quarters, axis=1) * math.sqrt(NLON / MM)
        for i in range(4):
            o_ref[4 * group + i] = points[LEV * i : LEV * (i + 1)]
    power = jnp.zeros((8, LANES), F32)
    for peer in range(YS * LEVS):
        power += y_ref[peer, :8, :].astype(F32)
    power = jnp.concatenate([power[i // 2 + 4 * (i % 2)][None] for i in range(8)], axis=0)
    degree = (iota((8, LANES), 0) * LANES + iota((8, LANES), 1)).astype(F32)
    spectrum_ref[...] = power / (2.0 * LEVELS * (degree + 1.0))


def in_hbm(x):
    return pltpu.with_memory_space_constraint(x, pltpu.HBM)


def exchange(x, axes):
    return lax.all_to_all(x, axes, split_axis=0, concat_axis=0, tiled=True)


def body(grid_fields, legendre, weights, kept_waves, slot_wavenumber, diffusion):
    forward_table, inverse_table = dft_tables()
    device = lax.axis_index(("y", "z", "x", "core")).astype(jnp.int32).reshape(1)
    chunk = (ZS, 4, YS * DATA + 2 * LANES)

    sent, order, column, kept, wave, diffusion = pl.pallas_call(
        fourier_kernel,
        in_specs=[SMEM, HBM, HBM, HBM, HBM, HBM, HBM],
        out_specs=[VMEM] * 6,
        out_shape=[
            jax.ShapeDtypeStruct((YS * LEVS, CHUNK, LANES), BF16),
            jax.ShapeDtypeStruct((1, HALF), jnp.int32),
            jax.ShapeDtypeStruct((LANES, 8), jnp.int32),
            jax.ShapeDtypeStruct((ROWS, 1), jnp.int32),
            jax.ShapeDtypeStruct((1, LANES), jnp.int32),
            jax.ShapeDtypeStruct((2 * LEVELS, 1), F32),
        ],
        scratch_shapes=[
            pltpu.SMEM((BAND,), jnp.int32),
            pltpu.SMEM((NLAT // 2,), F32),
            pltpu.SMEM((LEVELS,), F32),
            pltpu.VMEM((8, LANES), jnp.int32),
            pltpu.VMEM((BAND, LEV, NLON), BF16),
            pltpu.VMEM((STEPS, QUARTER, 2 * BLOCK), BF16),
            pltpu.VMEM((2, 2 * ROWS, QUARTER), BF16),
            pltpu.VMEM((4 * ROWS, QUARTER), BF16),
            pltpu.VMEM((4 * ROWS, HALF), BF16),
            pltpu.VMEM((2 * ROWS, 2 * ROWS), BF16),
            pltpu.VMEM((LANES, HALF), BF16),
            pltpu.VMEM((16, HALF), F32),
            pltpu.SemaphoreType.DMA((5 + STEPS,)),
        ],
        compiler_params=PARAMS,
        name="fourier",
    )(
        device,
        in_hbm(kept_waves),
        in_hbm(weights),
        in_hbm(diffusion),
        in_hbm(slot_wavenumber.reshape(8, LANES)),
        in_hbm(grid_fields.transpose(1, 0, 2)),
        in_hbm(jnp.asarray(forward_table)),
    )
    arrived = exchange(sent, ("y", "x", "core"))
    gathered = pl.pallas_call(
        gather_kernel,
        in_specs=[VMEM],
        out_specs=VMEM,
        out_shape=jax.ShapeDtypeStruct((ZS, 4, YS * DATA), BF16),
        compiler_params=PARAMS,
        name="gather",
    )(arrived)
    gathered = exchange(gathered, ("z",))
    spectral, back = pl.pallas_call(
        legendre_kernel,
        in_specs=[VMEM, VMEM, VMEM, VMEM],
        out_specs=[HBM, VMEM],
        out_shape=[
            jax.ShapeDtypeStruct((2, 2, LEVELS, 2, HALF), F32),
            jax.ShapeDtypeStruct(chunk, BF16),
        ],
        scratch_shapes=[
            pltpu.VMEM((2, 2, LEVELS, 2, HALF), F32),
            pltpu.VMEM((2, NLAT // 2, LANES), F32),
            pltpu.SemaphoreType.DMA((4,)),
        ],
        compiler_params=PARAMS,
        name="legendre",
    )(wave, diffusion, gathered, legendre)
    back = exchange(back, ("z",))
    scattered = pl.pallas_call(
        scatter_kernel,
        in_specs=[VMEM],
        out_specs=VMEM,
        out_shape=jax.ShapeDtypeStruct((YS * LEVS, 8 + CHUNK, LANES), BF16),
        compiler_params=PARAMS,
        name="scatter",
    )(back)
    returned = exchange(scattered, ("y", "x", "core"))
    grid_out, spectrum = pl.pallas_call(
        grid_kernel,
        in_specs=[SMEM, VMEM, VMEM, VMEM, VMEM, VMEM],
        out_specs=[VMEM, VMEM],
        out_shape=[
            jax.ShapeDtypeStruct((BAND, LEV, NLON), F32),
            jax.ShapeDtypeStruct((8, LANES), F32),
        ],
        compiler_params=PARAMS,
        name="grid",
    )(device, kept, order, column, returned, jnp.asarray(inverse_table))
    return (
        grid_out.transpose(1, 0, 2),
        spectral,
        spectrum.reshape(MM),
    )


def solution(mesh):
    fine = Mesh(mesh.devices.reshape(4, 16, 4, 2), ("y", "z", "x", "core"))
    lat, lev = ("y", "z"), ("x", "core")
    both = lat + lev
    in_specs = (P(lev, lat, None), P(both, None, None, None), P(), P(lat), P(), P())
    out_specs = (P(lev, lat, None), P(both, None, None, None, None), P())
    return jax.shard_map(body, mesh=fine, in_specs=in_specs, out_specs=out_specs, check_vma=False)
```

```python
import math

import jax
import jax.numpy as jnp
import ml_dtypes
import numpy as np
from jax import lax
from jax.experimental import pallas as pl
from jax.experimental.pallas import tpu as pltpu
from jax.sharding import Mesh
from jax.sharding import PartitionSpec as P

NLAT = 1280
NLON = 2688
MM = 1024
HALF = MM // 2
LEVELS = 32
BAND = 20
LEV = 4
ROWS = BAND * LEV
LATS = 64
LEVS = 8
YS = 4
ZS = 16
CHUNK = 2 * ROWS // YS
NORTH = LATS // 2
QUARTER = NLON // 4
STEPS = 4
BLOCK = MM // STEPS
TILES = BAND // 4
LANES = 128
DATA = TILES * LANES

BF16 = jnp.bfloat16
F32 = jnp.float32
VMEM = pl.BlockSpec(memory_space=pltpu.VMEM)
HBM = pl.BlockSpec(memory_space=pltpu.HBM)
SMEM = pl.BlockSpec(memory_space=pltpu.SMEM)
PARAMS = pltpu.CompilerParams(vmem_limit_bytes=20 * 1024 * 1024)


def dft_tables():
    sample = np.arange(QUARTER, dtype=np.int32)[:, None]
    number = np.arange(MM, dtype=np.int32)[None, :]
    angles = (sample * number % NLON).astype(np.float32) * np.float32(2.0 * math.pi / NLON)
    norm_scale = np.float32(1.0 / math.sqrt(NLON))
    cosine = (np.cos(angles) * norm_scale).astype(ml_dtypes.bfloat16)
    sine = (-np.sin(angles) * norm_scale).astype(ml_dtypes.bfloat16)
    rising = np.arange(LANES)
    places = np.concatenate([rising, BLOCK - 1 - rising])
    numbers = places[None, :] * STEPS + np.arange(STEPS)[:, None]
    forward = np.stack([cosine[:, numbers], sine[:, numbers]], axis=2)
    forward = np.ascontiguousarray(forward.transpose(1, 0, 2, 3)).reshape(STEPS, QUARTER, 2 * BLOCK)
    inverse = np.ascontiguousarray(forward.transpose(0, 2, 1)[[0, 2, 1, 3]])
    forward = np.stack([np.concatenate([forward[i], forward[i + 2]], axis=1) for i in range(2)])
    return forward, inverse


def iota(shape, dim):
    return lax.broadcasted_iota(jnp.int32, shape, dim)


def pair_number(shape, dim):
    place = iota(shape, dim)
    return place % LANES * STEPS + place // LANES


def slot_moves():
    source = iota((LANES, HALF), 0)
    to = iota((LANES, HALF), 1)
    choice = jnp.where(source == to // YS % 8 * 16 + to // LATS * 2, 1.0, 0.0).astype(BF16)
    row = iota((16, HALF), 0)
    lane = iota((16, HALF), 1)
    mine = row % 8 == lane % YS * 2 + lane // 32 % 2
    return choice, jnp.where(mine, jnp.where(row < 8, 32.0, 1.0), 0.0)


def slot_order(slots, choice, digit):
    digits = jnp.concatenate([slots // 32, slots % 32], axis=0).astype(F32).astype(BF16)
    moved = jnp.dot(digits, choice, preferred_element_type=F32)
    return jnp.sum(moved * digit, axis=0, keepdims=True).astype(jnp.int32)


def latitude_column(scalars, zero):
    band = iota((ROWS, 1), 0) // LEV
    column = jnp.full((ROWS, 1), zero)
    for j in range(BAND):
        column = jnp.where(band == j, scalars[j], column)
    return column


def class_mask(kept, step):
    place = iota((ROWS, BLOCK), 1)
    place = jnp.where(place < LANES, place, BLOCK + LANES - 1 - place)
    return place * STEPS + step < kept


def lower_of_pair(wave):
    return jnp.minimum(wave, MM - 1 - wave)


def row_choice(southern, side):
    to = iota((2 * ROWS, 2 * ROWS), side)
    source = iota((2 * ROWS, 2 * ROWS), 1 - side)
    band = to % CHUNK // (2 * LEV) * YS + to // CHUNK
    band = jnp.where(southern, BAND - 1 - band, band)
    wanted = (to % 2) * ROWS + band * LEV + to // 2 % LEV
    return jnp.where(source == wanted, 1.0, 0.0).astype(BF16)


def swap_lanes(even, odd, width):
    high = iota(even.shape, 1) // width % 2 == 1
    return (
        jnp.where(high, pltpu.roll(odd, width, 1), even),
        jnp.where(high, odd, pltpu.roll(even, LANES - width, 1)),
    )


def sort_pair(order, first, second):
    flip = jnp.broadcast_to(order >= HALF, first.shape)
    return jnp.where(flip, second, first), jnp.where(flip, first, second)


def swap_parts(parts):
    parts = list(parts)
    parts[0], parts[1] = swap_lanes(parts[0], parts[1], 1)
    parts[2], parts[3] = swap_lanes(parts[2], parts[3], 1)
    parts[0], parts[2] = swap_lanes(parts[0], parts[2], 2)
    parts[1], parts[3] = swap_lanes(parts[1], parts[3], 2)
    return parts


def fourier_kernel(
    device_ref, kept_hbm, weights_hbm, diffusion_hbm, slots_hbm, x_hbm, table_hbm, o_ref, order_ref, column_ref,
    kept_ref, wave_ref, diffusion_ref, kept_s, weights_s, diffusion_s, slots_v, x_v,
    table_v, even, odd, both, row_moves, moves, digit, sems
):
    small = [
        pltpu.make_async_copy(slots_hbm, slots_v, sems.at[0]),
        pltpu.make_async_copy(x_hbm, x_v, sems.at[1]),
        pltpu.make_async_copy(kept_hbm, kept_s, sems.at[2]),
        pltpu.make_async_copy(weights_hbm, weights_s, sems.at[3]),
        pltpu.make_async_copy(diffusion_hbm, diffusion_s, sems.at[4 + STEPS]),
    ]
    blocks = [pltpu.make_async_copy(table_hbm.at[i], table_v.at[i], sems.at[4 + i]) for i in range(2)]
    for copy in small + blocks:
        copy.start()
    lat = device_ref[0] // LEVS
    row_moves[...] = row_choice(lat >= NORTH, 0)
    moves[...], digit[...] = slot_moves()
    small[1].wait()

    def put(ref, place, value):
        high = value.astype(BF16)
        low = (value - high.astype(F32)).astype(BF16)
        for part, half in enumerate((high, low)):
            ref[pl.ds(place + part * ROWS, 16), :] = half

    for group in range(ROWS // 16):
        x = jnp.concatenate([x_v[4 * group + i].astype(F32) for i in range(4)], axis=0)
        x = [x[:, q * QUARTER : (q + 1) * QUARTER] for q in range(4)]
        sums = x[0] + x[2], x[1] + x[3]
        put(even.at[0], 16 * group, sums[0] + sums[1])
        put(even.at[1], 16 * group, sums[0] - sums[1])
        put(odd, 16 * group, x[0] - x[2])
        put(odd, 16 * group + 2 * ROWS, x[1] - x[3])
    for copy in small[:1] + small[2:] + blocks:
        copy.wait()
    kept = latitude_column([kept_s[j] for j in range(BAND)], jnp.int32(0))
    kept_ref[...] = kept
    latitudes = [lat * BAND + j for j in range(BAND)]
    weight = latitude_column([weights_s[jnp.minimum(i, NLAT - 1 - i)] for i in latitudes], F32(0.0))
    turned = jnp.dot(odd[...], table_v[1], preferred_element_type=F32)
    for step in range(STEPS):
        if step % 2 == 0:
            columns = slice(step * BLOCK, step * BLOCK + 2 * BLOCK)
            raw = jnp.dot(even[step // 2], table_v[0, :, columns], preferred_element_type=F32)
            raw = raw[:ROWS] + raw[ROWS:]
            real, imaginary = raw[:, :BLOCK], raw[:, BLOCK:]
        else:
            raw = turned[:, (step - 1) * BLOCK : (step + 1) * BLOCK]
            first = raw[:ROWS] + raw[ROWS : 2 * ROWS]
            second = raw[2 * ROWS : 3 * ROWS] + raw[3 * ROWS :]
            if step == 3:
                second = -second
            real = first[:, :BLOCK] + second[:, BLOCK:]
            imaginary = first[:, BLOCK:] - second[:, :BLOCK]
        scale = jnp.where(class_mask(kept, step), weight, 0.0)
        fourier = jnp.concatenate([real * scale, imaginary * scale], axis=0).astype(BF16)
        both[: 2 * ROWS, step * LANES : (step + 1) * LANES] = fourier[:, :LANES]
        both[2 * ROWS :, (3 - step) * LANES : (4 - step) * LANES] = fourier[:, LANES:]
    level = iota((2 * LEVELS, 1), 0) // 2
    diffusion = jnp.zeros((2 * LEVELS, 1), F32)
    for i in range(LEVELS):
        diffusion = jnp.where(level == i, diffusion_s[i], diffusion)
    diffusion_ref[...] = diffusion
    slots = slots_v[...]
    mine = iota((8, LANES), 0) * LANES + iota((8, LANES), 1) == device_ref[0] * 2
    mine = jnp.sum(jnp.where(mine, slots.astype(F32), 0.0), axis=0, keepdims=True)
    wave_ref[...] = jnp.broadcast_to(jnp.sum(mine, axis=1, keepdims=True).astype(jnp.int32), (1, LANES))
    order = slot_order(slots, moves[...], digit[...])
    order_ref[...] = order
    lower = lower_of_pair(order)
    columns = [lower[:, i * LANES : (i + 1) * LANES] for i in range(4)]
    column_ref[...] = jnp.concatenate(columns + columns, axis=0).T
    choice = jnp.where(lower == pair_number((HALF, HALF), 0), 1.0, 0.0).astype(BF16)
    moved = jnp.dot(both[...], choice, preferred_element_type=F32)
    moved = sort_pair(order, moved[: 2 * ROWS], moved[2 * ROWS :])
    moved = jnp.concatenate([half.astype(BF16) for half in moved], axis=1)
    moved = jnp.dot(row_moves[...], moved, preferred_element_type=F32)
    for i in range(LEVS // 2):
        place = i * LANES
        pair = swap_lanes(moved[:, place : place + LANES], moved[:, HALF + place : HALF + place + LANES], LATS)
        for b, block in zip((2 * i, 2 * i + 1), pair):
            parts = swap_parts([block[k * CHUNK : (k + 1) * CHUNK] for k in range(YS)])
            for y in range(YS):
                o_ref[y * LEVS + b] = parts[y].astype(BF16)


def gather_kernel(y_ref, o_ref):
    for y in range(YS):
        for j in range(TILES):
            block = [y_ref[y * LEVS + b, 8 * j : 8 * j + 8, :].astype(F32) for b in range(LEVS)]
            turned = jnp.concatenate(block, axis=0).astype(BF16).T.astype(F32)
            turned = jnp.concatenate([turned[:LATS], turned[LATS:]], axis=1)
            place = (y * TILES + j) * LANES
            o_ref[:, :, place : place + LANES] = turned.reshape(ZS, 4, LANES).astype(BF16)


def scatter_kernel(z_ref, o_ref):
    for y in range(YS):
        for j in range(TILES):
            place = (y * TILES + j) * LANES
            block = z_ref[:, :, place : place + LANES].astype(F32).reshape(LATS, LANES)
            turned = jnp.concatenate([block[:, :LATS], block[:, LATS:]], axis=0).T
            for b in range(LEVS):
                o_ref[y * LEVS + b, 8 + 8 * j : 16 + 8 * j, :] = turned[8 * b : 8 * b + 8].astype(BF16)
    power = jnp.sum(z_ref[:, :, YS * DATA :].astype(F32), axis=0)
    power = jnp.concatenate([power[:, :LANES], power[:, LANES:]], axis=0)
    for peer in range(YS * LEVS):
        o_ref[peer, :8, :] = power.astype(BF16)


def legendre_kernel(
    wave_ref, diffusion_ref, z_ref, table_ref, spectral_hbm, o_ref, spectral_v, comb, sems
):
    copies = []
    for group in range(NORTH * TILES // 4):
        north, south = [], []
        for u in range(4 * group, 4 * group + 4):
            a, tile = divmod(u, TILES)
            for side, lat in (north, a), (south, LATS - 1 - a):
                y, z = divmod(lat, ZS)
                place = (y * TILES + tile) * LANES
                side.append(z_ref[z, :, place : place + LANES].astype(F32))
        north = jnp.concatenate(north, axis=0)
        south = jnp.concatenate(south, axis=0)
        comb[0, 16 * group : 16 * group + 16, :] = north + south
        comb[1, 16 * group : 16 * group + 16, :] = north - south
    column = iota((2 * LEVELS, HALF), 1)
    diffusion = diffusion_ref[...]
    waves = [wave_ref[...], MM - 1 - wave_ref[...]]
    waves = [jnp.concatenate([wave] * (HALF // LANES), axis=1) for wave in waves]
    power = [jnp.zeros((1, HALF), F32), jnp.zeros((1, HALF), F32)]
    halves = []
    for q in range(2):
        left = comb[q].astype(BF16).T
        parts = []
        for t in range(2):
            wave = waves[t]
            raw = jnp.dot(left[64 * t : 64 * t + 64], table_ref[t, q], preferred_element_type=F32)
            degree = wave + 2 * column + q
            spectral = jnp.where(degree < MM, raw, 0.0)
            for level in range(LEVELS):
                spectral_v[t, q, level] = spectral[2 * level : 2 * level + 2]
            copies.append(pltpu.make_async_copy(spectral_v.at[t, q], spectral_hbm.at[t, q], sems.at[2 * t + q]))
            copies[-1].start()
            degree = degree.astype(F32)
            ratio = degree * (degree + 1.0) / (MM * (MM + 1.0))
            damped = (spectral / (1.0 + diffusion * ratio * ratio)).astype(BF16)
            parts.append(
                lax.dot_general(
                    table_ref[t, q], damped, (((1,), (1,)), ((), ())), preferred_element_type=F32
                )
            )
            energy = jnp.sum(spectral * spectral, axis=0, keepdims=True)
            first = wave + q
            moved = jnp.broadcast_to(energy, (8, HALF))
            for bit in range(9):
                moved = jnp.where(first // 2**bit // 2 % 2 == 1, pltpu.roll(moved, 2**bit, 1), moved)
            moved = moved[:1]
            for odd in range(2):
                power[odd] += jnp.where(first % 2 == odd, moved, 0.0)
        halves.append(jnp.concatenate(parts, axis=1))
    source = iota((LANES, 2 * LANES), 0)
    to = iota((LANES, 2 * LANES), 1)
    natural = jnp.zeros((8, 2 * LANES), F32)
    for odd in range(2):
        quarters = [power[odd][:, i * LANES : (i + 1) * LANES] for i in range(4)]
        quarters = jnp.concatenate(quarters + quarters, axis=0).astype(BF16)
        choice = jnp.where(to == 2 * source + odd, 1.0, 0.0).astype(BF16)
        natural += jnp.dot(quarters, choice, preferred_element_type=F32)
    natural = natural[:4].astype(BF16)
    for z in range(ZS):
        o_ref[z, :, YS * DATA :] = natural
    for half, side in enumerate((halves[0] + halves[1], halves[0] - halves[1])):
        for u in range(NORTH * TILES):
            a, tile = divmod(u, TILES)
            y, z = divmod(LATS - 1 - a if half else a, ZS)
            place = (y * TILES + tile) * LANES
            o_ref[z, :, place : place + LANES] = side[4 * u : 4 * u + 4].astype(BF16)
    for copy in copies:
        copy.wait()


def grid_kernel(device_ref, kept_ref, order_ref, column_ref, y_ref, table_ref, o_ref, spectrum_ref):
    kept = kept_ref[...]
    choice = row_choice(device_ref[0] >= NORTH * LEVS, 1)
    firsts, seconds = [], []
    for i in range(LEVS // 2):
        pair = []
        for b in (2 * i, 2 * i + 1):
            parts = swap_parts([y_ref[y * LEVS + b, 8:, :].astype(F32) for y in range(YS)])
            pair.append(jnp.concatenate(parts, axis=0))
        first, second = swap_lanes(pair[0], pair[1], LATS)
        firsts.append(first)
        seconds.append(second)
    back = sort_pair(order_ref[...], jnp.concatenate(firsts, axis=1), jnp.concatenate(seconds, axis=1))
    back = jnp.concatenate([half.astype(BF16) for half in back], axis=1)
    rows = jnp.dot(choice, back, preferred_element_type=F32).astype(BF16)
    rows = jnp.concatenate([rows[:, :HALF], rows[:, HALF:]], axis=0)
    number = pair_number((LANES, HALF), 1)
    choice = [jnp.where(column_ref[:, i : i + 1] == number, 1.0, 0.0).astype(BF16) for i in range(HALF // LANES)]
    numbered = jnp.dot(rows, jnp.concatenate(choice, axis=0), preferred_element_type=F32)
    lefts = []
    for step in range(STEPS):
        low = numbered[: 2 * ROWS, step * LANES : (step + 1) * LANES]
        high = numbered[2 * ROWS :, (3 - step) * LANES : (4 - step) * LANES]
        found = jnp.concatenate([low, high], axis=1)
        mask = class_mask(kept, step)
        real = jnp.where(mask, found[:ROWS], 0.0)
        imaginary = jnp.where(mask, found[ROWS:], 0.0)
        left = jnp.concatenate([real, imaginary], axis=1)
        if step == 1:
            left = jnp.concatenate([left, jnp.concatenate([-imaginary, real], axis=1)], axis=0)
        if step == 3:
            left = jnp.concatenate([left, jnp.concatenate([imaginary, -real], axis=1)], axis=0)
        lefts.append(left.astype(BF16))
    table = table_ref[2:].reshape(4 * BLOCK, QUARTER)
    odd = jnp.dot(jnp.concatenate([lefts[1], lefts[3]], axis=1), table, preferred_element_type=F32)
    first = jnp.dot(lefts[0], table_ref[0], preferred_element_type=F32)
    second = jnp.dot(lefts[2], table_ref[1], preferred_element_type=F32)
    plus, minus = first + second, first - second
    for group in range(ROWS // 16):
        place = slice(16 * group, 16 * group + 16)
        turned = slice(ROWS + 16 * group, ROWS + 16 * group + 16)
        quarters = [plus[place] + odd[place], minus[place] + odd[turned], plus[place] - odd[place], minus[place] - odd[turned]]
        points = jnp.concatenate(quarters, axis=1) * math.sqrt(NLON / MM)
        for i in range(4):
            o_ref[4 * group + i] = points[LEV * i : LEV * (i + 1)]
    power = jnp.zeros((8, LANES), F32)
    for peer in range(YS * LEVS):
        power += y_ref[peer, :8, :].astype(F32)
    power = jnp.concatenate([power[i // 2 + 4 * (i % 2)][None] for i in range(8)], axis=0)
    degree = (iota((8, LANES), 0) * LANES + iota((8, LANES), 1)).astype(F32)
    spectrum_ref[...] = power / (2.0 * LEVELS * (degree + 1.0))


def in_hbm(x):
    return pltpu.with_memory_space_constraint(x, pltpu.HBM)


def exchange(x, axes):
    return lax.all_to_all(x, axes, split_axis=0, concat_axis=0, tiled=True)


def body(grid_fields, legendre, weights, kept_waves, slot_wavenumber, diffusion):
    forward_table, inverse_table = dft_tables()
    device = lax.axis_index(("y", "z", "x", "core")).astype(jnp.int32).reshape(1)
    chunk = (ZS, 4, YS * DATA + 2 * LANES)

    sent, order, column, kept, wave, diffusion = pl.pallas_call(
        fourier_kernel,
        in_specs=[SMEM, HBM, HBM, HBM, HBM, HBM, HBM],
        out_specs=[VMEM] * 6,
        out_shape=[
            jax.ShapeDtypeStruct((YS * LEVS, CHUNK, LANES), BF16),
            jax.ShapeDtypeStruct((1, HALF), jnp.int32),
            jax.ShapeDtypeStruct((LANES, 8), jnp.int32),
            jax.ShapeDtypeStruct((ROWS, 1), jnp.int32),
            jax.ShapeDtypeStruct((1, LANES), jnp.int32),
            jax.ShapeDtypeStruct((2 * LEVELS, 1), F32),
        ],
        scratch_shapes=[
            pltpu.SMEM((BAND,), jnp.int32),
            pltpu.SMEM((NLAT // 2,), F32),
            pltpu.SMEM((LEVELS,), F32),
            pltpu.VMEM((8, LANES), jnp.int32),
            pltpu.VMEM((BAND, LEV, NLON), BF16),
            pltpu.VMEM((2, QUARTER, 4 * BLOCK), BF16),
            pltpu.VMEM((2, 2 * ROWS, QUARTER), BF16),
            pltpu.VMEM((4 * ROWS, QUARTER), BF16),
            pltpu.VMEM((4 * ROWS, HALF), BF16),
            pltpu.VMEM((2 * ROWS, 2 * ROWS), BF16),
            pltpu.VMEM((LANES, HALF), BF16),
            pltpu.VMEM((16, HALF), F32),
            pltpu.SemaphoreType.DMA((5 + STEPS,)),
        ],
        compiler_params=PARAMS,
        name="fourier",
    )(
        device,
        in_hbm(kept_waves),
        in_hbm(weights),
        in_hbm(diffusion),
        in_hbm(slot_wavenumber.reshape(8, LANES)),
        in_hbm(grid_fields.transpose(1, 0, 2)),
        in_hbm(jnp.asarray(forward_table)),
    )
    arrived = exchange(sent, ("y", "x", "core"))
    gathered = pl.pallas_call(
        gather_kernel,
        in_specs=[VMEM],
        out_specs=VMEM,
        out_shape=jax.ShapeDtypeStruct((ZS, 4, YS * DATA), BF16),
        compiler_params=PARAMS,
        name="gather",
    )(arrived)
    gathered = exchange(gathered, ("z",))
    spectral, back = pl.pallas_call(
        legendre_kernel,
        in_specs=[VMEM, VMEM, VMEM, VMEM],
        out_specs=[HBM, VMEM],
        out_shape=[
            jax.ShapeDtypeStruct((2, 2, LEVELS, 2, HALF), F32),
            jax.ShapeDtypeStruct(chunk, BF16),
        ],
        scratch_shapes=[
            pltpu.VMEM((2, 2, LEVELS, 2, HALF), F32),
            pltpu.VMEM((2, NLAT // 2, LANES), F32),
            pltpu.SemaphoreType.DMA((4,)),
        ],
        compiler_params=PARAMS,
        name="legendre",
    )(wave, diffusion, gathered, legendre)
    back = exchange(back, ("z",))
    scattered = pl.pallas_call(
        scatter_kernel,
        in_specs=[VMEM],
        out_specs=VMEM,
        out_shape=jax.ShapeDtypeStruct((YS * LEVS, 8 + CHUNK, LANES), BF16),
        compiler_params=PARAMS,
        name="scatter",
    )(back)
    returned = exchange(scattered, ("y", "x", "core"))
    grid_out, spectrum = pl.pallas_call(
        grid_kernel,
        in_specs=[SMEM, VMEM, VMEM, VMEM, VMEM, VMEM],
        out_specs=[VMEM, VMEM],
        out_shape=[
            jax.ShapeDtypeStruct((BAND, LEV, NLON), F32),
            jax.ShapeDtypeStruct((8, LANES), F32),
        ],
        compiler_params=PARAMS,
        name="grid",
    )(device, kept, order, column, returned, jnp.asarray(inverse_table))
    return (
        grid_out.transpose(1, 0, 2),
        spectral,
        spectrum.reshape(MM),
    )


def solution(mesh):
    fine = Mesh(mesh.devices.reshape(4, 16, 4, 2), ("y", "z", "x", "core"))
    lat, lev = ("y", "z"), ("x", "core")
    both = lat + lev
    in_specs = (P(lev, lat, None), P(both, None, None, None), P(), P(lat), P(), P())
    out_specs = (P(lev, lat, None), P(both, None, None, None, None), P())
    return jax.shard_map(body, mesh=fine, in_specs=in_specs, out_specs=out_specs, check_vma=False)
```

```python
import math

import jax
import jax.numpy as jnp
import ml_dtypes
import numpy as np
from jax import lax
from jax.experimental import pallas as pl
from jax.experimental.pallas import tpu as pltpu
from jax.sharding import Mesh
from jax.sharding import PartitionSpec as P

NLAT = 1280
NLON = 2688
MM = 1024
HALF = MM // 2
LEVELS = 32
BAND = 20
LEV = 4
ROWS = BAND * LEV
LATS = 64
LEVS = 8
YS = 4
ZS = 16
CHUNK = 2 * ROWS // YS
NORTH = LATS // 2
QUARTER = NLON // 4
STEPS = 4
BLOCK = MM // STEPS
TILES = BAND // 4
LANES = 128
DATA = TILES * LANES

BF16 = jnp.bfloat16
F32 = jnp.float32
VMEM = pl.BlockSpec(memory_space=pltpu.VMEM)
HBM = pl.BlockSpec(memory_space=pltpu.HBM)
SMEM = pl.BlockSpec(memory_space=pltpu.SMEM)
PARAMS = pltpu.CompilerParams(vmem_limit_bytes=20 * 1024 * 1024)


def dft_tables():
    sample = np.arange(QUARTER, dtype=np.int32)[:, None]
    number = np.arange(MM, dtype=np.int32)[None, :]
    angles = (sample * number % NLON).astype(np.float32) * np.float32(2.0 * math.pi / NLON)
    norm_scale = np.float32(1.0 / math.sqrt(NLON))
    cosine = (np.cos(angles) * norm_scale).astype(ml_dtypes.bfloat16)
    sine = (-np.sin(angles) * norm_scale).astype(ml_dtypes.bfloat16)
    rising = np.arange(LANES)
    places = np.concatenate([rising, BLOCK - 1 - rising])
    numbers = places[None, :] * STEPS + np.arange(STEPS)[:, None]
    forward = np.stack([cosine[:, numbers], sine[:, numbers]], axis=2)
    forward = np.ascontiguousarray(forward.transpose(1, 0, 2, 3)).reshape(STEPS, QUARTER, 2 * BLOCK)
    inverse = np.ascontiguousarray(forward.transpose(0, 2, 1)[[0, 2, 1, 3]])
    forward = np.stack([np.concatenate([forward[i], forward[i + 2]], axis=1) for i in range(2)])
    return forward, inverse


def iota(shape, dim):
    return lax.broadcasted_iota(jnp.int32, shape, dim)


def pair_number(shape, dim):
    place = iota(shape, dim)
    return place % LANES * STEPS + place // LANES


def slot_moves():
    source = iota((LANES, HALF), 0)
    to = iota((LANES, HALF), 1)
    choice = jnp.where(source == to // YS % 8 * 16 + to // LATS * 2, 1.0, 0.0).astype(BF16)
    row = iota((16, HALF), 0)
    lane = iota((16, HALF), 1)
    mine = row % 8 == lane % YS * 2 + lane // 32 % 2
    return choice, jnp.where(mine, jnp.where(row < 8, 32.0, 1.0), 0.0)


def slot_order(slots, choice, digit):
    digits = jnp.concatenate([slots // 32, slots % 32], axis=0).astype(F32).astype(BF16)
    moved = jnp.dot(digits, choice, preferred_element_type=F32)
    return jnp.sum(moved * digit, axis=0, keepdims=True).astype(jnp.int32)


def latitude_column(scalars, zero):
    band = iota((ROWS, 1), 0) // LEV
    column = jnp.full((ROWS, 1), zero)
    for j in range(BAND):
        column = jnp.where(band == j, scalars[j], column)
    return column


def class_mask(kept, step):
    place = iota((ROWS, BLOCK), 1)
    place = jnp.where(place < LANES, place, BLOCK + LANES - 1 - place)
    return place * STEPS + step < kept


def lower_of_pair(wave):
    return jnp.minimum(wave, MM - 1 - wave)


def row_choice(southern, side):
    to = iota((2 * ROWS, 2 * ROWS), side)
    source = iota((2 * ROWS, 2 * ROWS), 1 - side)
    band = to % CHUNK // (2 * LEV) * YS + to // CHUNK
    band = jnp.where(southern, BAND - 1 - band, band)
    wanted = (to % 2) * ROWS + band * LEV + to // 2 % LEV
    return jnp.where(source == wanted, 1.0, 0.0).astype(BF16)


def swap_lanes(even, odd, width):
    high = iota(even.shape, 1) // width % 2 == 1
    return (
        jnp.where(high, pltpu.roll(odd, width, 1), even),
        jnp.where(high, odd, pltpu.roll(even, LANES - width, 1)),
    )


def sort_pair(order, first, second):
    flip = jnp.broadcast_to(order >= HALF, first.shape)
    return jnp.where(flip, second, first), jnp.where(flip, first, second)


def swap_parts(parts):
    parts = list(parts)
    parts[0], parts[1] = swap_lanes(parts[0], parts[1], 1)
    parts[2], parts[3] = swap_lanes(parts[2], parts[3], 1)
    parts[0], parts[2] = swap_lanes(parts[0], parts[2], 2)
    parts[1], parts[3] = swap_lanes(parts[1], parts[3], 2)
    return parts


def fourier_kernel(
    device_ref, kept_hbm, weights_hbm, diffusion_hbm, slots_hbm, x_hbm, table_hbm, o_ref, order_ref, column_ref,
    kept_ref, wave_ref, diffusion_ref, kept_s, weights_s, diffusion_s, slots_v, x_v,
    table_v, even, odd, both, row_moves, moves, digit, sems
):
    small = [
        pltpu.make_async_copy(slots_hbm, slots_v, sems.at[0]),
        pltpu.make_async_copy(x_hbm, x_v, sems.at[1]),
        pltpu.make_async_copy(kept_hbm, kept_s, sems.at[2]),
        pltpu.make_async_copy(weights_hbm, weights_s, sems.at[3]),
        pltpu.make_async_copy(diffusion_hbm, diffusion_s, sems.at[4 + STEPS]),
    ]
    blocks = [pltpu.make_async_copy(table_hbm.at[i], table_v.at[i], sems.at[4 + i]) for i in range(2)]
    for copy in small + blocks:
        copy.start()
    lat = device_ref[0] // LEVS
    row_moves[...] = row_choice(lat >= NORTH, 0)
    moves[...], digit[...] = slot_moves()
    small[1].wait()

    def put(ref, place, value):
        high = value.astype(BF16)
        low = (value - high.astype(F32)).astype(BF16)
        for part, half in enumerate((high, low)):
            ref[pl.ds(place + part * ROWS, 16), :] = half

    for group in range(ROWS // 16):
        x = jnp.concatenate([x_v[4 * group + i].astype(F32) for i in range(4)], axis=0)
        x = [x[:, q * QUARTER : (q + 1) * QUARTER] for q in range(4)]
        sums = x[0] + x[2], x[1] + x[3]
        put(even.at[0], 16 * group, sums[0] + sums[1])
        put(even.at[1], 16 * group, sums[0] - sums[1])
        put(odd, 16 * group, x[0] - x[2])
        put(odd, 16 * group + 2 * ROWS, x[1] - x[3])
    for copy in small[:1] + small[2:] + blocks:
        copy.wait()
    kept = latitude_column([kept_s[j] for j in range(BAND)], jnp.int32(0))
    kept_ref[...] = kept
    latitudes = [lat * BAND + j for j in range(BAND)]
    weight = latitude_column([weights_s[jnp.minimum(i, NLAT - 1 - i)] for i in latitudes], F32(0.0))
    turned = jnp.dot(odd[...], table_v[1], preferred_element_type=F32)
    for step in range(STEPS):
        if step % 2 == 0:
            columns = slice(step * BLOCK, step * BLOCK + 2 * BLOCK)
            raw = jnp.dot(even[step // 2], table_v[0, :, columns], preferred_element_type=F32)
            raw = raw[:ROWS] + raw[ROWS:]
            real, imaginary = raw[:, :BLOCK], raw[:, BLOCK:]
        else:
            raw = turned[:, (step - 1) * BLOCK : (step + 1) * BLOCK]
            first = raw[:ROWS] + raw[ROWS : 2 * ROWS]
            second = raw[2 * ROWS : 3 * ROWS] + raw[3 * ROWS :]
            if step == 3:
                second = -second
            real = first[:, :BLOCK] + second[:, BLOCK:]
            imaginary = first[:, BLOCK:] - second[:, :BLOCK]
        scale = jnp.where(class_mask(kept, step), weight, 0.0)
        fourier = jnp.concatenate([real * scale, imaginary * scale], axis=0).astype(BF16)
        both[: 2 * ROWS, step * LANES : (step + 1) * LANES] = fourier[:, :LANES]
        both[2 * ROWS :, (3 - step) * LANES : (4 - step) * LANES] = fourier[:, LANES:]
    level = iota((2 * LEVELS, 1), 0) // 2
    diffusion = jnp.zeros((2 * LEVELS, 1), F32)
    for i in range(LEVELS):
        diffusion = jnp.where(level == i, diffusion_s[i], diffusion)
    diffusion_ref[...] = diffusion
    slots = slots_v[...]
    mine = iota((8, LANES), 0) * LANES + iota((8, LANES), 1) == device_ref[0] * 2
    mine = jnp.sum(jnp.where(mine, slots.astype(F32), 0.0), axis=0, keepdims=True)
    wave_ref[...] = jnp.broadcast_to(jnp.sum(mine, axis=1, keepdims=True).astype(jnp.int32), (1, LANES))
    order = slot_order(slots, moves[...], digit[...])
    order_ref[...] = order
    lower = lower_of_pair(order)
    columns = [lower[:, i * LANES : (i + 1) * LANES] for i in range(4)]
    column_ref[...] = jnp.concatenate(columns + columns, axis=0).T
    choice = jnp.where(lower == pair_number((HALF, HALF), 0), 1.0, 0.0).astype(BF16)
    moved = jnp.dot(both[...], choice, preferred_element_type=F32)
    moved = sort_pair(order, moved[: 2 * ROWS], moved[2 * ROWS :])
    moved = jnp.concatenate([half.astype(BF16) for half in moved], axis=1)
    moved = jnp.dot(row_moves[...], moved, preferred_element_type=F32)
    for i in range(LEVS // 2):
        place = i * LANES
        pair = swap_lanes(moved[:, place : place + LANES], moved[:, HALF + place : HALF + place + LANES], LATS)
        for b, block in zip((2 * i, 2 * i + 1), pair):
            parts = swap_parts([block[k * CHUNK : (k + 1) * CHUNK] for k in range(YS)])
            for y in range(YS):
                o_ref[y * LEVS + b] = parts[y].astype(BF16)


def gather_kernel(y_ref, o_ref):
    for y in range(YS):
        for j in range(TILES):
            block = [y_ref[y * LEVS + b, 8 * j : 8 * j + 8, :].astype(F32) for b in range(LEVS)]
            turned = jnp.concatenate(block, axis=0).astype(BF16).T.astype(F32)
            turned = jnp.concatenate([turned[:LATS], turned[LATS:]], axis=1)
            place = (y * TILES + j) * LANES
            o_ref[:, :, place : place + LANES] = turned.reshape(ZS, 4, LANES).astype(BF16)


def scatter_kernel(z_ref, o_ref):
    for y in range(YS):
        for j in range(TILES):
            place = (y * TILES + j) * LANES
            block = z_ref[:, :, place : place + LANES].astype(F32).reshape(LATS, LANES)
            turned = jnp.concatenate([block[:, :LATS], block[:, LATS:]], axis=0).T
            for b in range(LEVS):
                o_ref[y * LEVS + b, 8 + 8 * j : 16 + 8 * j, :] = turned[8 * b : 8 * b + 8].astype(BF16)
    power = jnp.sum(z_ref[:, :, YS * DATA :].astype(F32), axis=0)
    power = jnp.concatenate([power[:, :LANES], power[:, LANES:]], axis=0)
    for peer in range(YS * LEVS):
        o_ref[peer, :8, :] = power.astype(BF16)


def legendre_kernel(
    wave_ref, diffusion_ref, z_ref, table_ref, spectral_hbm, o_ref, spectral_v, comb, sems
):
    copies = []
    for group in range(NORTH * TILES // 4):
        north, south = [], []
        for u in range(4 * group, 4 * group + 4):
            a, tile = divmod(u, TILES)
            for side, lat in (north, a), (south, LATS - 1 - a):
                y, z = divmod(lat, ZS)
                place = (y * TILES + tile) * LANES
                side.append(z_ref[z, :, place : place + LANES].astype(F32))
        north = jnp.concatenate(north, axis=0)
        south = jnp.concatenate(south, axis=0)
        comb[0, 16 * group : 16 * group + 16, :] = (north + south).astype(BF16)
        comb[1, 16 * group : 16 * group + 16, :] = (north - south).astype(BF16)
    column = iota((2 * LEVELS, HALF), 1)
    diffusion = diffusion_ref[...]
    waves = [wave_ref[...], MM - 1 - wave_ref[...]]
    waves = [jnp.concatenate([wave] * (HALF // LANES), axis=1) for wave in waves]
    power = [jnp.zeros((1, HALF), F32), jnp.zeros((1, HALF), F32)]
    halves = []
    for q in range(2):
        left = comb[q].T
        parts = []
        for t in range(2):
            wave = waves[t]
            raw = jnp.dot(left[64 * t : 64 * t + 64], table_ref[t, q], preferred_element_type=F32)
            degree = wave + 2 * column + q
            spectral = jnp.where(degree < MM, raw, 0.0)
            for level in range(LEVELS):
                spectral_v[t, q, level] = spectral[2 * level : 2 * level + 2]
            copies.append(pltpu.make_async_copy(spectral_v.at[t, q], spectral_hbm.at[t, q], sems.at[2 * t + q]))
            copies[-1].start()
            degree = degree.astype(F32)
            ratio = degree * (degree + 1.0) / (MM * (MM + 1.0))
            damped = (spectral / (1.0 + diffusion * ratio * ratio)).astype(BF16)
            parts.append(
                lax.dot_general(
                    table_ref[t, q], damped, (((1,), (1,)), ((), ())), preferred_element_type=F32
                )
            )
            energy = jnp.sum(spectral * spectral, axis=0, keepdims=True)
            first = wave + q
            moved = jnp.broadcast_to(energy, (8, HALF))
            for bit in range(9):
                moved = jnp.where(first // 2**bit // 2 % 2 == 1, pltpu.roll(moved, 2**bit, 1), moved)
            moved = moved[:1]
            for odd in range(2):
                power[odd] += jnp.where(first % 2 == odd, moved, 0.0)
        halves.append(jnp.concatenate(parts, axis=1))
    source = iota((LANES, 2 * LANES), 0)
    to = iota((LANES, 2 * LANES), 1)
    natural = jnp.zeros((8, 2 * LANES), F32)
    for odd in range(2):
        quarters = [power[odd][:, i * LANES : (i + 1) * LANES] for i in range(4)]
        quarters = jnp.concatenate(quarters + quarters, axis=0).astype(BF16)
        choice = jnp.where(to == 2 * source + odd, 1.0, 0.0).astype(BF16)
        natural += jnp.dot(quarters, choice, preferred_element_type=F32)
    natural = natural[:4].astype(BF16)
    for z in range(ZS):
        o_ref[z, :, YS * DATA :] = natural
    for half, side in enumerate((halves[0] + halves[1], halves[0] - halves[1])):
        for u in range(NORTH * TILES):
            a, tile = divmod(u, TILES)
            y, z = divmod(LATS - 1 - a if half else a, ZS)
            place = (y * TILES + tile) * LANES
            o_ref[z, :, place : place + LANES] = side[4 * u : 4 * u + 4].astype(BF16)
    for copy in copies:
        copy.wait()


def grid_kernel(device_ref, kept_ref, order_ref, column_ref, y_ref, table_ref, o_ref, spectrum_ref):
    kept = kept_ref[...]
    choice = row_choice(device_ref[0] >= NORTH * LEVS, 1)
    firsts, seconds = [], []
    for i in range(LEVS // 2):
        pair = []
        for b in (2 * i, 2 * i + 1):
            parts = swap_parts([y_ref[y * LEVS + b, 8:, :].astype(F32) for y in range(YS)])
            pair.append(jnp.concatenate(parts, axis=0))
        first, second = swap_lanes(pair[0], pair[1], LATS)
        firsts.append(first)
        seconds.append(second)
    back = sort_pair(order_ref[...], jnp.concatenate(firsts, axis=1), jnp.concatenate(seconds, axis=1))
    back = jnp.concatenate([half.astype(BF16) for half in back], axis=1)
    rows = jnp.dot(choice, back, preferred_element_type=F32).astype(BF16)
    rows = jnp.concatenate([rows[:, :HALF], rows[:, HALF:]], axis=0)
    number = pair_number((LANES, HALF), 1)
    choice = [jnp.where(column_ref[:, i : i + 1] == number, 1.0, 0.0).astype(BF16) for i in range(HALF // LANES)]
    numbered = jnp.dot(rows, jnp.concatenate(choice, axis=0), preferred_element_type=F32)
    lefts = []
    for step in range(STEPS):
        low = numbered[: 2 * ROWS, step * LANES : (step + 1) * LANES]
        high = numbered[2 * ROWS :, (3 - step) * LANES : (4 - step) * LANES]
        found = jnp.concatenate([low, high], axis=1)
        mask = class_mask(kept, step)
        real = jnp.where(mask, found[:ROWS], 0.0)
        imaginary = jnp.where(mask, found[ROWS:], 0.0)
        left = jnp.concatenate([real, imaginary], axis=1)
        if step == 1:
            left = jnp.concatenate([left, jnp.concatenate([-imaginary, real], axis=1)], axis=0)
        if step == 3:
            left = jnp.concatenate([left, jnp.concatenate([imaginary, -real], axis=1)], axis=0)
        lefts.append(left.astype(BF16))
    table = table_ref[2:].reshape(4 * BLOCK, QUARTER)
    odd = jnp.dot(jnp.concatenate([lefts[1], lefts[3]], axis=1), table, preferred_element_type=F32)
    first = jnp.dot(lefts[0], table_ref[0], preferred_element_type=F32)
    second = jnp.dot(lefts[2], table_ref[1], preferred_element_type=F32)
    plus, minus = first + second, first - second
    for group in range(ROWS // 16):
        place = slice(16 * group, 16 * group + 16)
        turned = slice(ROWS + 16 * group, ROWS + 16 * group + 16)
        quarters = [plus[place] + odd[place], minus[place] + odd[turned], plus[place] - odd[place], minus[place] - odd[turned]]
        points = jnp.concatenate(quarters, axis=1) * math.sqrt(NLON / MM)
        for i in range(4):
            o_ref[4 * group + i] = points[LEV * i : LEV * (i + 1)]
    power = jnp.zeros((8, LANES), F32)
    for peer in range(YS * LEVS):
        power += y_ref[peer, :8, :].astype(F32)
    power = jnp.concatenate([power[i // 2 + 4 * (i % 2)][None] for i in range(8)], axis=0)
    degree = (iota((8, LANES), 0) * LANES + iota((8, LANES), 1)).astype(F32)
    spectrum_ref[...] = power / (2.0 * LEVELS * (degree + 1.0))


def in_hbm(x):
    return pltpu.with_memory_space_constraint(x, pltpu.HBM)


def exchange(x, axes):
    return lax.all_to_all(x, axes, split_axis=0, concat_axis=0, tiled=True)


def body(grid_fields, legendre, weights, kept_waves, slot_wavenumber, diffusion):
    forward_table, inverse_table = dft_tables()
    device = lax.axis_index(("y", "z", "x", "core")).astype(jnp.int32).reshape(1)
    chunk = (ZS, 4, YS * DATA + 2 * LANES)

    sent, order, column, kept, wave, diffusion = pl.pallas_call(
        fourier_kernel,
        in_specs=[SMEM, HBM, HBM, HBM, HBM, HBM, HBM],
        out_specs=[VMEM] * 6,
        out_shape=[
            jax.ShapeDtypeStruct((YS * LEVS, CHUNK, LANES), BF16),
            jax.ShapeDtypeStruct((1, HALF), jnp.int32),
            jax.ShapeDtypeStruct((LANES, 8), jnp.int32),
            jax.ShapeDtypeStruct((ROWS, 1), jnp.int32),
            jax.ShapeDtypeStruct((1, LANES), jnp.int32),
            jax.ShapeDtypeStruct((2 * LEVELS, 1), F32),
        ],
        scratch_shapes=[
            pltpu.SMEM((BAND,), jnp.int32),
            pltpu.SMEM((NLAT // 2,), F32),
            pltpu.SMEM((LEVELS,), F32),
            pltpu.VMEM((8, LANES), jnp.int32),
            pltpu.VMEM((BAND, LEV, NLON), BF16),
            pltpu.VMEM((2, QUARTER, 4 * BLOCK), BF16),
            pltpu.VMEM((2, 2 * ROWS, QUARTER), BF16),
            pltpu.VMEM((4 * ROWS, QUARTER), BF16),
            pltpu.VMEM((4 * ROWS, HALF), BF16),
            pltpu.VMEM((2 * ROWS, 2 * ROWS), BF16),
            pltpu.VMEM((LANES, HALF), BF16),
            pltpu.VMEM((16, HALF), F32),
            pltpu.SemaphoreType.DMA((5 + STEPS,)),
        ],
        compiler_params=PARAMS,
        name="fourier",
    )(
        device,
        in_hbm(kept_waves),
        in_hbm(weights),
        in_hbm(diffusion),
        in_hbm(slot_wavenumber.reshape(8, LANES)),
        in_hbm(grid_fields.transpose(1, 0, 2)),
        in_hbm(jnp.asarray(forward_table)),
    )
    arrived = exchange(sent, ("y", "x", "core"))
    gathered = pl.pallas_call(
        gather_kernel,
        in_specs=[VMEM],
        out_specs=VMEM,
        out_shape=jax.ShapeDtypeStruct((ZS, 4, YS * DATA), BF16),
        compiler_params=PARAMS,
        name="gather",
    )(arrived)
    gathered = exchange(gathered, ("z",))
    spectral, back = pl.pallas_call(
        legendre_kernel,
        in_specs=[VMEM, VMEM, VMEM, VMEM],
        out_specs=[HBM, VMEM],
        out_shape=[
            jax.ShapeDtypeStruct((2, 2, LEVELS, 2, HALF), F32),
            jax.ShapeDtypeStruct(chunk, BF16),
        ],
        scratch_shapes=[
            pltpu.VMEM((2, 2, LEVELS, 2, HALF), F32),
            pltpu.VMEM((2, NLAT // 2, LANES), BF16),
            pltpu.SemaphoreType.DMA((4,)),
        ],
        compiler_params=PARAMS,
        name="legendre",
    )(wave, diffusion, gathered, legendre)
    back = exchange(back, ("z",))
    scattered = pl.pallas_call(
        scatter_kernel,
        in_specs=[VMEM],
        out_specs=VMEM,
        out_shape=jax.ShapeDtypeStruct((YS * LEVS, 8 + CHUNK, LANES), BF16),
        compiler_params=PARAMS,
        name="scatter",
    )(back)
    returned = exchange(scattered, ("y", "x", "core"))
    grid_out, spectrum = pl.pallas_call(
        grid_kernel,
        in_specs=[SMEM, VMEM, VMEM, VMEM, VMEM, VMEM],
        out_specs=[VMEM, VMEM],
        out_shape=[
            jax.ShapeDtypeStruct((BAND, LEV, NLON), F32),
            jax.ShapeDtypeStruct((8, LANES), F32),
        ],
        compiler_params=PARAMS,
        name="grid",
    )(device, kept, order, column, returned, jnp.asarray(inverse_table))
    return (
        grid_out.transpose(1, 0, 2),
        spectral,
        spectrum.reshape(MM),
    )


def solution(mesh):
    fine = Mesh(mesh.devices.reshape(4, 16, 4, 2), ("y", "z", "x", "core"))
    lat, lev = ("y", "z"), ("x", "core")
    both = lat + lev
    in_specs = (P(lev, lat, None), P(both, None, None, None), P(), P(lat), P(), P())
    out_specs = (P(lev, lat, None), P(both, None, None, None, None), P())
    return jax.shard_map(body, mesh=fine, in_specs=in_specs, out_specs=out_specs, check_vma=False)
```
